256 devices in a mesh: gx: 32 (over z, y_lo, core), gy: 8 (over y_hi, x).
Axes of the slice: x: 4, y: 4 (y_hi: 2, y_lo: 2; y = y_hi * 2 + y_lo), z: 8, core: 2. Of those that a mesh axis runs over, the one named last changes fastest.
Arguments:
- coords: float32 [32, 8, 8, 1024], P('gx', 'gy'), may hold values from 0 to 1, as said below
- probes: float32 [32, 8, 16, 1024], P('gx', 'gy'), may hold values from -6 to 6
- precond: float32 [32, 8, 1024], P('gx', 'gy'), may hold values from 0.25 to 1
- counts: int32 [32, 8], P('gx', 'gy'), may hold values from 192 to 1024, as said below
- neighbours: int32 [32, 8, 8, 8], P('gx', 'gy'), may hold values from 0 to 72, as said below
- inducing: int32 [32, 8, 16], P('gx', 'gy'), may hold values from 0 to 1023, as said below
- factor: float32 [4096, 4096], P('gy'), may hold values from -0.00390625 to 0.00390625
Outputs:
- solution: float32 [32, 8, 16, 1024], P('gx', 'gy')
- residual: float32 [32, 8, 16, 1024], P('gx', 'gy')
The draws below stay inside these ranges and needn't reach their ends.
Inputs may be any that keep to these rules, and one draw needn't show every extreme that they name: `counts`: slots at or past a cell's count are padding; some cell holds exactly 1024 points in every draw. `neighbours`: the listing is symmetric and lists each block itself; the distinct blocks of one cell listed by all blocks of the cell beside it along one grid axis number at most 4, by a diagonal neighbour cell at most 2, and both bounds are reached; no entry leaves the grid. `inducing`: distinct slots below the cell's count. `coords`: the first two inputs place each point inside its cell's box, (cx + a) / 32 and (cy + b) / 8 with a, b in [0, 1).
All inputs are finite; a program needn't handle non-finite values.
Results may differ from the reference program's by a relative error of at most 0.0048.
The reference program's roundings to bfloat16 on the way count: a program that leaves them out, or rounds other values in their place, can miss the bound.
Values may be sent and summed in bfloat16 or wider, within the bound.
No kernel may reach another device: no remote copies, remote signals or barrier semaphores. Data moves between devices by JAX's collectives and lax.ppermute only.
A program may use at most 64 MiB of HBM per device.

```python
import math
import jax
import jax.numpy as jnp
from jax import lax

FEAT = 8
PROBES = 16
BLOCK = 128
CAP = 8
M = 4096
ITERS = 2
GRID_X = 32
GRID_Y = 8
PTS = 1024
NPTS = 262144
IPD = 16


def cell_counts(key):
    key = jax.random.fold_in(key, 11)
    first, second = jax.random.split(key)
    drawn = jax.random.randint(first, (GRID_X * GRID_Y,), CAP * 24, CAP * 64)
    chosen = jax.random.randint(second, (), 0, GRID_X * GRID_Y)
    filled = jnp.where(jnp.arange(GRID_X * GRID_Y) == chosen, CAP * BLOCK, drawn)
    return filled.reshape(GRID_X, GRID_Y).astype(jnp.int32)


def block_bands(key):
    key = jax.random.fold_in(key, 23)
    scores = jax.random.randint(key, (GRID_X, GRID_Y, CAP), 0, 1 << 20) * CAP + jnp.arange(CAP)
    order = jnp.argsort(scores, axis=-1)
    return (order % 4).astype(jnp.int32)


def draw_counts(key, part):
    return cell_counts(key)


def draw_neighbours(key, part):
    bands = block_bands(key)
    share_count = CAP // 4
    ranked = jnp.argsort(bands * CAP + jnp.arange(CAP), axis=-1).astype(jnp.int32)
    cell_x = jnp.arange(GRID_X)[:, None, None]
    cell_y = jnp.arange(GRID_Y)[None, :, None]
    offset_x = bands % 2
    offset_y = bands // 2
    base_x = (cell_x - offset_x) // 2 * 2 + offset_x
    base_y = (cell_y - offset_y) // 2 * 2 + offset_y
    column = bands[..., None] * share_count + jnp.arange(share_count)
    pieces = []
    for step_x in range(2):
        for step_y in range(2):
            target_x = base_x + step_x
            target_y = base_y + step_y
            inside = (target_x >= 0) & (target_x < GRID_X) & (target_y >= 0) & (target_y < GRID_Y)
            safe_x = jnp.clip(target_x, 0, GRID_X - 1)
            safe_y = jnp.clip(target_y, 0, GRID_Y - 1)
            partner = ranked[safe_x[..., None], safe_y[..., None], column]
            offset = (target_x - cell_x + 1) * 3 + (target_y - cell_y + 1)
            coded = offset[..., None] * CAP + partner
            pieces.append(jnp.where(inside[..., None], coded, 9 * CAP))
    return jnp.concatenate(pieces, axis=-1).astype(jnp.int32)


def draw_inducing(key, part):
    counts = cell_counts(key)
    key = jax.random.fold_in(key, 7)
    stride = counts // IPD
    drawn = jax.random.randint(key, (GRID_X, GRID_Y, IPD), 0, 1 << 20)
    return (jnp.arange(IPD) * stride[..., None] + drawn % stride[..., None]).astype(jnp.int32)


def draw_coords(key, part):
    key = jax.random.fold_in(key, 13)
    first, second = jax.random.split(key)
    place = jax.random.uniform(first, (GRID_X, GRID_Y, 2, PTS))
    spread = jax.random.uniform(second, (GRID_X, GRID_Y, FEAT - 2, PTS)) * 0.25
    place = jnp.minimum(place, 0.999)
    cell_x = jnp.arange(GRID_X, dtype=jnp.float32)[:, None, None]
    cell_y = jnp.arange(GRID_Y, dtype=jnp.float32)[None, :, None]
    first_dim = (cell_x + place[:, :, 0, :]) / GRID_X
    second_dim = (cell_y + place[:, :, 1, :]) / GRID_Y
    return jnp.concatenate([first_dim[:, :, None, :], second_dim[:, :, None, :], spread], axis=2).astype(jnp.float32)


def steps_of(stream_key, shape, cuts, smallest, high):
    level = 1.0
    for dim, blocks in cuts:
        steps = jax.random.uniform(jax.random.fold_in(jax.random.fold_in(stream_key, 6), dim), (blocks,), jnp.float32, smallest / len(cuts), high / len(cuts))
        level = level * jnp.repeat(jnp.exp(steps), shape[dim] // blocks).reshape((-1,) + (1,) * (len(shape) - 1 - dim))
    return level


def noise(rng, shape, scale, bound, cuts=(), held_as=jnp.bfloat16):
    values = scale * jax.random.normal(rng, shape, jnp.float32)
    if cuts:
        values = values * steps_of(rng, shape, cuts, -0.22, 0.18)
    return jnp.clip(values, -bound, bound).astype(held_as)


def setup_inputs(seed: int = 0) -> dict:
    splits = jax.random.split(jax.random.key(seed), 8)
    coords = draw_coords(jax.random.fold_in(splits[7], 71), 0)
    probes = noise(splits[1], (GRID_X, GRID_Y, PROBES, PTS), 1.0, 6.0, ((0, 32), (1, 8)), jnp.float32)
    precond = jnp.clip(jnp.exp(math.log(1.0) - 1.3862944 * jax.random.uniform(splits[2], (GRID_X, GRID_Y, PTS), jnp.float32) ** steps_of(splits[2], (GRID_X, GRID_Y, PTS), ((0, 32), (1, 8)), -0.2, 0.2)), 0.25, 1.0)
    counts = draw_counts(jax.random.fold_in(splits[7], 71), 0)
    neighbours = draw_neighbours(jax.random.fold_in(splits[7], 71), 0)
    inducing = draw_inducing(jax.random.fold_in(splits[7], 71), 0)
    factor = noise(splits[6], (M, M), (M * NPTS // 512) ** -0.5, 0.00390625, ((0, 8),), jnp.float32)
    return dict(coords=coords, probes=probes, precond=precond, counts=counts, neighbours=neighbours, inducing=inducing, factor=factor)


noise_level = 1.0
sparse_amp = 1.0
support_radius = 0.32
width_sq = 0.045

def wendland(dist_sq):
    ratio = jnp.sqrt(dist_sq) / support_radius
    remain = jnp.maximum(1.0 - ratio, 0.0)
    square = remain * remain
    return sparse_amp * square * square * square * remain * (7.0 * ratio + 1.0)

def inducing_rows(points, centres):
    total = jnp.zeros((points.shape[1], centres.shape[1]), jnp.float32)
    for feature in range(points.shape[0]):
        spacing = points[feature][:, None] - centres[feature][None, :]
        total = total + spacing * spacing
    return jnp.exp(-total / width_sq).astype(jnp.bfloat16)

def block_table(region):
    feats = region.shape[2]
    slots = region.shape[3] // BLOCK
    table = region.reshape(9, feats, slots, BLOCK).transpose(0, 2, 1, 3).reshape(9 * slots, feats, BLOCK)
    return jnp.concatenate([table, jnp.zeros((1, feats, BLOCK), region.dtype)], axis=0)

def kernel_tiles(own_points, partner_points):
    total = jnp.zeros((own_points.shape[0], BLOCK, partner_points.shape[1], BLOCK), jnp.float32)
    for feature in range(own_points.shape[1]):
        spacing = own_points[:, feature, :, None, None] - partner_points[:, None, :, feature, :]
        total = total + spacing * spacing
    return wendland(total).astype(jnp.bfloat16)

def sparse_tiles(own_points, partner_points, partner_values):
    kernel = kernel_tiles(own_points, partner_points)
    return jnp.einsum('giej,gecj->gci', kernel.astype(jnp.float32), partner_values.astype(jnp.float32))

def reference(coords, probes, precond, counts, neighbours, inducing, factor):
    cells = GRID_X * GRID_Y
    cell_ids = jnp.arange(cells, dtype=jnp.int32)
    zero_index = jnp.zeros((), jnp.int32)
    live = (jnp.arange(PTS, dtype=jnp.int32)[None, None, :] < counts[:, :, None]).astype(jnp.float32)
    centres = jnp.take_along_axis(coords, inducing[:, :, None, :], axis=3)
    centres = centres.transpose(2, 0, 1, 3).reshape(FEAT, M)
    coord_pad = jnp.pad(coords, ((1, 1), (1, 1), (0, 0), (0, 0)))

    def cell_kernel(cell):
        return inducing_rows(coords[cell // GRID_Y, cell % GRID_Y], centres)

    def operate(search):
        packed = search.astype(jnp.bfloat16)
        value_pad = jnp.pad(packed, ((1, 1), (1, 1), (0, 0), (0, 0)))

        def sparse_cell(cell):
            row_index = cell // GRID_Y
            col_index = cell % GRID_Y
            near_points = lax.dynamic_slice(coord_pad, (row_index, col_index, zero_index, zero_index), (3, 3, FEAT, PTS))
            near_values = lax.dynamic_slice(value_pad, (row_index, col_index, zero_index, zero_index), (3, 3, PROBES, PTS))
            point_table = block_table(near_points)
            value_table = block_table(near_values)
            entries = neighbours[row_index, col_index]
            own = coords[row_index, col_index].reshape(FEAT, CAP, BLOCK).transpose(1, 0, 2)
            result = sparse_tiles(own, point_table[entries], value_table[entries])
            return result.transpose(1, 0, 2).reshape(PROBES, PTS)
        sparse = lax.map(sparse_cell, cell_ids).reshape(GRID_X, GRID_Y, PROBES, PTS)

        def project_cell(cell):
            return jnp.dot(packed[cell // GRID_Y, cell % GRID_Y], cell_kernel(cell), preferred_element_type=jnp.float32)
        summed = lax.optimization_barrier(jnp.sum(lax.map(project_cell, cell_ids), axis=0))
        coeffs = jnp.dot(summed, factor, precision=lax.Precision.HIGHEST, preferred_element_type=jnp.float32)
        weights = jnp.dot(coeffs, factor.T, precision=lax.Precision.HIGHEST, preferred_element_type=jnp.float32).astype(jnp.bfloat16)

        def expand_cell(cell):
            return lax.dot_general(weights, cell_kernel(cell), (((1,), (1,)), ((), ())), preferred_element_type=jnp.float32)
        low = lax.map(expand_cell, cell_ids).reshape(GRID_X, GRID_Y, PROBES, PTS)
        return live[:, :, None, :] * (noise_level * search + sparse + low)

    def inner(left, right):
        return lax.optimization_barrier(jnp.sum(left * right, axis=(0, 1, 3)))
    scaling = precond[:, :, None, :]
    residual = probes * live[:, :, None, :]
    solution = jnp.zeros_like(residual)
    search = scaling * residual
    rz_now = inner(residual, search)
    for step_index in range(ITERS):
        image = operate(search)
        alpha = (rz_now / inner(search, image))[None, None, :, None]
        solution = solution + alpha * search
        residual = residual - alpha * image
        if step_index + 1 < ITERS:
            precon = scaling * residual
            rz_next = inner(residual, precon)
            search = precon + (rz_next / rz_now)[None, None, :, None] * search
            rz_now = rz_next
    return (solution, residual)
```

```python
import jax
import jax.numpy as jnp
from jax import lax
from jax.sharding import Mesh, PartitionSpec as P

FEAT = 8
BLOCK = 128
ITERS = 2
PROBES = 16
SHARE = 128

noise_level = 1.0
sparse_amp = 1.0
support_radius = 0.32
width_sq = 0.045
group_blocks = 4

ALL = ("z", "yl", "c", "yh", "x")
PLANE = ("yh", "x", "yl", "c")
CELLS = ("yl", "c", "yh", "x")
GX = ("z", "yl", "c")
GY = ("yh", "x")


def padded(block, sides, width):
    for axis, dim in sides:
        count = lax.axis_size(axis)
        forward = [(i, i + 1) for i in range(count - 1)]
        backward = [(target, source) for source, target in forward]
        low = lax.ppermute(
            lax.slice_in_dim(block, block.shape[dim] - width, None, axis=dim), axis, forward
        )
        high = lax.ppermute(lax.slice_in_dim(block, 0, width, axis=dim), axis, backward)
        block = jnp.concatenate([low, block, high], axis=dim)
    return block


def wendland(dist_sq):
    ratio = jnp.sqrt(dist_sq) / support_radius
    remain = jnp.maximum(1.0 - ratio, 0.0)
    square = remain * remain
    return sparse_amp * square * square * square * remain * (7.0 * ratio + 1.0)


def inducing_rows(points, centres):
    total = jnp.zeros((points.shape[1], centres.shape[1]), jnp.float32)
    for feature in range(points.shape[0]):
        spacing = points[feature][:, None] - centres[feature][None, :]
        total = total + spacing * spacing
    return jnp.exp(-total / width_sq).astype(jnp.bfloat16)


def block_table(region):
    feats = region.shape[2]
    slots = region.shape[3] // BLOCK
    table = (
        region.reshape(9, feats, slots, BLOCK)
        .transpose(0, 2, 1, 3)
        .reshape(9 * slots, feats, BLOCK)
    )
    return jnp.concatenate([table, jnp.zeros((1, feats, BLOCK), region.dtype)], axis=0)


def kernel_tiles(own_points, partner_points):
    total = jnp.zeros((own_points.shape[0], BLOCK, partner_points.shape[1], BLOCK), jnp.float32)
    for feature in range(own_points.shape[1]):
        spacing = own_points[:, feature, :, None, None] - partner_points[:, None, :, feature, :]
        total = total + spacing * spacing
    return wendland(total).astype(jnp.bfloat16)


def exchange(parts, axes):
    return lax.all_to_all(parts, axes, 0, 0, tiled=True)


def spread(value, axes):
    count = lax.axis_size(axes)
    return exchange(jnp.broadcast_to(value[None], (count,) + value.shape), axes)


def total_scalars(row):
    row = jnp.sum(spread(row, CELLS), axis=0)
    return jnp.sum(spread(row, "z"), axis=0)


def quad_partner(value, step):
    pairs = [(i, i ^ step) for i in range(4)]
    return lax.ppermute(value, ("yl", "c"), pairs)


def on_device(coords, probes, precond, counts, neighbours, inducing, factor):
    slots = coords.shape[3]
    blocks_cell = slots // BLOCK
    groups = blocks_cell // group_blocks
    quad = lax.axis_index("yl") * 2 + lax.axis_index("c")
    live_count = counts[0, 0]
    live = (jnp.arange(slots, dtype=jnp.int32) < live_count).astype(jnp.float32)[None, :]
    own_points = coords[0, 0]
    entry_codes = neighbours[0, 0]
    scaling = precond[0, 0][None, :]
    residual = probes[0, 0] * live
    solution = jnp.zeros_like(residual)
    search = scaling * residual

    centre_local = jnp.take(own_points, inducing[0, 0], axis=1)
    plane_centres = spread(centre_local.reshape(1, 128), CELLS).reshape(32, 128)
    centres = spread(plane_centres, "z").reshape(256, FEAT, 16)
    centres = centres.transpose(1, 0, 2).reshape(FEAT, 4096)

    columns = factor.shape[1] // 4
    factor_cols = lax.dynamic_slice_in_dim(factor, quad * columns, columns, 1)
    factor_part = jnp.concatenate(
        [
            lax.dynamic_slice_in_dim(factor_cols, (quad ^ step) * SHARE, SHARE, 0)
            for step in range(4)
        ],
        axis=0,
    )

    near_points = padded(coords, ((GX, 0), (GY, 1)), 1)
    point_table = block_table(near_points)
    own_blocks = own_points.reshape(FEAT, blocks_cell, BLOCK).transpose(1, 0, 2)

    def tile_group(index):
        start = index * group_blocks
        own = lax.dynamic_slice_in_dim(own_blocks, start, group_blocks, 0)
        picks = lax.dynamic_slice_in_dim(entry_codes, start, group_blocks, 0)
        return kernel_tiles(own, point_table[picks])

    stored_tiles = lax.map(tile_group, jnp.arange(groups, dtype=jnp.int32))
    grouped = own_points.reshape(FEAT, blocks_cell // group_blocks, group_blocks * BLOCK).transpose(
        1, 0, 2
    )
    kernel_rows = lax.map(lambda portion: inducing_rows(portion, centres), grouped).reshape(
        slots, centres.shape[1]
    )

    def inner(left, right):
        return jnp.sum(left * right, axis=1)

    def pack(*sums):
        row = jnp.concatenate(sums)
        return jnp.pad(row, (0, 128 - row.shape[0]))[None, :]

    rz_part = inner(residual, search)
    for step_index in range(ITERS):
        packed = search.astype(jnp.bfloat16)
        near_values = padded(packed[None, None], ((GX, 0), (GY, 1)), 1)
        value_table = block_table(near_values)

        def one_group(index, result):
            start = index * group_blocks
            picks = lax.dynamic_slice_in_dim(entry_codes, start, group_blocks, 0)
            tiles = lax.dynamic_index_in_dim(stored_tiles, index, 0, keepdims=False)
            partial_out = jnp.einsum(
                "giej,gecj->gci", tiles, value_table[picks], preferred_element_type=jnp.float32
            )
            return lax.dynamic_update_slice_in_dim(result, partial_out, start, 0)

        result = lax.fori_loop(
            0, groups, one_group, jnp.zeros((blocks_cell, PROBES, BLOCK), jnp.float32)
        )
        sparse = result.transpose(1, 0, 2).reshape(PROBES, slots)

        terms = jnp.dot(packed, kernel_rows, preferred_element_type=jnp.float32)
        parts = terms.reshape(PROBES, 32, SHARE).transpose(1, 0, 2)
        share = jnp.sum(exchange(parts, PLANE), axis=0)
        share = jnp.sum(spread(share, "z"), axis=0)
        quad_shares = jnp.concatenate(
            [share] + [quad_partner(share, step) for step in (1, 2, 3)], axis=1
        )
        coeff_terms = jnp.dot(
            quad_shares,
            factor_part,
            precision=lax.Precision.HIGHEST,
            preferred_element_type=jnp.float32,
        )
        coeffs = jnp.sum(spread(coeff_terms, GY), axis=0)
        weight_terms = lax.dot_general(
            coeffs,
            factor_part,
            (((1,), (1,)), ((), ())),
            precision=lax.Precision.HIGHEST,
            preferred_element_type=jnp.float32,
        )
        weights = weight_terms[:, :SHARE]
        for step in (1, 2, 3):
            weights = weights + quad_partner(
                weight_terms[:, step * SHARE : (step + 1) * SHARE], step
            )
        weights = spread(weights.astype(jnp.bfloat16), PLANE)
        weights = weights.transpose(1, 0, 2).reshape(PROBES, 4096)
        low = lax.dot_general(
            weights,
            kernel_rows,
            (((1,), (1,)), ((), ())),
            preferred_element_type=jnp.float32,
        )
        image = live * (noise_level * search + sparse + low)
        curve_part = inner(search, image)
        if step_index == 0:
            sums = total_scalars(pack(rz_part, curve_part))[0]
            rz_now, curve = sums[:PROBES], sums[PROBES : 2 * PROBES]
        else:
            curve = total_scalars(pack(curve_part))[0, :PROBES]
        alpha = (rz_now / curve)[:, None]
        solution = solution + alpha * search
        residual = residual - alpha * image
        if step_index + 1 < ITERS:
            precon = scaling * residual
            rz_next = total_scalars(pack(inner(residual, precon)))[0, :PROBES]
            search = precon + (rz_next / rz_now)[:, None] * search
            rz_now = rz_next
    return (solution[None, None], residual[None, None])


def solution(mesh):
    fine = Mesh(mesh.devices.reshape(8, 2, 2, 2, 4), ALL)
    placed = (
        P(GX, GY, None, None),
        P(GX, GY, None, None),
        P(GX, GY, None),
        P(GX, GY),
        P(GX, GY, None, None),
        P(GX, GY, None),
        P(GY, None),
    )
    return jax.shard_map(
        on_device,
        mesh=fine,
        in_specs=placed,
        out_specs=(P(GX, GY, None, None), P(GX, GY, None, None)),
        check_vma=False,
    )
```

```python
import jax
import jax.numpy as jnp
from jax import lax
from jax.experimental import pallas as pl
from jax.experimental.pallas import tpu as pltpu
from jax.sharding import Mesh, PartitionSpec as P

FEAT = 8
BLOCK = 128
PROBES = 16
PTS = 1024
SHARE = 128
CHUNK = 512
CHUNKS = 8
CAP = 8
EMPTY = 72

support_radius = 0.32
width_sq = 0.045
LOG2E = 1.4426950408889634

ALL = ("z", "yl", "c", "yh", "x")
PLANE = ("yh", "x", "yl", "c")
CELLS = ("yl", "c", "yh", "x")
GX = ("z", "yl", "c")
GY = ("yh", "x")
f32 = jnp.float32
bf16 = jnp.bfloat16

VMEM = pl.BlockSpec(memory_space=pltpu.VMEM)
SMEM = pl.BlockSpec(memory_space=pltpu.SMEM)
PARAMS = pltpu.CompilerParams(vmem_limit_bytes=32 * 1024 * 1024)


def exchange(parts, axes):
    return lax.all_to_all(parts, axes, 0, 0, tiled=True)


def spread(value, axes):
    count = lax.axis_size(axes)
    return exchange(jnp.broadcast_to(value[None], (count,) + value.shape), axes)


def quad_partner(value, step):
    pairs = [(i, i ^ step) for i in range(4)]
    return lax.ppermute(value, ("yl", "c"), pairs)


def beside(value, axes):
    count = lax.axis_size(axes)
    forward = [(i, i + 1) for i in range(count - 1)]
    backward = [(target, source) for source, target in forward]
    return lax.ppermute(value, axes, forward), lax.ppermute(value, axes, backward)


def split3(value):
    first = value.astype(bf16).astype(f32)
    rest = value - first
    second = rest.astype(bf16).astype(f32)
    return first, second, (rest - second).astype(bf16).astype(f32)


def augmented(points, scale, left):
    centred = points - 0.5
    norm = scale * jnp.sum(centred * centred, axis=0, keepdims=True)
    norms = [jnp.broadcast_to(part, points.shape) for part in split3(norm)]
    row = lax.broadcasted_iota(jnp.int32, points.shape, 0)
    if left:
        one, two, three = split3(centred)
        order = [one, one, two, one, two, three]
        base = 0
    else:
        one, two, three = split3((-2.0 * scale) * centred)
        order = [one, two, one, three, two, one]
        base = 3
    extra = jnp.where(row < 6, 1.0, 0.0)
    for index, part in enumerate(norms):
        extra = jnp.where(row == base + index, part, extra)
    return jnp.concatenate(order + [extra, jnp.zeros_like(extra)], axis=0).astype(bf16)


def as_lanes(column, offset):
    row = lax.broadcasted_iota(jnp.int32, (PROBES, 128), 0)
    lane = lax.broadcasted_iota(jnp.int32, (PROBES, 128), 1)
    return jnp.sum(jnp.where(lane == row + offset, column, 0.0), axis=0, keepdims=True)


def as_column(row_value, offset):
    row = lax.broadcasted_iota(jnp.int32, (PROBES, 128), 0)
    lane = lax.broadcasted_iota(jnp.int32, (PROBES, 128), 1)
    return jnp.sum(jnp.where(lane == row + offset, row_value, 0.0), axis=1, keepdims=True)


def live_lanes(count):
    lane = lax.broadcasted_iota(jnp.int32, (1, PTS), 1)
    return jnp.where(lane < count, 1.0, 0.0)


def nt_dot(left, right):
    return lax.dot_general(left, right, (((1,), (1,)), ((), ())), preferred_element_type=f32)


def prepare_kernel(coords, probes, precond, counts, inducing, centre_out, halo_out):
    points = coords[...]
    lane = lax.broadcasted_iota(jnp.int32, (FEAT, PTS), 1)
    short = lax.broadcasted_iota(jnp.int32, (FEAT, 128), 1)
    centre = jnp.zeros((FEAT, 128), f32)
    for index in range(16):
        picked = jnp.sum(
            jnp.where(lane == inducing[0, index], points, 0.0), axis=1, keepdims=True
        )
        centre = jnp.where(short == index, picked, centre)
    centre_out[...] = jnp.broadcast_to(centre[None], centre_out.shape)
    halo_out[:FEAT] = points
    halo_out[FEAT:] = precond[...] * (probes[...] * live_lanes(counts[0, 0]))


def prepare(coords, probes, precond, counts, inducing):
    return pl.pallas_call(
        prepare_kernel,
        out_shape=(
            jax.ShapeDtypeStruct((32, FEAT, 128), f32),
            jax.ShapeDtypeStruct((FEAT + PROBES, PTS), f32),
        ),
        in_specs=[VMEM, VMEM, VMEM, SMEM, SMEM],
        out_specs=(VMEM, VMEM),
        compiler_params=PARAMS,
        name="prepare",
    )(coords, probes, precond, counts, inducing)


def compact_kernel(parts, out):
    for tile in range(4):
        total = parts[8 * tile]
        for cell in range(1, 8):
            total = total + pltpu.roll(parts[8 * tile + cell], 16 * cell, 1)
        out[:, :, tile * 128 : (tile + 1) * 128] = jnp.broadcast_to(total[None], (8, FEAT, 128))


def compact(parts):
    return pl.pallas_call(
        compact_kernel,
        out_shape=jax.ShapeDtypeStruct((8, FEAT, CHUNK), f32),
        in_specs=[VMEM],
        out_specs=VMEM,
        compiler_params=PARAMS,
        name="compact",
    )(parts)


def rows_kernel(halo, centres, rows_out, sums_out, left, packed):
    @pl.when(pl.program_id(0) == 0)
    def _():
        left[...] = augmented(halo[:FEAT], -LOG2E / width_sq, True).astype(f32).T.astype(bf16)
        packed[...] = halo[FEAT:].astype(bf16)

    right = augmented(centres[0], -LOG2E / width_sq, False)
    power = jnp.dot(left[...], right, preferred_element_type=f32)
    rows = jnp.exp2(jnp.minimum(power, 0.0)).astype(bf16)
    rows_out[0] = rows
    sums = jnp.dot(packed[...], rows, preferred_element_type=f32)
    for part in range(4):
        sums_out[part] = sums[:, part * SHARE : (part + 1) * SHARE]


def make_rows(halo, centres):
    return pl.pallas_call(
        rows_kernel,
        grid=(CHUNKS,),
        out_shape=(
            jax.ShapeDtypeStruct((CHUNKS, PTS, CHUNK), bf16),
            jax.ShapeDtypeStruct((32, PROBES, SHARE), f32),
        ),
        in_specs=[
            pl.BlockSpec((FEAT + PROBES, PTS), lambda g: (0, 0)),
            pl.BlockSpec((1, FEAT, CHUNK), lambda g: (g, 0, 0)),
        ],
        out_specs=(
            pl.BlockSpec((1, PTS, CHUNK), lambda g: (g, 0, 0)),
            pl.BlockSpec((4, PROBES, SHARE), lambda g: (g, 0, 0)),
        ),
        scratch_shapes=[pltpu.VMEM((PTS, 64), bf16), pltpu.VMEM((PROBES, PTS), bf16)],
        compiler_params=PARAMS,
        name="rows",
    )(halo, centres)


def project_kernel(packed, rows, sums_out):
    sums = jnp.dot(packed[...], rows[0], preferred_element_type=f32)
    for part in range(4):
        sums_out[part] = sums[:, part * SHARE : (part + 1) * SHARE]


def project(packed, rows):
    height = packed.shape[0]
    return pl.pallas_call(
        project_kernel,
        grid=(CHUNKS,),
        out_shape=jax.ShapeDtypeStruct((32, height, SHARE), f32),
        in_specs=[
            pl.BlockSpec((height, PTS), lambda g: (0, 0)),
            pl.BlockSpec((1, PTS, CHUNK), lambda g: (g, 0, 0)),
        ],
        out_specs=pl.BlockSpec((4, height, SHARE), lambda g: (g, 0, 0)),
        compiler_params=PARAMS,
        name="project",
    )(packed, rows)


def fill_table(table, sources, first, last, dtype):
    for place_x in range(3):
        for place_y in range(3):
            for block in range(CAP):
                table[(place_x * 3 + place_y) * CAP + block] = sources[place_y][
                    place_x, first:last, block * BLOCK : (block + 1) * BLOCK
                ].astype(dtype)
    table[EMPTY] = jnp.zeros(table.shape[1:], dtype)


def tiles_kernel(codes, near_low, near_mid, near_high, tiles_out, sparse_out, points, values):
    block = pl.program_id(0)
    sources = (near_low, near_mid, near_high)

    @pl.when(block == 0)
    def _():
        fill_table(points, sources, 0, FEAT, f32)
        fill_table(values, sources, FEAT, FEAT + PROBES, bf16)

    scale = 1.0 / (support_radius * support_radius)
    own = augmented(points[4 * CAP + block], scale, True).astype(f32).T.astype(bf16)
    total = jnp.zeros((PROBES, BLOCK), f32)
    for entry in range(CAP):
        code = codes[block, entry]
        other = augmented(points[code], scale, False)
        square = jnp.maximum(jnp.dot(own, other, preferred_element_type=f32), 0.0)
        ratio = jnp.sqrt(square)
        remain = jnp.maximum(1.0 - ratio, 0.0)
        second = remain * remain
        fourth = second * second
        tile = (fourth * second * remain * (7.0 * ratio + 1.0)).astype(bf16)
        tiles_out[0, :, entry * BLOCK : (entry + 1) * BLOCK] = tile
        total = total + nt_dot(values[code], tile)
    sparse_out[...] = total


def make_tiles(codes, near_low, near_mid, near_high):
    whole = pl.BlockSpec((3, FEAT + PROBES, PTS), lambda b: (0, 0, 0))
    return pl.pallas_call(
        tiles_kernel,
        grid=(CAP,),
        out_shape=(
            jax.ShapeDtypeStruct((CAP, BLOCK, PTS), bf16),
            jax.ShapeDtypeStruct((PROBES, PTS), f32),
        ),
        in_specs=[SMEM, whole, whole, whole],
        out_specs=(
            pl.BlockSpec((1, BLOCK, PTS), lambda b: (b, 0, 0)),
            pl.BlockSpec((PROBES, BLOCK), lambda b: (0, b)),
        ),
        scratch_shapes=[
            pltpu.VMEM((EMPTY + 1, FEAT, BLOCK), f32),
            pltpu.VMEM((EMPTY + 1, PROBES, BLOCK), bf16),
        ],
        compiler_params=PARAMS,
        name="tiles",
    )(codes, near_low, near_mid, near_high)


def sparse_kernel(codes, near_low, near_mid, near_high, tiles, search, residual, precond, sparse_out, sums_out, values):
    fill_table(values, (near_low, near_mid, near_high), 0, PROBES, bf16)
    for block in range(CAP):
        total = jnp.zeros((PROBES, BLOCK), f32)
        for entry in range(CAP):
            total = total + nt_dot(
                values[codes[block, entry]],
                tiles[block, :, entry * BLOCK : (entry + 1) * BLOCK],
            )
        sparse_out[:, block * BLOCK : (block + 1) * BLOCK] = total
    field = search[...]
    left = residual[...]
    curve = jnp.sum(field * (field + sparse_out[...]), axis=1, keepdims=True)
    norm = jnp.sum(left * (precond[...] * left), axis=1, keepdims=True)
    lane = lax.broadcasted_iota(jnp.int32, (PROBES, 128), 1)
    sums_out[...] = jnp.where(lane == 0, curve, jnp.where(lane == 1, norm, 0.0))


def apply_tiles(codes, near_low, near_mid, near_high, tiles, search, residual, precond):
    return pl.pallas_call(
        sparse_kernel,
        out_shape=(
            jax.ShapeDtypeStruct((PROBES, PTS), f32),
            jax.ShapeDtypeStruct((PROBES, 128), f32),
        ),
        in_specs=[SMEM] + [VMEM] * 7,
        out_specs=(VMEM, VMEM),
        scratch_shapes=[pltpu.VMEM((EMPTY + 1, PROBES, BLOCK), bf16)],
        compiler_params=PARAMS,
        name="sparse",
    )(codes, near_low, near_mid, near_high, tiles, search, residual, precond)


def expand_step(weights, rows, total):
    @pl.when(pl.program_id(0) == 0)
    def _():
        total[...] = jnp.zeros_like(total)

    part = jnp.concatenate([weights[i, :PROBES] for i in range(4)], axis=1)
    total[...] += nt_dot(part, rows[0])


def image_kernel(weights, rows, counts, halo, sparse, precond, probes, image_out, sums_out, total):
    expand_step(weights, rows, total)

    @pl.when(pl.program_id(0) == CHUNKS - 1)
    def _():
        search = halo[FEAT:]
        image = live_lanes(counts[0, 0]) * (search + sparse[...] + total[...])
        image_out[...] = image
        scale = precond[...]
        norm = jnp.sum(search * (probes[...] * live_lanes(counts[0, 0])), axis=1, keepdims=True)
        curve = jnp.sum(search * image, axis=1, keepdims=True)
        square = jnp.sum(scale * image * image, axis=1, keepdims=True)
        sums_out[...] = as_lanes(norm, 0) + as_lanes(curve, 16) + as_lanes(square, 32)


def make_image(weights, rows, counts, halo, sparse, precond, probes):
    height = weights.shape[1]
    return pl.pallas_call(
        image_kernel,
        grid=(CHUNKS,),
        out_shape=(
            jax.ShapeDtypeStruct((PROBES, PTS), f32),
            jax.ShapeDtypeStruct((1, 128), f32),
        ),
        in_specs=[
            pl.BlockSpec((4, height, SHARE), lambda g: (g, 0, 0)),
            pl.BlockSpec((1, PTS, CHUNK), lambda g: (g, 0, 0)),
            SMEM,
            pl.BlockSpec((FEAT + PROBES, PTS), lambda g: (0, 0)),
            pl.BlockSpec((PROBES, PTS), lambda g: (0, 0)),
            pl.BlockSpec((1, PTS), lambda g: (0, 0)),
            pl.BlockSpec((PROBES, PTS), lambda g: (0, 0)),
        ],
        out_specs=(
            pl.BlockSpec((PROBES, PTS), lambda g: (0, 0)),
            pl.BlockSpec((1, 128), lambda g: (0, 0)),
        ),
        scratch_shapes=[pltpu.VMEM((PROBES, PTS), f32)],
        compiler_params=PARAMS,
        name="image",
    )(weights, rows, counts, halo, sparse, precond, probes)


def update_kernel(sums, halo, probes, precond, counts, image, residual_out, search_out, packed_out, solution_out):
    rz_now = as_column(sums[...], 0)
    alpha = rz_now / as_column(sums[...], 16)
    rz_next = alpha * alpha * as_column(sums[...], 32) - rz_now
    search = halo[FEAT:]
    solution_out[...] = alpha * search
    residual = probes[...] * live_lanes(counts[0, 0]) - alpha * image[...]
    residual_out[...] = residual
    following = precond[...] * residual + (rz_next / rz_now) * search
    search_out[...] = following
    rounded = following.astype(bf16)
    packed_out[:PROBES] = rounded
    packed_out[PROBES:] = (following - rounded.astype(f32)).astype(bf16)


def update(sums, halo, probes, precond, counts, image):
    field = jax.ShapeDtypeStruct((PROBES, PTS), f32)
    return pl.pallas_call(
        update_kernel,
        out_shape=(field, field, jax.ShapeDtypeStruct((2 * PROBES, PTS), bf16), field),
        in_specs=[VMEM, VMEM, VMEM, VMEM, SMEM, VMEM],
        out_specs=(VMEM,) * 4,
        compiler_params=PARAMS,
        name="update",
    )(sums, halo, probes, precond, counts, image)


def finish_kernel(weights, rows, every, counts, search, sparse, residual, solution, sums, solution_out, residual_out, total):
    expand_step(weights, rows, total)

    @pl.when(pl.program_id(0) == CHUNKS - 1)
    def _():
        field = search[...]
        image = live_lanes(counts[0, 0]) * (field + sparse[...] + total[...])
        dots = jnp.sum(every[:, PROBES:].astype(f32), axis=0)
        dot = jnp.sum(dots, axis=1, keepdims=True)
        totals = sums[...]
        curve = totals[:, 0:1] + dot
        alpha = totals[:, 1:2] / curve
        solution_out[...] = solution[...] + alpha * field
        residual_out[...] = residual[...] - alpha * image


def finish(weights, rows, counts, search, sparse, residual, solution, sums):
    field = jax.ShapeDtypeStruct((PROBES, PTS), f32)
    still = pl.BlockSpec((PROBES, PTS), lambda g: (0, 0))
    height = weights.shape[1]
    return pl.pallas_call(
        finish_kernel,
        grid=(CHUNKS,),
        out_shape=(field, field),
        in_specs=[
            pl.BlockSpec((4, height, SHARE), lambda g: (g, 0, 0)),
            pl.BlockSpec((1, PTS, CHUNK), lambda g: (g, 0, 0)),
            pl.BlockSpec((32, height, SHARE), lambda g: (0, 0, 0)),
            SMEM,
            still,
            still,
            still,
            still,
            pl.BlockSpec((PROBES, 128), lambda g: (0, 0)),
        ],
        out_specs=(still, still),
        scratch_shapes=[pltpu.VMEM((PROBES, PTS), f32)],
        compiler_params=PARAMS,
        name="finish",
    )(weights, rows, weights, counts, search, sparse, residual, solution, sums)


def on_device(coords, probes, precond, counts, neighbours, inducing, factor):
    quad = lax.axis_index("yl") * 2 + lax.axis_index("c")
    points = coords[0, 0]
    sides = probes[0, 0]
    scaling = precond[0]
    codes = neighbours[0, 0]

    centre_parts, halo = prepare(points, sides, scaling, counts, inducing[0])
    centres = exchange(compact(exchange(centre_parts, CELLS)), "z")

    columns = factor.shape[1] // 4
    factor_cols = lax.dynamic_slice_in_dim(factor, quad * columns, columns, 1)
    factor_part = jnp.concatenate(
        [
            lax.dynamic_slice_in_dim(factor_cols, (quad ^ step) * SHARE, SHARE, 0)
            for step in range(4)
        ],
        axis=0,
    )

    def surround(value):
        low, high = beside(value, GX)
        column = jnp.stack([low, value, high])
        left, right = beside(column, GY)
        return left, column, right

    near = surround(halo)
    rows, parts = make_rows(halo, centres)
    tiles, sparse = make_tiles(codes, *near)

    def weights_of(parts, sums):
        share = jnp.sum(exchange(parts, PLANE), axis=0)
        if sums is not None:
            share = jnp.concatenate([share, sums], axis=0)
        share = jnp.sum(spread(share, "z"), axis=0)
        own = share[:PROBES]
        quad_shares = jnp.concatenate(
            [own] + [quad_partner(own, step) for step in (1, 2, 3)], axis=1
        )
        terms = jnp.dot(
            quad_shares, factor_part, precision=lax.Precision.HIGHEST, preferred_element_type=f32
        )
        if sums is not None:
            terms = jnp.concatenate([terms, share[2 * PROBES :]], axis=1)
        coeffs = jnp.sum(spread(terms, GY), axis=0)
        terms = lax.dot_general(
            coeffs[:, :columns],
            factor_part,
            (((1,), (1,)), ((), ())),
            precision=lax.Precision.HIGHEST,
            preferred_element_type=f32,
        )
        totals = None
        if sums is not None:
            totals = coeffs[:, columns:]
        weights = terms[:, :SHARE]
        sent = totals
        for step in (1, 2, 3):
            part = terms[:, step * SHARE : (step + 1) * SHARE]
            if sums is None:
                weights = weights + quad_partner(part, step)
            else:
                got = quad_partner(jnp.concatenate([part, sent], axis=1), step)
                weights = weights + got[:, :SHARE]
                totals = totals + got[:, SHARE:]
        weights = weights.astype(bf16)
        if sums is not None:
            unrounded = share[:PROBES] + share[PROBES : 2 * PROBES]
            dot = jnp.sum(weights.astype(f32) * unrounded, axis=1, keepdims=True)
            first = lax.reduce_precision(dot, 8, 7)
            second = lax.reduce_precision(dot - first, 8, 7)
            third = dot - first - second
            lane = lax.broadcasted_iota(jnp.int32, (PROBES, SHARE), 1)
            row = jnp.where(
                lane == 0, first, jnp.where(lane == 1, second, jnp.where(lane == 2, third, 0.0))
            )
            weights = jnp.concatenate([weights, row.astype(bf16)], axis=0)
        return spread(weights, PLANE), totals

    weights, _ = weights_of(parts, None)
    image, row = make_image(weights, rows, counts, halo, sparse, scaling, sides)
    row = jnp.sum(spread(row, CELLS), axis=0)
    row = jnp.sum(spread(row, "z"), axis=0)
    residual, search, packed, solution = update(row, halo, sides, scaling, counts, image)

    near = surround(packed[:PROBES])
    parts = project(packed, rows)
    sparse, sums = apply_tiles(codes, *near, tiles, search, residual, scaling)
    weights, totals = weights_of(parts, sums)
    solution, residual = finish(
        weights, rows, counts, search, sparse, residual, solution, totals
    )
    return (solution[None, None], residual[None, None])


def solution(mesh):
    fine = Mesh(mesh.devices.reshape(8, 2, 2, 2, 4), ALL)
    placed = (
        P(GX, GY, None, None),
        P(GX, GY, None, None),
        P(GX, GY, None),
        P(GX, GY),
        P(GX, GY, None, None),
        P(GX, GY, None),
        P(GY, None),
    )
    return jax.shard_map(
        on_device,
        mesh=fine,
        in_specs=placed,
        out_specs=(P(GX, GY, None, None), P(GX, GY, None, None)),
        check_vma=False,
    )
```

```python
import jax
import jax.numpy as jnp
from jax import lax
from jax.experimental import pallas as pl
from jax.experimental.pallas import tpu as pltpu
from jax.sharding import Mesh, PartitionSpec as P

FEAT = 8
BLOCK = 128
PROBES = 16
PTS = 1024
SHARE = 128
CHUNK = 512
CHUNKS = 8
CAP = 8
EMPTY = 72
QUARTER = 1024

support_radius = 0.32
width_sq = 0.045
LOG2E = 1.4426950408889634

ALL = ("z", "yl", "c", "yh", "x")
PLANE = ("yh", "x", "yl", "c")
CELLS = ("yl", "c", "yh", "x")
GX = ("z", "yl", "c")
GY = ("yh", "x")
f32 = jnp.float32
bf16 = jnp.bfloat16

VMEM = pl.BlockSpec(memory_space=pltpu.VMEM)
SMEM = pl.BlockSpec(memory_space=pltpu.SMEM)
SMALL = pltpu.CompilerParams(vmem_limit_bytes=16 * 1024 * 1024)
MIDDLE = pltpu.CompilerParams(vmem_limit_bytes=24 * 1024 * 1024)
LARGE = pltpu.CompilerParams(vmem_limit_bytes=57 * 1024 * 1024)


def exchange(parts, axes):
    return lax.all_to_all(parts, axes, 0, 0, tiled=True)


def quad_partner(value, step):
    pairs = [(i, i ^ step) for i in range(4)]
    return lax.ppermute(value, ("yl", "c"), pairs)


def even_pairs(value, axes):
    return lax.ppermute(value, axes, [(i, i ^ 1) for i in range(lax.axis_size(axes))])


def odd_pairs(value, axes):
    count = lax.axis_size(axes)
    pairs = [(i, i + 1) for i in range(1, count - 1, 2)]
    return lax.ppermute(value, axes, pairs + [(j, i) for i, j in pairs])


def after(value, *others):
    return lax.optimization_barrier((value,) + others)[0]


def split3(value):
    first = value.astype(bf16).astype(f32)
    rest = value - first
    second = rest.astype(bf16).astype(f32)
    return first, second, (rest - second).astype(bf16).astype(f32)


def augmented(points, scale, left):
    centred = points - 0.5
    norm = scale * jnp.sum(centred * centred, axis=0, keepdims=True)
    norms = [jnp.broadcast_to(part, points.shape) for part in split3(norm)]
    row = lax.broadcasted_iota(jnp.int32, points.shape, 0)
    if left:
        one, two, three = split3(centred)
        order = [one, one, two, one, two, three]
        base = 0
    else:
        one, two, three = split3((-2.0 * scale) * centred)
        order = [one, two, one, three, two, one]
        base = 3
    extra = jnp.where(row < 6, 1.0, 0.0)
    for index, part in enumerate(norms):
        extra = jnp.where(row == base + index, part, extra)
    return jnp.concatenate(order + [extra, jnp.zeros_like(extra)], axis=0).astype(bf16)


def as_lanes(column, offset):
    row = lax.broadcasted_iota(jnp.int32, (PROBES, 128), 0)
    lane = lax.broadcasted_iota(jnp.int32, (PROBES, 128), 1)
    return jnp.sum(jnp.where(lane == row + offset, column, 0.0), axis=0, keepdims=True)


def as_column(row_value, offset):
    row = lax.broadcasted_iota(jnp.int32, (PROBES, 128), 0)
    lane = lax.broadcasted_iota(jnp.int32, (PROBES, 128), 1)
    return jnp.sum(jnp.where(lane == row + offset, row_value, 0.0), axis=1, keepdims=True)


def live_lanes(count):
    lane = lax.broadcasted_iota(jnp.int32, (1, PTS), 1)
    return jnp.where(lane < count, 1.0, 0.0)


def nt_dot(left, right):
    return lax.dot_general(left, right, (((1,), (1,)), ((), ())), preferred_element_type=f32)


def call(kernel, name, out_shape, in_specs, args, scratch=(), grid=None, out_specs=None, params=SMALL, flops=0, moved=0):
    if out_specs is None:
        out_specs = jax.tree.map(lambda _: VMEM, out_shape)
    options = {} if grid is None else {"grid": grid}
    return pl.pallas_call(
        kernel,
        out_shape=out_shape,
        in_specs=in_specs,
        out_specs=out_specs,
        scratch_shapes=list(scratch),
        compiler_params=params,
        cost_estimate=pl.CostEstimate(flops=flops, bytes_accessed=moved, transcendentals=0),
        name=name,
        **options,
    )(*args)


def shape(*dims, dtype=f32):
    return jax.ShapeDtypeStruct(dims, dtype)


FIELD = shape(PROBES, PTS)


def prepare_kernel(coords, probes, precond, counts, inducing, centre_out, halo_out):
    points = coords[...]
    lane = lax.broadcasted_iota(jnp.int32, (FEAT, PTS), 1)
    short = lax.broadcasted_iota(jnp.int32, (FEAT, 128), 1)
    centre = jnp.zeros((FEAT, 128), f32)
    for index in range(16):
        picked = jnp.sum(
            jnp.where(lane == inducing[0, index], points, 0.0), axis=1, keepdims=True
        )
        centre = jnp.where(short == index, picked, centre)
    centre_out[...] = jnp.broadcast_to(centre[None], centre_out.shape)
    halo_out[:FEAT] = points
    halo_out[FEAT:] = precond[...] * (probes[...] * live_lanes(counts[0, 0]))


def prepare(coords, probes, precond, counts, inducing):
    return call(
        prepare_kernel,
        "prepare",
        (shape(32, FEAT, 128), shape(FEAT + PROBES, PTS)),
        [VMEM, VMEM, VMEM, SMEM, SMEM],
        (coords, probes, precond, counts, inducing),
        params=LARGE,
    )


def compact_kernel(parts, out):
    for tile in range(4):
        total = parts[8 * tile]
        for cell in range(1, 8):
            total = total + pltpu.roll(parts[8 * tile + cell], 16 * cell, 1)
        out[:, :, tile * 128 : (tile + 1) * 128] = jnp.broadcast_to(total[None], (8, FEAT, 128))


def compact(parts):
    return call(compact_kernel, "compact", shape(8, FEAT, CHUNK), [VMEM], (parts,))


def factor_kernel(quad, factor, first_out, second_out, third_out):
    first, second, third = split3(factor[...])
    first_out[...] = first.astype(bf16)
    second_out[...] = second.astype(bf16)
    third_out[...] = third.astype(bf16)


def split_factor(quad, factor):
    block = pl.BlockSpec((SHARE, QUARTER), lambda k, quad: (k, 0))
    return pl.pallas_call(
        factor_kernel,
        out_shape=(shape(4 * SHARE, QUARTER, dtype=bf16),) * 3,
        grid_spec=pltpu.PrefetchScalarGridSpec(
            num_scalar_prefetch=1,
            grid=(4,),
            in_specs=[pl.BlockSpec((SHARE, QUARTER), lambda k, quad: (quad[0] ^ k, quad[0]))],
            out_specs=(block,) * 3,
        ),
        compiler_params=LARGE,
        cost_estimate=pl.CostEstimate(flops=0, bytes_accessed=8 << 20, transcendentals=0),
        name="factor",
    )(quad, factor)


def rows_kernel(halo, centres, rows_out, sums_out, left, packed):
    @pl.when(pl.program_id(0) == 0)
    def _():
        left[...] = augmented(halo[:FEAT], -LOG2E / width_sq, True).astype(f32).T.astype(bf16)
        packed[...] = halo[FEAT:].astype(bf16)

    right = augmented(centres[0], -LOG2E / width_sq, False)
    power = jnp.dot(left[...], right, preferred_element_type=f32)
    rows = jnp.exp2(jnp.minimum(power, 0.0)).astype(bf16)
    rows_out[0] = rows
    sums = jnp.dot(packed[...], rows, preferred_element_type=f32)
    for part in range(4):
        sums_out[part] = sums[:, part * SHARE : (part + 1) * SHARE]


def make_rows(halo, centres):
    return call(
        rows_kernel,
        "rows",
        (shape(CHUNKS, PTS, CHUNK, dtype=bf16), shape(32, PROBES, SHARE)),
        [
            pl.BlockSpec((FEAT + PROBES, PTS), lambda g: (0, 0)),
            pl.BlockSpec((1, FEAT, CHUNK), lambda g: (g, 0, 0)),
        ],
        (halo, centres),
        scratch=[pltpu.VMEM((PTS, 64), bf16), pltpu.VMEM((PROBES, PTS), bf16)],
        grid=(CHUNKS,),
        out_specs=(
            pl.BlockSpec((1, PTS, CHUNK), lambda g: (g, 0, 0)),
            pl.BlockSpec((4, PROBES, SHARE), lambda g: (g, 0, 0)),
        ),
        params=MIDDLE,
        moved=16 << 20,
    )


def project_kernel(packed, rows, sums_out):
    sums = jnp.dot(packed[...], rows[0], preferred_element_type=f32)
    for part in range(4):
        sums_out[part] = sums[:, part * SHARE : (part + 1) * SHARE]


def project(packed, rows):
    height = packed.shape[0]
    return call(
        project_kernel,
        "project",
        shape(32, height, SHARE),
        [
            pl.BlockSpec((height, PTS), lambda g: (0, 0)),
            pl.BlockSpec((1, PTS, CHUNK), lambda g: (g, 0, 0)),
        ],
        (packed, rows),
        grid=(CHUNKS,),
        out_specs=pl.BlockSpec((4, height, SHARE), lambda g: (g, 0, 0)),
        params=MIDDLE,
        moved=16 << 20,
    )


def fill_table(table, sides, sources, first, last, dtype):
    places_x = (1, 2 - 2 * sides[0, 0], 2 * sides[0, 0])
    places_y = (1, 2 - 2 * sides[0, 1], 2 * sides[0, 1])
    for place_y, source in zip(places_y, sources):
        for index, place_x in enumerate(places_x):
            start = (place_x * 3 + place_y) * CAP
            values = source[index, first:last].astype(dtype)
            for block in range(CAP):
                table[start + block] = values[:, block * BLOCK : (block + 1) * BLOCK]
    table[EMPTY] = jnp.zeros(table.shape[1:], dtype)


def partners(table, codes, block):
    return jnp.concatenate([table[codes[block, entry]] for entry in range(CAP)], axis=1)


def tiles_kernel(codes, sides, near, even, odd, tiles_out, sparse_out, points, values):
    block = pl.program_id(0)

    @pl.when(block == 0)
    def _():
        fill_table(points, sides, (near, even, odd), 0, FEAT, f32)
        fill_table(values, sides, (near, even, odd), FEAT, FEAT + PROBES, bf16)

    scale = 1.0 / (support_radius * support_radius)
    own = augmented(points[4 * CAP + block], scale, True).astype(f32).T.astype(bf16)
    other = augmented(partners(points, codes, block), scale, False)
    square = jnp.maximum(jnp.dot(own, other, preferred_element_type=f32), 0.0)
    ratio = jnp.sqrt(square)
    remain = jnp.maximum(1.0 - ratio, 0.0)
    second = remain * remain
    fourth = second * second
    tile = (fourth * second * remain * (7.0 * ratio + 1.0)).astype(bf16)
    tiles_out[0] = tile
    sparse_out[...] = nt_dot(partners(values, codes, block), tile)


def make_tiles(codes, sides, near, even, odd):
    whole = pl.BlockSpec((3, FEAT + PROBES, PTS), lambda b: (0, 0, 0))
    return call(
        tiles_kernel,
        "tiles",
        (shape(CAP, BLOCK, PTS, dtype=bf16), FIELD),
        [SMEM, SMEM, whole, whole, whole],
        (codes, sides, near, even, odd),
        scratch=[
            pltpu.VMEM((EMPTY + 1, FEAT, BLOCK), f32),
            pltpu.VMEM((EMPTY + 1, PROBES, BLOCK), bf16),
        ],
        grid=(CAP,),
        out_specs=(
            pl.BlockSpec((1, BLOCK, PTS), lambda b: (b, 0, 0)),
            pl.BlockSpec((PROBES, BLOCK), lambda b: (0, b)),
        ),
        moved=16 << 20,
    )


def steps_of(row):
    rz_now = as_column(row, 0)
    alpha = rz_now / as_column(row, 16)
    return alpha, alpha * alpha * as_column(row, 32) / rz_now - 1.0


def row_total(rows):
    total = rows[0]
    for index in range(1, rows.shape[0]):
        total = total + rows[index]
    return total


def sparse_kernel(
    codes, sides, near, even, odd, tiles, search, residual, precond, sparse_out, sums_out, values
):
    fill_table(values, sides, (near, even, odd), 0, PROBES, bf16)
    for block in range(CAP):
        sparse_out[:, block * BLOCK : (block + 1) * BLOCK] = nt_dot(
            partners(values, codes, block), tiles[block]
        )
    field = search[...]
    left = residual[...]
    curve = jnp.sum(field * (field + sparse_out[...]), axis=1, keepdims=True)
    norm = jnp.sum(left * (precond[...] * left), axis=1, keepdims=True)
    lane = lax.broadcasted_iota(jnp.int32, (PROBES, 128), 1)
    sums_out[...] = jnp.where(lane == 0, curve, jnp.where(lane == 1, norm, 0.0))


def apply_tiles(codes, sides, nears, tiles, search, residual, precond):
    return call(
        sparse_kernel,
        "sparse",
        (FIELD, shape(PROBES, 128)),
        [SMEM, SMEM] + [VMEM] * 7,
        (codes, sides, *nears, tiles, search, residual, precond),
        scratch=[pltpu.VMEM((EMPTY + 1, PROBES, BLOCK), bf16)],
        moved=6 << 20,
    )


def stack_kernel(own, even, odd, out):
    out[0] = own[...]
    out[1] = even[...]
    out[2] = odd[...]


def surround(value, *first):
    column = call(
        stack_kernel,
        "stack",
        shape(3, *value.shape, dtype=value.dtype),
        [VMEM] * 3,
        (value, even_pairs(value, GX), odd_pairs(value, GX)),
    )
    column = after(column, *first)
    return column, even_pairs(column, GY), odd_pairs(column, GY)


def expand_step(weights, rows, total):
    @pl.when(pl.program_id(0) == 0)
    def _():
        total[...] = jnp.zeros_like(total)

    part = jnp.concatenate([weights[i, :PROBES] for i in range(4)], axis=1)
    total[...] += nt_dot(part, rows[0])


def image_kernel(
    weights, rows, counts, halo, sparse, precond, probes, image_out, sums_out, total
):
    expand_step(weights, rows, total)

    @pl.when(pl.program_id(0) == CHUNKS - 1)
    def _():
        search = halo[FEAT:]
        live = live_lanes(counts[0, 0])
        image = live * (search + sparse[...] + total[...])
        image_out[...] = image
        norm = jnp.sum(search * (probes[...] * live), axis=1, keepdims=True)
        curve = jnp.sum(search * image, axis=1, keepdims=True)
        square = jnp.sum(precond[...] * image * image, axis=1, keepdims=True)
        row = as_lanes(norm, 0) + as_lanes(curve, 16) + as_lanes(square, 32)
        for index in range(32):
            sums_out[index] = row


def make_image(weights, rows, counts, halo, sparse, precond, probes):
    height = weights.shape[1]
    still = pl.BlockSpec((PROBES, PTS), lambda g: (0, 0))
    return call(
        image_kernel,
        "image",
        (FIELD, shape(32, 1, 128)),
        [
            pl.BlockSpec((4, height, SHARE), lambda g: (g, 0, 0)),
            pl.BlockSpec((1, PTS, CHUNK), lambda g: (g, 0, 0)),
            SMEM,
            pl.BlockSpec((FEAT + PROBES, PTS), lambda g: (0, 0)),
            still,
            pl.BlockSpec((1, PTS), lambda g: (0, 0)),
            still,
        ],
        (weights, rows, counts, halo, sparse, precond, probes),
        scratch=[pltpu.VMEM((PROBES, PTS), f32)],
        grid=(CHUNKS,),
        out_specs=(still, pl.BlockSpec((32, 1, 128), lambda g: (0, 0, 0))),
        params=MIDDLE,
        moved=16 << 20,
    )


def update_kernel(
    rows, halo, probes, precond, counts, image,
    residual_out, search_out, packed_out, rounded_out, solution_out,
):
    alpha, beta = steps_of(row_total(rows))
    search = halo[FEAT:]
    solution_out[...] = alpha * search
    residual = probes[...] * live_lanes(counts[0, 0]) - alpha * image[...]
    residual_out[...] = residual
    following = precond[...] * residual + beta * search
    search_out[...] = following
    rounded = following.astype(bf16)
    rounded_out[...] = rounded
    packed_out[:PROBES] = rounded
    packed_out[PROBES:] = (following - rounded.astype(f32)).astype(bf16)


def update(rows, halo, probes, precond, counts, image):
    return call(
        update_kernel,
        "update",
        (
            FIELD,
            FIELD,
            shape(2 * PROBES, PTS, dtype=bf16),
            shape(PROBES, PTS, dtype=bf16),
            FIELD,
        ),
        [VMEM, VMEM, VMEM, VMEM, SMEM, VMEM],
        (rows, halo, probes, precond, counts, image),
    )


def sum_rows_kernel(rows, out):
    total = row_total(rows)
    for index in range(out.shape[0]):
        out[index] = total


def sum_rows(rows, count):
    return call(sum_rows_kernel, "sum_rows", shape(count, 1, 128), [VMEM], (rows,))


def sum_share_kernel(*refs):
    parts, out = refs[0], refs[-1]
    total = jnp.sum(parts[...], axis=0)
    if len(refs) == 3:
        total = jnp.concatenate([total, refs[1][...]], axis=0)
    out[...] = jnp.broadcast_to(total[None], out.shape)


def sum_share(parts, *sums):
    height = parts.shape[1] + sum(value.shape[0] for value in sums)
    return call(
        sum_share_kernel,
        "sum_share",
        shape(8, height, SHARE),
        [VMEM] * (1 + len(sums)),
        (parts, *sums),
    )


def sum_depth_kernel(parts, *outs):
    total = jnp.sum(parts[...], axis=0)
    for index, out in enumerate(outs):
        out[...] = total[index * PROBES : (index + 1) * PROBES]


def sum_depth(parts):
    count = parts.shape[1] // PROBES
    return call(
        sum_depth_kernel, "sum_depth", (shape(PROBES, SHARE),) * count, [VMEM], (parts,)
    )


def six_products(value, factors, dot):
    first, second, third = split3(value)
    total = dot(third.astype(bf16), factors[0][...])
    total = total + dot(second.astype(bf16), factors[1][...])
    total = total + dot(first.astype(bf16), factors[2][...])
    total = total + dot(second.astype(bf16), factors[0][...])
    total = total + dot(first.astype(bf16), factors[1][...])
    return total + dot(first.astype(bf16), factors[0][...])


def nn_dot(left, right):
    return jnp.dot(left, right, preferred_element_type=f32)


def coeffs_kernel(*refs):
    shares, factors, out = refs[:4], refs[4:7], refs[-1]
    value = jnp.concatenate([ref[...] for ref in shares], axis=1)
    terms = six_products(value, factors, nn_dot)
    if len(refs) == 9:
        terms = jnp.concatenate([terms, refs[7][...]], axis=1)
    out[...] = jnp.broadcast_to(terms[None], out.shape)


def coeff_terms(shares, factors, *sums):
    width = QUARTER + SHARE * len(sums)
    return call(
        coeffs_kernel,
        "coeffs",
        shape(8, PROBES, width),
        [VMEM] * (7 + len(sums)),
        (*shares, *factors, *sums),
    )


def weights_kernel(parts, first, second, third, *outs):
    total = jnp.sum(parts[...], axis=0)
    terms = six_products(total[:, :QUARTER], (first, second, third), nt_dot)
    for index, out in enumerate(outs):
        out[:, :SHARE] = terms[:, index * SHARE : (index + 1) * SHARE]
        if out.shape[1] > SHARE:
            out[:, SHARE:] = total[:, QUARTER:]


def weight_terms(parts, factors):
    width = SHARE + parts.shape[2] - QUARTER
    return call(
        weights_kernel,
        "weights",
        (shape(PROBES, width),) * 4,
        [VMEM] * 4,
        (parts, *factors),
    )


def gather_kernel(own, first, second, third, out):
    total = own[...] + first[...] + second[...] + third[...]
    out[...] = jnp.broadcast_to(total.astype(bf16)[None], out.shape)


def gather_weights(terms):
    return call(
        gather_kernel, "gather", shape(32, PROBES, SHARE, dtype=bf16), [VMEM] * 4, tuple(terms)
    )


def gather_last_kernel(own, first, second, third, rounded, rest, out, sums_out):
    total = own[...] + first[...] + second[...] + third[...]
    weights = total[:, :SHARE].astype(bf16)
    sums_out[...] = total[:, SHARE:]
    unrounded = rounded[...] + rest[...]
    dot = jnp.sum(weights.astype(f32) * unrounded, axis=1, keepdims=True)
    lane = lax.broadcasted_iota(jnp.int32, (PROBES, SHARE), 1)
    row = jnp.zeros((PROBES, SHARE), f32)
    for index, part in enumerate(split3(dot)):
        row = jnp.where(lane == index, part, row)
    both = jnp.concatenate([weights, row.astype(bf16)], axis=0)
    out[...] = jnp.broadcast_to(both[None], out.shape)


def gather_last(terms, rounded, rest):
    return call(
        gather_last_kernel,
        "gather_last",
        (shape(32, 2 * PROBES, SHARE, dtype=bf16), shape(PROBES, 128)),
        [VMEM] * 6,
        (*terms, rounded, rest),
    )


def finish_kernel(
    weights, rows, every, counts, search, sparse, residual, solution, sums, solution_out,
    residual_out, total,
):
    expand_step(weights, rows, total)

    @pl.when(pl.program_id(0) == CHUNKS - 1)
    def _():
        field = search[...]
        image = live_lanes(counts[0, 0]) * (field + sparse[...] + total[...])
        dots = jnp.sum(every[:, PROBES:].astype(f32), axis=0)
        dot = jnp.sum(dots, axis=1, keepdims=True)
        totals = sums[...]
        alpha = totals[:, 1:2] / (totals[:, 0:1] + dot)
        solution_out[...] = solution[...] + alpha * field
        residual_out[...] = residual[...] - alpha * image


def finish(weights, rows, counts, search, sparse, residual, solution, sums):
    still = pl.BlockSpec((PROBES, PTS), lambda g: (0, 0))
    height = weights.shape[1]
    return call(
        finish_kernel,
        "finish",
        (FIELD, FIELD),
        [
            pl.BlockSpec((4, height, SHARE), lambda g: (g, 0, 0)),
            pl.BlockSpec((1, PTS, CHUNK), lambda g: (g, 0, 0)),
            pl.BlockSpec((32, height, SHARE), lambda g: (0, 0, 0)),
            SMEM,
            still,
            still,
            still,
            still,
            pl.BlockSpec((PROBES, 128), lambda g: (0, 0)),
        ],
        (weights, rows, weights, counts, search, sparse, residual, solution, sums),
        scratch=[pltpu.VMEM((PROBES, PTS), f32)],
        grid=(CHUNKS,),
        out_specs=(still, still),
        params=MIDDLE,
        moved=16 << 20,
    )


def on_device(coords, probes, precond, counts, neighbours, inducing, factor):
    quad = lax.axis_index("yl") * 2 + lax.axis_index("c")
    sides = jnp.stack([lax.axis_index("c"), lax.axis_index("x") % 2]).reshape(1, 2)
    points = coords[0, 0]
    given = probes[0, 0]
    scaling = precond[0]
    codes = neighbours[0, 0]

    centre_parts, halo = prepare(points, given, scaling, counts, inducing[0])

    got = exchange(centre_parts, CELLS)
    factors = split_factor(after(quad.reshape(1), halo), factor)
    halos = surround(halo)
    got = after(got, halos[0], *factors)
    compacted = compact(got)
    centres = exchange(compacted, "z")
    tiles, sparse = make_tiles(codes, sides, after(halos[0], compacted), halos[1], halos[2])
    centres = after(centres, tiles, sparse)
    rows, parts = make_rows(halo, centres)

    def depth_of(got, *sums):
        return sum_depth(exchange(sum_share(got, *sums), "z"))

    def terms_of(depth):
        own = depth[0]
        shares = [own] + [quad_partner(own, step) for step in (1, 2, 3)]
        terms = exchange(coeff_terms(shares, factors, *depth[2:]), GY)
        terms = weight_terms(terms, factors)
        return [terms[0]] + [quad_partner(terms[step], step) for step in (1, 2, 3)]

    terms = terms_of(depth_of(exchange(parts, PLANE)))
    weights = exchange(gather_weights(terms), PLANE)
    image, row = make_image(weights, rows, counts, halo, sparse, scaling, given)
    row = exchange(sum_rows(exchange(row, CELLS), 8), "z")
    residual, search, packed, rounded, solution = update(
        row, halo, given, scaling, counts, image
    )

    parts = project(packed, rows)
    nears = surround(rounded, parts)
    got = exchange(after(parts, nears[0]), PLANE)
    sparse, sums = apply_tiles(
        codes, sides, (after(nears[0], got),) + nears[1:], tiles, search, residual, scaling
    )
    depth = depth_of(got, sums)
    weights, totals = gather_last(terms_of(depth), depth[0], depth[1])
    weights = exchange(weights, PLANE)
    solution, residual = finish(
        weights, rows, counts, search, sparse, residual, solution, totals
    )
    return (solution[None, None], residual[None, None])


def solution(mesh):
    fine = Mesh(mesh.devices.reshape(8, 2, 2, 2, 4), ALL)
    placed = (
        P(GX, GY, None, None),
        P(GX, GY, None, None),
        P(GX, GY, None),
        P(GX, GY),
        P(GX, GY, None, None),
        P(GX, GY, None),
        P(GY, None),
    )
    return jax.shard_map(
        on_device,
        mesh=fine,
        in_specs=placed,
        out_specs=(P(GX, GY, None, None), P(GX, GY, None, None)),
        check_vma=False,
    )
```

```python
import functools

import jax
import jax.numpy as jnp
from jax import lax
from jax.experimental import pallas as pl
from jax.experimental.pallas import tpu as pltpu
from jax.sharding import Mesh, PartitionSpec as P

FEAT = 8
BLOCK = 128
PROBES = 16
PTS = 1024
SHARE = 128
CHUNK = 512
CHUNKS = 8
CAP = 8
EMPTY = 72
HALF = 4
QUARTER = 1024

support_radius = 0.32
width_sq = 0.045
LOG2E = 1.4426950408889634

ALL = ("z", "yl", "c", "yh", "x")
PLANE = ("yh", "x", "yl", "c")
GX = ("z", "yl", "c")
GY = ("yh", "x")
f32 = jnp.float32
bf16 = jnp.bfloat16

VMEM = pl.BlockSpec(memory_space=pltpu.VMEM)
SMEM = pl.BlockSpec(memory_space=pltpu.SMEM)
SMALL = pltpu.CompilerParams(vmem_limit_bytes=16 * 1024 * 1024)
MIDDLE = pltpu.CompilerParams(vmem_limit_bytes=24 * 1024 * 1024)
LARGE = pltpu.CompilerParams(vmem_limit_bytes=57 * 1024 * 1024)


def exchange(parts, axes):
    return lax.all_to_all(parts, axes, 0, 0, tiled=True)


def quad_partner(value, step):
    pairs = [(i, i ^ step) for i in range(4)]
    return lax.ppermute(value, ("yl", "c"), pairs)


def even_pairs(value, axes):
    return lax.ppermute(value, axes, [(i, i ^ 1) for i in range(lax.axis_size(axes))])


def odd_pairs(value, axes):
    count = lax.axis_size(axes)
    pairs = [(i, i + 1) for i in range(1, count - 1, 2)]
    return lax.ppermute(value, axes, pairs + [(j, i) for i, j in pairs])


def after(value, *others):
    return lax.optimization_barrier((value,) + others)[0]


def split3(value):
    first = value.astype(bf16).astype(f32)
    rest = value - first
    second = rest.astype(bf16).astype(f32)
    return first, second, (rest - second).astype(bf16).astype(f32)


def augmented(points, scale, left):
    centred = points - 0.5
    norm = scale * jnp.sum(centred * centred, axis=0, keepdims=True)
    norms = [jnp.broadcast_to(part, points.shape) for part in split3(norm)]
    row = lax.broadcasted_iota(jnp.int32, points.shape, 0)
    if left:
        one, two, three = split3(centred)
        order = [one, one, two, one, two, three]
        base = 0
    else:
        one, two, three = split3((-2.0 * scale) * centred)
        order = [one, two, one, three, two, one]
        base = 3
    extra = jnp.where(row < 6, 1.0, 0.0)
    for index, part in enumerate(norms):
        extra = jnp.where(row == base + index, part, extra)
    return jnp.concatenate(order + [extra, jnp.zeros_like(extra)], axis=0).astype(bf16)


def as_lanes(column, offset):
    row = lax.broadcasted_iota(jnp.int32, (PROBES, 128), 0)
    lane = lax.broadcasted_iota(jnp.int32, (PROBES, 128), 1)
    return jnp.sum(jnp.where(lane == row + offset, column, 0.0), axis=0, keepdims=True)


def as_column(row_value, offset):
    row = lax.broadcasted_iota(jnp.int32, (PROBES, 128), 0)
    lane = lax.broadcasted_iota(jnp.int32, (PROBES, 128), 1)
    return jnp.sum(jnp.where(lane == row + offset, row_value, 0.0), axis=1, keepdims=True)


def live_lanes(count):
    lane = lax.broadcasted_iota(jnp.int32, (1, PTS), 1)
    return jnp.where(lane < count, 1.0, 0.0)


def nt_dot(left, right):
    return lax.dot_general(left, right, (((1,), (1,)), ((), ())), preferred_element_type=f32)


def call(kernel, name, out_shape, in_specs, args, scratch=(), grid=None, out_specs=None, params=SMALL, flops=0, moved=0):
    if out_specs is None:
        out_specs = jax.tree.map(lambda _: VMEM, out_shape)
    options = {} if grid is None else {"grid": grid}
    return pl.pallas_call(
        kernel,
        out_shape=out_shape,
        in_specs=in_specs,
        out_specs=out_specs,
        scratch_shapes=list(scratch),
        compiler_params=params,
        cost_estimate=pl.CostEstimate(flops=flops, bytes_accessed=moved, transcendentals=0),
        name=name,
        **options,
    )(*args)


def shape(*dims, dtype=f32):
    return jax.ShapeDtypeStruct(dims, dtype)


FIELD = shape(PROBES, PTS)


def prepare_kernel(place, coords, probes, precond, counts, inducing, centre_out, halo_out):
    points = coords[...]
    lane = lax.broadcasted_iota(jnp.int32, (FEAT, PTS), 1)
    short = lax.broadcasted_iota(jnp.int32, (FEAT, 128), 1)
    centre = jnp.zeros((FEAT, 128), f32)
    for index in range(16):
        picked = jnp.sum(
            jnp.where(lane == inducing[0, index], points, 0.0), axis=1, keepdims=True
        )
        centre = jnp.where(short == index, picked, centre)
    row = centre[:1]
    for feature in range(1, FEAT):
        row = row + pltpu.roll(centre, 128 - 16 * feature, 1)[feature : feature + 1]
    centre_out[...] = jnp.broadcast_to(row[None], centre_out.shape)
    halo_out[:FEAT] = points
    halo_out[FEAT:] = precond[...] * (probes[...] * live_lanes(counts[0, 0]))


def prepare(place, coords, probes, precond, counts, inducing):
    return call(
        prepare_kernel,
        "prepare",
        (shape(256, 1, 128), shape(FEAT + PROBES, PTS)),
        [SMEM, VMEM, VMEM, VMEM, SMEM, SMEM],
        (place, coords, probes, precond, counts, inducing),
        params=LARGE,
    )


def factor_kernel(place, columns, first_out, second_out, third_out):
    for index in range(4):
        start = pl.multiple_of((place[0, 0] ^ index) * SHARE, SHARE)
        parts = split3(columns[pl.ds(start, SHARE), :])
        for out, part in zip((first_out, second_out, third_out), parts):
            out[index * SHARE : (index + 1) * SHARE] = part.astype(bf16)


def split_factor(place, columns):
    return call(
        factor_kernel,
        "factor",
        (shape(4 * SHARE, QUARTER, dtype=bf16),) * 3,
        [SMEM, VMEM],
        (place, columns),
        moved=8 << 20,
    )


def centre_columns(parts):
    group = lax.broadcasted_iota(jnp.int32, (8, 128), 1) // 16
    tiles = []
    for index in range(4):
        tile = pltpu.roll(parts[8 * index : 8 * index + 8], 0, 1, stride=16, stride_axis=0)
        for bit in (1, 2, 4):
            tile = jnp.where(group & bit != 0, pltpu.roll(tile, 8 - bit, 0), tile)
        tiles.append(pltpu.roll(tile, 0, 1, stride=16, stride_axis=0))
    return jnp.concatenate(tiles, axis=1)


def rows_kernel(halo, centres, rows_out, sums_out, left, packed):
    @pl.when(pl.program_id(0) == 0)
    def _():
        left[...] = augmented(halo[:FEAT], -LOG2E / width_sq, True).astype(f32).T.astype(bf16)
        packed[...] = halo[FEAT:].astype(bf16)

    right = augmented(centre_columns(centres[...]), -LOG2E / width_sq, False)
    power = jnp.dot(left[...], right, preferred_element_type=f32)
    rows = jnp.exp2(jnp.minimum(power, 0.0)).astype(bf16)
    rows_out[0] = rows
    sums = jnp.dot(packed[...], rows, preferred_element_type=f32)
    for part in range(4):
        sums_out[part] = sums[:, part * SHARE : (part + 1) * SHARE]


def make_rows(halo, centres):
    return call(
        rows_kernel,
        "rows",
        (shape(CHUNKS, PTS, CHUNK, dtype=bf16), shape(32, PROBES, SHARE)),
        [
            pl.BlockSpec((FEAT + PROBES, PTS), lambda g: (0, 0)),
            pl.BlockSpec((32, 128), lambda g: (g, 0)),
        ],
        (halo, centres),
        scratch=[pltpu.VMEM((PTS, 64), bf16), pltpu.VMEM((PROBES, PTS), bf16)],
        grid=(CHUNKS,),
        out_specs=(
            pl.BlockSpec((1, PTS, CHUNK), lambda g: (g, 0, 0)),
            pl.BlockSpec((4, PROBES, SHARE), lambda g: (g, 0, 0)),
        ),
        params=MIDDLE,
        moved=16 << 20,
    )


def project_kernel(packed, rows, sums_out):
    sums = jnp.dot(packed[...], rows[0], preferred_element_type=f32)
    for part in range(4):
        sums_out[part] = sums[:, part * SHARE : (part + 1) * SHARE]


def project(packed, rows):
    height = packed.shape[0]
    return call(
        project_kernel,
        "project",
        shape(32, height, SHARE),
        [
            pl.BlockSpec((height, PTS), lambda g: (0, 0)),
            pl.BlockSpec((1, PTS, CHUNK), lambda g: (g, 0, 0)),
        ],
        (packed, rows),
        grid=(CHUNKS,),
        out_specs=pl.BlockSpec((4, height, SHARE), lambda g: (g, 0, 0)),
        params=MIDDLE,
        moved=16 << 20,
    )


def fill_table(table, place, sources, first, last, dtype):
    places_x = (1, 2 - 2 * place[0, 1], 2 * place[0, 1])
    places_y = (1, 2 - 2 * place[0, 2], 2 * place[0, 2])
    for place_y, source in zip(places_y, sources):
        for index, place_x in enumerate(places_x):
            start = (place_x * 3 + place_y) * CAP
            values = source[index, first:last].astype(dtype)
            for block in range(CAP):
                table[start + block] = values[:, block * BLOCK : (block + 1) * BLOCK]
    table[EMPTY] = jnp.zeros(table.shape[1:], dtype)


def partners(table, codes, block):
    return jnp.concatenate([table[codes[block, entry]] for entry in range(CAP)], axis=1)


def tiles_kernel(base, codes, place, near, even, odd, tiles_out, sparse_out, points, values):
    block = base + pl.program_id(0)

    @pl.when(pl.program_id(0) == 0)
    def _():
        fill_table(points, place, (near, even, odd), 0, FEAT, f32)
        fill_table(values, place, (near, even, odd), FEAT, FEAT + PROBES, bf16)

    scale = 1.0 / (support_radius * support_radius)
    own = augmented(points[4 * CAP + block], scale, True).astype(f32).T.astype(bf16)
    other = augmented(partners(points, codes, block), scale, False)
    square = jnp.maximum(jnp.dot(own, other, preferred_element_type=f32), 0.0)
    ratio = jnp.sqrt(square)
    remain = jnp.maximum(1.0 - ratio, 0.0)
    second = remain * remain
    fourth = second * second
    tile = (fourth * second * remain * (7.0 * ratio + 1.0)).astype(bf16)
    tiles_out[0] = tile
    sparse_out[...] = nt_dot(partners(values, codes, block), tile)


def make_tiles(half, codes, place, near, even, odd):
    whole = pl.BlockSpec((3, FEAT + PROBES, PTS), lambda b: (0, 0, 0))
    return call(
        functools.partial(tiles_kernel, half * HALF),
        "tiles",
        (shape(HALF, BLOCK, PTS, dtype=bf16), shape(PROBES, HALF * BLOCK)),
        [SMEM, SMEM, whole, whole, whole],
        (codes, place, near, even, odd),
        scratch=[
            pltpu.VMEM((EMPTY + 1, FEAT, BLOCK), f32),
            pltpu.VMEM((EMPTY + 1, PROBES, BLOCK), bf16),
        ],
        grid=(HALF,),
        out_specs=(
            pl.BlockSpec((1, BLOCK, PTS), lambda b: (b, 0, 0)),
            pl.BlockSpec((PROBES, BLOCK), lambda b: (0, b)),
        ),
        moved=8 << 20,
    )


def steps_of(row):
    rz_now = as_column(row, 0)
    alpha = rz_now / as_column(row, 16)
    return alpha, alpha * alpha * as_column(row, 32) / rz_now - 1.0


def sparse_kernel(
    codes, place, near, even, odd, tiles_low, tiles_high, search, residual, precond,
    sparse_out, sums_out, values,
):
    fill_table(values, place, (near, even, odd), 0, PROBES, bf16)
    for block in range(CAP):
        sparse_out[:, block * BLOCK : (block + 1) * BLOCK] = nt_dot(
            partners(values, codes, block), (tiles_low, tiles_high)[block // HALF][block % HALF]
        )
    field = search[...]
    left = residual[...]
    curve = jnp.sum(field * (field + sparse_out[...]), axis=1, keepdims=True)
    norm = jnp.sum(left * (precond[...] * left), axis=1, keepdims=True)
    lane = lax.broadcasted_iota(jnp.int32, (PROBES, 128), 1)
    sums_out[...] = jnp.where(lane == 0, curve, jnp.where(lane == 1, norm, 0.0))


def apply_tiles(codes, place, nears, tiles, search, residual, precond):
    return call(
        sparse_kernel,
        "sparse",
        (FIELD, shape(PROBES, 128)),
        [SMEM, SMEM] + [VMEM] * 8,
        (codes, place, *nears, *tiles, search, residual, precond),
        scratch=[pltpu.VMEM((EMPTY + 1, PROBES, BLOCK), bf16)],
        moved=6 << 20,
    )


def stack_kernel(own, even, odd, out):
    out[0] = own[...]
    out[1] = even[...]
    out[2] = odd[...]


def surround(value, even, odd):
    column = call(
        stack_kernel,
        "stack",
        shape(3, *value.shape, dtype=value.dtype),
        [VMEM] * 3,
        (value, even, odd),
    )
    return column, even_pairs(column, GY), odd_pairs(column, GY)


def expand_step(weights, rows, total):
    @pl.when(pl.program_id(0) == 0)
    def _():
        total[...] = jnp.zeros_like(total)

    part = jnp.concatenate([weights[i, :PROBES] for i in range(4)], axis=1)
    total[...] += nt_dot(part, rows[0])


def image_kernel(
    weights, rows, counts, halo, sparse_low, sparse_high, precond, probes, image_out, sums_out, total
):
    expand_step(weights, rows, total)

    @pl.when(pl.program_id(0) == CHUNKS - 1)
    def _():
        search = halo[FEAT:]
        live = live_lanes(counts[0, 0])
        sparse = jnp.concatenate([sparse_low[...], sparse_high[...]], axis=1)
        image = live * (search + sparse + total[...])
        image_out[...] = image
        norm = jnp.sum(search * (probes[...] * live), axis=1, keepdims=True)
        curve = jnp.sum(search * image, axis=1, keepdims=True)
        square = jnp.sum(precond[...] * image * image, axis=1, keepdims=True)
        row = as_lanes(norm, 0) + as_lanes(curve, 16) + as_lanes(square, 32)
        sums_out[...] = jnp.broadcast_to(row[None], sums_out.shape)


def make_image(weights, rows, counts, halo, sparse, precond, probes):
    height = weights.shape[1]
    still = pl.BlockSpec((PROBES, PTS), lambda g: (0, 0))
    half = pl.BlockSpec((PROBES, HALF * BLOCK), lambda g: (0, 0))
    return call(
        image_kernel,
        "image",
        (FIELD, shape(256, 1, 128)),
        [
            pl.BlockSpec((4, height, SHARE), lambda g: (g, 0, 0)),
            pl.BlockSpec((1, PTS, CHUNK), lambda g: (g, 0, 0)),
            SMEM,
            pl.BlockSpec((FEAT + PROBES, PTS), lambda g: (0, 0)),
            half,
            half,
            pl.BlockSpec((1, PTS), lambda g: (0, 0)),
            still,
        ],
        (weights, rows, counts, halo, *sparse, precond, probes),
        scratch=[pltpu.VMEM((PROBES, PTS), f32)],
        grid=(CHUNKS,),
        out_specs=(still, pl.BlockSpec((256, 1, 128), lambda g: (0, 0, 0))),
        params=MIDDLE,
        moved=16 << 20,
    )


def update_kernel(
    rows, halo, probes, precond, counts, image,
    residual_out, search_out, packed_out, rounded_out, solution_out,
):
    alpha, beta = steps_of(jnp.sum(rows[...], axis=0))
    search = halo[FEAT:]
    solution_out[...] = alpha * search
    residual = probes[...] * live_lanes(counts[0, 0]) - alpha * image[...]
    residual_out[...] = residual
    following = precond[...] * residual + beta * search
    search_out[...] = following
    rounded = following.astype(bf16)
    rounded_out[...] = rounded
    packed_out[:PROBES] = rounded
    packed_out[PROBES:] = (following - rounded.astype(f32)).astype(bf16)


def update(rows, halo, probes, precond, counts, image):
    return call(
        update_kernel,
        "update",
        (
            FIELD,
            FIELD,
            shape(2 * PROBES, PTS, dtype=bf16),
            shape(PROBES, PTS, dtype=bf16),
            FIELD,
        ),
        [VMEM, VMEM, VMEM, VMEM, SMEM, VMEM],
        (rows, halo, probes, precond, counts, image),
    )


def sum_share_kernel(*refs):
    parts, out = refs[0], refs[-1]
    total = jnp.sum(parts[...], axis=0)
    if len(refs) == 3:
        total = jnp.concatenate([total, refs[1][...]], axis=0)
    out[...] = jnp.broadcast_to(total[None], out.shape)


def sum_share(parts, *sums):
    height = parts.shape[1] + sum(value.shape[0] for value in sums)
    return call(
        sum_share_kernel,
        "sum_share",
        shape(8, height, SHARE),
        [VMEM] * (1 + len(sums)),
        (parts, *sums),
    )


def sum_depth_kernel(parts, *outs):
    total = jnp.sum(parts[...], axis=0)
    for index, out in enumerate(outs):
        out[...] = total[index * PROBES : (index + 1) * PROBES]


def sum_depth(parts):
    count = parts.shape[1] // PROBES
    return call(
        sum_depth_kernel, "sum_depth", (shape(PROBES, SHARE),) * count, [VMEM], (parts,)
    )


def six_products(value, factors, dot):
    first, second, third = split3(value)
    stacked = jnp.concatenate([third, second, first], axis=0).astype(bf16)
    by_first = dot(stacked, factors[0][...])
    by_second = dot(stacked[PROBES:], factors[1][...])
    by_third = dot(stacked[2 * PROBES :], factors[2][...])
    small = by_first[:PROBES] + by_second[:PROBES] + by_third
    middle = by_first[PROBES : 2 * PROBES] + by_second[PROBES:]
    return by_first[2 * PROBES :] + (middle + small)


def nn_dot(left, right):
    return jnp.dot(left, right, preferred_element_type=f32)


def coeffs_kernel(*refs):
    shares, factors, out = refs[:4], refs[4:7], refs[-1]
    value = jnp.concatenate([ref[...] for ref in shares], axis=1)
    terms = six_products(value, factors, nn_dot)
    if len(refs) == 9:
        terms = jnp.concatenate([terms, refs[7][...]], axis=1)
    out[...] = jnp.broadcast_to(terms[None], out.shape)


def coeff_terms(shares, factors, *sums):
    width = QUARTER + SHARE * len(sums)
    return call(
        coeffs_kernel,
        "coeffs",
        shape(8, PROBES, width),
        [VMEM] * (7 + len(sums)),
        (*shares, *factors, *sums),
    )


def weights_kernel(parts, first, second, third, *outs):
    total = jnp.sum(parts[...], axis=0)
    terms = six_products(total[:, :QUARTER], (first, second, third), nt_dot)
    for index, out in enumerate(outs):
        out[:, :SHARE] = terms[:, index * SHARE : (index + 1) * SHARE]
        if out.shape[1] > SHARE:
            out[:, SHARE:] = total[:, QUARTER:]


def weight_terms(parts, factors):
    width = SHARE + parts.shape[2] - QUARTER
    return call(
        weights_kernel,
        "weights",
        (shape(PROBES, width),) * 4,
        [VMEM] * 4,
        (parts, *factors),
    )


def gather_kernel(own, first, second, third, out):
    total = own[...] + first[...] + second[...] + third[...]
    out[...] = jnp.broadcast_to(total.astype(bf16)[None], out.shape)


def gather_weights(terms):
    return call(
        gather_kernel, "gather", shape(32, PROBES, SHARE, dtype=bf16), [VMEM] * 4, tuple(terms)
    )


def gather_last_kernel(own, first, second, third, rounded, rest, out, sums_out):
    total = own[...] + first[...] + second[...] + third[...]
    weights = total[:, :SHARE].astype(bf16)
    sums_out[...] = total[:, SHARE:]
    unrounded = rounded[...] + rest[...]
    dot = jnp.sum(weights.astype(f32) * unrounded, axis=1, keepdims=True)
    lane = lax.broadcasted_iota(jnp.int32, (PROBES, SHARE), 1)
    row = jnp.zeros((PROBES, SHARE), f32)
    for index, part in enumerate(split3(dot)):
        row = jnp.where(lane == index, part, row)
    both = jnp.concatenate([weights, row.astype(bf16)], axis=0)
    out[...] = jnp.broadcast_to(both[None], out.shape)


def gather_last(terms, rounded, rest):
    return call(
        gather_last_kernel,
        "gather_last",
        (shape(32, 2 * PROBES, SHARE, dtype=bf16), shape(PROBES, 128)),
        [VMEM] * 6,
        (*terms, rounded, rest),
    )


def finish_kernel(
    weights, rows, every, counts, search, sparse, residual, solution, sums, solution_out,
    residual_out, total,
):
    expand_step(weights, rows, total)

    @pl.when(pl.program_id(0) == CHUNKS - 1)
    def _():
        field = search[...]
        image = live_lanes(counts[0, 0]) * (field + sparse[...] + total[...])
        dots = jnp.sum(every[:, PROBES:].astype(f32), axis=0)
        dot = jnp.sum(dots, axis=1, keepdims=True)
        totals = sums[...]
        alpha = totals[:, 1:2] / (totals[:, 0:1] + dot)
        solution_out[...] = solution[...] + alpha * field
        residual_out[...] = residual[...] - alpha * image


def finish(weights, rows, counts, search, sparse, residual, solution, sums):
    still = pl.BlockSpec((PROBES, PTS), lambda g: (0, 0))
    height = weights.shape[1]
    return call(
        finish_kernel,
        "finish",
        (FIELD, FIELD),
        [
            pl.BlockSpec((4, height, SHARE), lambda g: (g, 0, 0)),
            pl.BlockSpec((1, PTS, CHUNK), lambda g: (g, 0, 0)),
            pl.BlockSpec((32, height, SHARE), lambda g: (0, 0, 0)),
            SMEM,
            still,
            still,
            still,
            still,
            pl.BlockSpec((PROBES, 128), lambda g: (0, 0)),
        ],
        (weights, rows, weights, counts, search, sparse, residual, solution, sums),
        scratch=[pltpu.VMEM((PROBES, PTS), f32)],
        grid=(CHUNKS,),
        out_specs=(still, still),
        params=MIDDLE,
        moved=16 << 20,
    )


def on_device(coords, probes, precond, counts, neighbours, inducing, factor):
    quad = lax.axis_index("yl") * 2 + lax.axis_index("c")
    place = jnp.stack([quad, lax.axis_index("c"), lax.axis_index("x") & 1]).reshape(1, 3)
    points = coords[0, 0]
    given = probes[0, 0]
    scaling = precond[0]
    codes = neighbours[0, 0]

    centre_parts, halo = prepare(place, points, given, scaling, counts, inducing[0])

    even, odd = even_pairs(halo, GX), odd_pairs(halo, GX)
    centres = exchange(centre_parts, ALL).reshape(256, 128)
    halos = surround(after(halo, centres), even, odd)
    columns = lax.dynamic_slice_in_dim(after(factor, halos[0]), quad * QUARTER, QUARTER, 1)
    factors = split_factor(place, columns)
    rows, parts = make_rows(halo, after(centres, halos[0], *factors))
    parts = after(parts, *halos)

    def depth_of(got, *sums):
        return sum_depth(exchange(sum_share(got, *sums), "z"))

    def coeffs_of(depth, beside):
        own = depth[0]
        shares = [own] + [quad_partner(own, step) for step in (1, 2, 3)]
        shares[0] = after(own, *beside)
        return exchange(coeff_terms(shares, factors, *depth[2:]), GY)

    def terms_of(coeffs):
        terms = weight_terms(coeffs, factors)
        return [terms[0]] + [quad_partner(terms[step], step) for step in (1, 2, 3)]

    depth = depth_of(exchange(parts, PLANE))
    low = make_tiles(0, codes, place, after(halos[0], depth[0]), *halos[1:])
    coeffs = coeffs_of(depth, low)
    terms = weight_terms(coeffs, factors)
    high = make_tiles(1, codes, place, after(halos[0], terms[0]), *halos[1:])
    terms = [after(terms[0], *high)] + [quad_partner(terms[step], step) for step in (1, 2, 3)]
    weights = exchange(gather_weights(terms), PLANE)
    tiles, sparse = zip(low, high)
    image, row = make_image(weights, rows, counts, halo, sparse, scaling, given)
    row = exchange(row, ALL)
    residual, search, packed, rounded, solution = update(
        row, halo, given, scaling, counts, image
    )

    even, odd = even_pairs(rounded, GX), odd_pairs(rounded, GX)
    parts = project(packed, rows)

    nears = surround(after(rounded, parts), even, odd)
    got = exchange(after(parts, nears[0]), PLANE)
    sparse, sums = apply_tiles(
        codes, place, (after(nears[0], got),) + nears[1:], tiles, search, residual, scaling
    )
    depth = depth_of(got, sums)
    weights, totals = gather_last(terms_of(coeffs_of(depth, ())), depth[0], depth[1])
    weights = exchange(weights, PLANE)
    solution, residual = finish(
        weights, rows, counts, search, sparse, residual, solution, totals
    )
    return (solution[None, None], residual[None, None])


def solution(mesh):
    fine = Mesh(mesh.devices.reshape(8, 2, 2, 2, 4), ALL)
    placed = (
        P(GX, GY, None, None),
        P(GX, GY, None, None),
        P(GX, GY, None),
        P(GX, GY),
        P(GX, GY, None, None),
        P(GX, GY, None),
        P(GY, None),
    )
    return jax.shard_map(
        on_device,
        mesh=fine,
        in_specs=placed,
        out_specs=(P(GX, GY, None, None), P(GX, GY, None, None)),
        check_vma=False,
    )
```

```python
import functools

import jax
import jax.numpy as jnp
from jax import lax
from jax.experimental import pallas as pl
from jax.experimental.pallas import tpu as pltpu
from jax.sharding import Mesh, PartitionSpec as P

FEAT = 8
BLOCK = 128
PROBES = 16
PTS = 1024
SHARE = 128
CHUNK = 512
CHUNKS = 8
CAP = 8
EMPTY = 72
HALF = 4
QUARTER = 1024

support_radius = 0.32
width_sq = 0.045
LOG2E = 1.4426950408889634

ALL = ("z", "yl", "c", "yh", "x")
PLANE = ("yh", "x", "yl", "c")
GX = ("z", "yl", "c")
GY = ("yh", "x")
f32 = jnp.float32
bf16 = jnp.bfloat16

VMEM = pl.BlockSpec(memory_space=pltpu.VMEM)
SMEM = pl.BlockSpec(memory_space=pltpu.SMEM)
SMALL = pltpu.CompilerParams(vmem_limit_bytes=16 * 1024 * 1024)
MIDDLE = pltpu.CompilerParams(vmem_limit_bytes=24 * 1024 * 1024)
LARGE = pltpu.CompilerParams(vmem_limit_bytes=57 * 1024 * 1024)


def exchange(parts, axes):
    return lax.all_to_all(parts, axes, 0, 0, tiled=True)


def quad_index():
    return lax.axis_index("yl") * 2 + lax.axis_index("c")


def quad_partner(value, step):
    pairs = [(i, i ^ step) for i in range(4)]
    return lax.ppermute(value, ("yl", "c"), pairs)


def even_pairs(value, axes):
    return lax.ppermute(value, axes, [(i, i ^ 1) for i in range(lax.axis_size(axes))])


def odd_pairs(value, axes):
    count = lax.axis_size(axes)
    pairs = [(i, i + 1) for i in range(1, count - 1, 2)]
    return lax.ppermute(value, axes, pairs + [(j, i) for i, j in pairs])


def after(value, *others):
    return lax.optimization_barrier((value,) + others)[0]


def split3(value):
    first = value.astype(bf16).astype(f32)
    rest = value - first
    second = rest.astype(bf16).astype(f32)
    return first, second, (rest - second).astype(bf16).astype(f32)


def augmented(points, scale, left):
    centred = points - 0.5
    norm = scale * jnp.sum(centred * centred, axis=0, keepdims=True)
    norms = [jnp.broadcast_to(part, points.shape) for part in split3(norm)]
    row = lax.broadcasted_iota(jnp.int32, points.shape, 0)
    if left:
        one, two, three = split3(centred)
        order = [one, one, two, one, two, three]
        base = 0
    else:
        one, two, three = split3((-2.0 * scale) * centred)
        order = [one, two, one, three, two, one]
        base = 3
    extra = jnp.where(row < 6, 1.0, 0.0)
    for index, part in enumerate(norms):
        extra = jnp.where(row == base + index, part, extra)
    return jnp.concatenate(order + [extra, jnp.zeros_like(extra)], axis=0).astype(bf16)


def as_lanes(column, offset):
    row = lax.broadcasted_iota(jnp.int32, (PROBES, 128), 0)
    lane = lax.broadcasted_iota(jnp.int32, (PROBES, 128), 1)
    return jnp.sum(jnp.where(lane == row + offset, column, 0.0), axis=0, keepdims=True)


def as_column(row_value, offset):
    row = lax.broadcasted_iota(jnp.int32, (PROBES, 128), 0)
    lane = lax.broadcasted_iota(jnp.int32, (PROBES, 128), 1)
    return jnp.sum(jnp.where(lane == row + offset, row_value, 0.0), axis=1, keepdims=True)


def live_lanes(count):
    lane = lax.broadcasted_iota(jnp.int32, (1, PTS), 1)
    return jnp.where(lane < count, 1.0, 0.0)


def nt_dot(left, right):
    return lax.dot_general(left, right, (((1,), (1,)), ((), ())), preferred_element_type=f32)


def call(kernel, name, out_shape, in_specs, args, scratch=(), grid=None, out_specs=None, params=SMALL, flops=0, moved=0):
    if out_specs is None:
        out_specs = jax.tree.map(lambda _: VMEM, out_shape)
    options = {} if grid is None else {"grid": grid}
    return pl.pallas_call(
        kernel,
        out_shape=out_shape,
        in_specs=in_specs,
        out_specs=out_specs,
        scratch_shapes=list(scratch),
        compiler_params=params,
        cost_estimate=pl.CostEstimate(flops=flops, bytes_accessed=moved, transcendentals=0),
        name=name,
        **options,
    )(*args)


def shape(*dims, dtype=f32):
    return jax.ShapeDtypeStruct(dims, dtype)


FIELD = shape(PROBES, PTS)


def prepare_kernel(coords, probes, precond, counts, inducing, centre_out, halo_out):
    points = coords[...]
    lane = lax.broadcasted_iota(jnp.int32, (FEAT, PTS), 1)
    short = lax.broadcasted_iota(jnp.int32, (FEAT, 128), 1)
    centre = jnp.zeros((FEAT, 128), f32)
    for index in range(16):
        picked = jnp.sum(
            jnp.where(lane == inducing[0, index], points, 0.0), axis=1, keepdims=True
        )
        centre = jnp.where(short == index, picked, centre)
    row = centre[:1]
    for feature in range(1, FEAT):
        row = row + pltpu.roll(centre, 128 - 16 * feature, 1)[feature : feature + 1]
    centre_out[...] = jnp.broadcast_to(row[None], centre_out.shape)
    halo_out[:FEAT] = points
    halo_out[FEAT:] = precond[...] * (probes[...] * live_lanes(counts[0, 0]))


def prepare(coords, probes, precond, counts, inducing):
    return call(
        prepare_kernel,
        "prepare",
        (shape(256, 1, 128), shape(FEAT + PROBES, PTS)),
        [VMEM, VMEM, VMEM, SMEM, SMEM],
        (coords, probes, precond, counts, inducing),
        params=LARGE,
    )


def factor_kernel(columns, first_out, second_out, third_out):
    quad = quad_index()
    for index in range(4):
        start = pl.multiple_of((quad ^ index) * SHARE, SHARE)
        parts = split3(columns[pl.ds(start, SHARE), :])
        for out, part in zip((first_out, second_out, third_out), parts):
            out[index * SHARE : (index + 1) * SHARE] = part.astype(bf16)


def split_factor(columns):
    return call(
        factor_kernel,
        "factor",
        (shape(4 * SHARE, QUARTER, dtype=bf16),) * 3,
        [VMEM],
        (columns,),
        moved=8 << 20,
    )


def centre_columns(parts):
    group = lax.broadcasted_iota(jnp.int32, (8, 128), 1) // 16
    tiles = []
    for index in range(4):
        tile = pltpu.roll(parts[8 * index : 8 * index + 8], 0, 1, stride=16, stride_axis=0)
        for bit in (1, 2, 4):
            tile = jnp.where(group & bit != 0, pltpu.roll(tile, 8 - bit, 0), tile)
        tiles.append(pltpu.roll(tile, 0, 1, stride=16, stride_axis=0))
    return jnp.concatenate(tiles, axis=1)


def rows_kernel(halo, centres, rows_out, sums_out, left, packed):
    left[...] = augmented(halo[:FEAT], -LOG2E / width_sq, True).astype(f32).T.astype(bf16)
    packed[...] = halo[FEAT:].astype(bf16)

    def chunk(step, carry):
        cells = centres[pl.ds(pl.multiple_of(step * 32, 32), 32), :]
        right = augmented(centre_columns(cells), -LOG2E / width_sq, False)
        power = jnp.dot(left[...], right, preferred_element_type=f32)
        rows = jnp.exp2(jnp.minimum(power, 0.0)).astype(bf16)
        rows_out[step] = rows
        sums = jnp.dot(packed[...], rows, preferred_element_type=f32)
        for part in range(4):
            sums_out[4 * step + part] = sums[:, part * SHARE : (part + 1) * SHARE]
        return carry

    lax.fori_loop(0, CHUNKS, chunk, 0, unroll=2)


def make_rows(halo, centres):
    return call(
        rows_kernel,
        "rows",
        (shape(CHUNKS, PTS, CHUNK, dtype=bf16), shape(32, PROBES, SHARE)),
        [VMEM, VMEM],
        (halo, centres),
        scratch=[pltpu.VMEM((PTS, 64), bf16), pltpu.VMEM((PROBES, PTS), bf16)],
        params=MIDDLE,
        moved=16 << 20,
    )


def project_kernel(packed, rows, sums_out):
    for step in range(CHUNKS):
        sums = jnp.dot(packed[...], rows[step], preferred_element_type=f32)
        for part in range(4):
            sums_out[4 * step + part] = sums[:, part * SHARE : (part + 1) * SHARE]


def project(packed, rows):
    return call(
        project_kernel,
        "project",
        shape(32, packed.shape[0], SHARE),
        [VMEM, VMEM],
        (packed, rows),
        params=MIDDLE,
        moved=16 << 20,
    )


def fill_table(table, sources, first, last, dtype):
    side_x, side_y = lax.axis_index("c"), lax.axis_index("x") & 1
    places_x = (1, 2 - 2 * side_x, 2 * side_x)
    places_y = (1, 2 - 2 * side_y, 2 * side_y)
    for place_y, source in zip(places_y, sources):
        for index, place_x in enumerate(places_x):
            start = (place_x * 3 + place_y) * CAP
            values = source[index, first:last].astype(dtype)
            for block in range(CAP):
                table[start + block] = values[:, block * BLOCK : (block + 1) * BLOCK]
    table[EMPTY] = jnp.zeros(table.shape[1:], dtype)


def partners(table, codes, block):
    return jnp.concatenate([table[codes[block, entry]] for entry in range(CAP)], axis=1)


def tiles_kernel(base, codes, near, even, odd, tiles_out, sparse_out, points, values):
    fill_table(points, (near, even, odd), 0, FEAT, f32)
    fill_table(values, (near, even, odd), FEAT, FEAT + PROBES, bf16)
    scale = 1.0 / (support_radius * support_radius)
    for index in range(HALF):
        block = base + index
        own = augmented(points[4 * CAP + block], scale, True).astype(f32).T.astype(bf16)
        other = augmented(partners(points, codes, block), scale, False)
        square = jnp.maximum(jnp.dot(own, other, preferred_element_type=f32), 0.0)
        ratio = jnp.sqrt(square)
        remain = jnp.maximum(1.0 - ratio, 0.0)
        second = remain * remain
        fourth = second * second
        tile = (fourth * second * remain * (7.0 * ratio + 1.0)).astype(bf16)
        tiles_out[index] = tile
        sparse_out[:, index * BLOCK : (index + 1) * BLOCK] = nt_dot(
            partners(values, codes, block), tile
        )


def make_tiles(half, codes, near, even, odd):
    return call(
        functools.partial(tiles_kernel, half * HALF),
        "tiles",
        (shape(HALF, BLOCK, PTS, dtype=bf16), shape(PROBES, HALF * BLOCK)),
        [SMEM, VMEM, VMEM, VMEM],
        (codes, near, even, odd),
        scratch=[
            pltpu.VMEM((EMPTY + 1, FEAT, BLOCK), f32),
            pltpu.VMEM((EMPTY + 1, PROBES, BLOCK), bf16),
        ],
        moved=8 << 20,
    )


def steps_of(row):
    rz_now = as_column(row, 0)
    alpha = rz_now / as_column(row, 16)
    return alpha, alpha * alpha * as_column(row, 32) / rz_now - 1.0


def sparse_kernel(
    codes, near, even, odd, tiles_low, tiles_high, search, residual, precond,
    sparse_out, sums_out, values,
):
    fill_table(values, (near, even, odd), 0, PROBES, bf16)
    for block in range(CAP):
        sparse_out[:, block * BLOCK : (block + 1) * BLOCK] = nt_dot(
            partners(values, codes, block), (tiles_low, tiles_high)[block // HALF][block % HALF]
        )
    field = search[...]
    left = residual[...]
    curve = jnp.sum(field * (field + sparse_out[...]), axis=1, keepdims=True)
    norm = jnp.sum(left * (precond[...] * left), axis=1, keepdims=True)
    lane = lax.broadcasted_iota(jnp.int32, (PROBES, 128), 1)
    sums_out[...] = jnp.where(lane == 0, curve, jnp.where(lane == 1, norm, 0.0))


def apply_tiles(codes, nears, tiles, search, residual, precond):
    return call(
        sparse_kernel,
        "sparse",
        (FIELD, shape(PROBES, 128)),
        [SMEM] + [VMEM] * 8,
        (codes, *nears, *tiles, search, residual, precond),
        scratch=[pltpu.VMEM((EMPTY + 1, PROBES, BLOCK), bf16)],
        moved=6 << 20,
    )


def stack_kernel(own, even, odd, out):
    out[0] = own[...]
    out[1] = even[...]
    out[2] = odd[...]


def surround(value, even, odd):
    column = call(
        stack_kernel,
        "stack",
        shape(3, *value.shape, dtype=value.dtype),
        [VMEM] * 3,
        (value, even, odd),
    )
    return column, even_pairs(column, GY), odd_pairs(column, GY)


def expand(weights, rows):
    total = jnp.zeros((PROBES, PTS), f32)
    for step in range(CHUNKS):
        part = jnp.concatenate([weights[4 * step + i, :PROBES] for i in range(4)], axis=1)
        total = total + nt_dot(part, rows[step])
    return total


def image_kernel(
    weights, rows, counts, halo, sparse_low, sparse_high, precond, probes, image_out, sums_out
):
    search = halo[FEAT:]
    live = live_lanes(counts[0, 0])
    sparse = jnp.concatenate([sparse_low[...], sparse_high[...]], axis=1)
    image = live * (search + sparse + expand(weights, rows))
    image_out[...] = image
    norm = jnp.sum(search * (probes[...] * live), axis=1, keepdims=True)
    curve = jnp.sum(search * image, axis=1, keepdims=True)
    square = jnp.sum(precond[...] * image * image, axis=1, keepdims=True)
    row = as_lanes(norm, 0) + as_lanes(curve, 16) + as_lanes(square, 32)
    sums_out[...] = jnp.broadcast_to(row[None], sums_out.shape)


def make_image(weights, rows, counts, halo, sparse, precond, probes):
    return call(
        image_kernel,
        "image",
        (FIELD, shape(256, 1, 128)),
        [VMEM, VMEM, SMEM] + [VMEM] * 5,
        (weights, rows, counts, halo, *sparse, precond, probes),
        params=MIDDLE,
        moved=16 << 20,
    )


def update_kernel(
    rows, halo, probes, precond, counts, image,
    residual_out, search_out, packed_out, rounded_out, solution_out,
):
    alpha, beta = steps_of(jnp.sum(rows[...], axis=0))
    search = halo[FEAT:]
    solution_out[...] = alpha * search
    residual = probes[...] * live_lanes(counts[0, 0]) - alpha * image[...]
    residual_out[...] = residual
    following = precond[...] * residual + beta * search
    search_out[...] = following
    rounded = following.astype(bf16)
    rounded_out[...] = rounded
    packed_out[:PROBES] = rounded
    packed_out[PROBES:] = (following - rounded.astype(f32)).astype(bf16)


def update(rows, halo, probes, precond, counts, image):
    return call(
        update_kernel,
        "update",
        (
            FIELD,
            FIELD,
            shape(2 * PROBES, PTS, dtype=bf16),
            shape(PROBES, PTS, dtype=bf16),
            FIELD,
        ),
        [VMEM, VMEM, VMEM, VMEM, SMEM, VMEM],
        (rows, halo, probes, precond, counts, image),
    )


def sum_share_kernel(*refs):
    parts, out = refs[0], refs[-1]
    total = jnp.sum(parts[...], axis=0)
    if len(refs) == 3:
        total = jnp.concatenate([total, refs[1][...]], axis=0)
    out[...] = jnp.broadcast_to(total[None], out.shape)


def sum_share(parts, *sums):
    height = parts.shape[1] + sum(value.shape[0] for value in sums)
    return call(
        sum_share_kernel,
        "sum_share",
        shape(8, height, SHARE),
        [VMEM] * (1 + len(sums)),
        (parts, *sums),
    )


def sum_depth_kernel(parts, *outs):
    total = jnp.sum(parts[...], axis=0)
    for index, out in enumerate(outs):
        out[...] = total[index * PROBES : (index + 1) * PROBES]


def sum_depth(parts):
    count = parts.shape[1] // PROBES
    return call(
        sum_depth_kernel, "sum_depth", (shape(PROBES, SHARE),) * count, [VMEM], (parts,)
    )


def six_products(value, factors, dot):
    first, second, third = split3(value)
    stacked = jnp.concatenate([third, second, first], axis=0).astype(bf16)
    by_first = dot(stacked, factors[0][...])
    by_second = dot(stacked[PROBES:], factors[1][...])
    by_third = dot(stacked[2 * PROBES :], factors[2][...])
    small = by_first[:PROBES] + by_second[:PROBES] + by_third
    middle = by_first[PROBES : 2 * PROBES] + by_second[PROBES:]
    return by_first[2 * PROBES :] + (middle + small)


def nn_dot(left, right):
    return jnp.dot(left, right, preferred_element_type=f32)


def coeffs_kernel(*refs):
    shares, factors, out = refs[:4], refs[4:7], refs[-1]
    value = jnp.concatenate([ref[...] for ref in shares], axis=1)
    terms = six_products(value, factors, nn_dot)
    if len(refs) == 9:
        terms = jnp.concatenate([terms, refs[7][...]], axis=1)
    out[...] = jnp.broadcast_to(terms[None], out.shape)


def coeff_terms(shares, factors, *sums):
    width = QUARTER + SHARE * len(sums)
    return call(
        coeffs_kernel,
        "coeffs",
        shape(8, PROBES, width),
        [VMEM] * (7 + len(sums)),
        (*shares, *factors, *sums),
    )


def weights_kernel(parts, first, second, third, *outs):
    total = jnp.sum(parts[...], axis=0)
    terms = six_products(total[:, :QUARTER], (first, second, third), nt_dot)
    for index, out in enumerate(outs):
        out[:, :SHARE] = terms[:, index * SHARE : (index + 1) * SHARE]
        if out.shape[1] > SHARE:
            out[:, SHARE:] = total[:, QUARTER:]


def weight_terms(parts, factors):
    width = SHARE + parts.shape[2] - QUARTER
    return call(
        weights_kernel,
        "weights",
        (shape(PROBES, width),) * 4,
        [VMEM] * 4,
        (parts, *factors),
    )


def gather_kernel(own, first, second, third, out):
    total = own[...] + first[...] + second[...] + third[...]
    out[...] = jnp.broadcast_to(total.astype(bf16)[None], out.shape)


def gather_weights(terms):
    return call(
        gather_kernel, "gather", shape(32, PROBES, SHARE, dtype=bf16), [VMEM] * 4, tuple(terms)
    )


def gather_last_kernel(own, first, second, third, rounded, rest, out, sums_out):
    total = own[...] + first[...] + second[...] + third[...]
    weights = total[:, :SHARE].astype(bf16)
    sums_out[...] = total[:, SHARE:]
    unrounded = rounded[...] + rest[...]
    dot = jnp.sum(weights.astype(f32) * unrounded, axis=1, keepdims=True)
    lane = lax.broadcasted_iota(jnp.int32, (PROBES, SHARE), 1)
    row = jnp.zeros((PROBES, SHARE), f32)
    for index, part in enumerate(split3(dot)):
        row = jnp.where(lane == index, part, row)
    both = jnp.concatenate([weights, row.astype(bf16)], axis=0)
    out[...] = jnp.broadcast_to(both[None], out.shape)


def gather_last(terms, rounded, rest):
    return call(
        gather_last_kernel,
        "gather_last",
        (shape(32, 2 * PROBES, SHARE, dtype=bf16), shape(PROBES, 128)),
        [VMEM] * 6,
        (*terms, rounded, rest),
    )


def finish_kernel(
    weights, rows, counts, search, sparse, residual, solution, sums, solution_out, residual_out
):
    field = search[...]
    image = live_lanes(counts[0, 0]) * (field + sparse[...] + expand(weights, rows))
    dots = jnp.sum(weights[:, PROBES:].astype(f32), axis=0)
    dot = jnp.sum(dots, axis=1, keepdims=True)
    totals = sums[...]
    alpha = totals[:, 1:2] / (totals[:, 0:1] + dot)
    solution_out[...] = solution[...] + alpha * field
    residual_out[...] = residual[...] - alpha * image


def finish(weights, rows, counts, search, sparse, residual, solution, sums):
    return call(
        finish_kernel,
        "finish",
        (FIELD, FIELD),
        [VMEM, VMEM, SMEM] + [VMEM] * 5,
        (weights, rows, counts, search, sparse, residual, solution, sums),
        params=MIDDLE,
        moved=16 << 20,
    )


def on_device(coords, probes, precond, counts, neighbours, inducing, factor):
    points = coords[0, 0]
    given = probes[0, 0]
    scaling = precond[0]
    codes = neighbours[0, 0]

    centre_parts, halo = prepare(points, given, scaling, counts, inducing[0])

    even, odd = even_pairs(halo, GX), odd_pairs(halo, GX)
    centres = exchange(centre_parts, ALL).reshape(256, 128)
    columns = lax.dynamic_slice_in_dim(factor, quad_index() * QUARTER, QUARTER, 1)
    centres = after(centres, columns)
    halos = surround(after(halo, centres), even, odd)
    factors = split_factor(after(columns, halos[0]))
    rows, parts = make_rows(halo, after(centres, halos[0], *factors))
    parts = after(parts, *halos)

    def depth_of(got, *sums):
        return sum_depth(exchange(sum_share(got, *sums), "z"))

    def coeffs_of(depth, beside):
        own = depth[0]
        shares = [own] + [quad_partner(own, step) for step in (1, 2, 3)]
        shares[0] = after(own, *beside)
        return exchange(coeff_terms(shares, factors, *depth[2:]), GY)

    def terms_of(coeffs):
        terms = weight_terms(coeffs, factors)
        return [terms[0]] + [quad_partner(terms[step], step) for step in (1, 2, 3)]

    depth = depth_of(exchange(parts, PLANE))
    low = make_tiles(0, codes, after(halos[0], depth[0]), *halos[1:])
    coeffs = coeffs_of(depth, low)
    terms = weight_terms(coeffs, factors)
    high = make_tiles(1, codes, after(halos[0], terms[0]), *halos[1:])
    terms = [after(terms[0], *high)] + [quad_partner(terms[step], step) for step in (1, 2, 3)]
    weights = exchange(gather_weights(terms), PLANE)
    tiles, sparse = zip(low, high)
    image, row = make_image(weights, rows, counts, halo, sparse, scaling, given)
    row = exchange(row, ALL)
    residual, search, packed, rounded, solution = update(
        row, halo, given, scaling, counts, image
    )

    even, odd = even_pairs(rounded, GX), odd_pairs(rounded, GX)
    parts = project(packed, rows)

    nears = surround(after(rounded, parts), even, odd)
    got = exchange(after(parts, nears[0]), PLANE)
    sparse, sums = apply_tiles(
        codes, (after(nears[0], got),) + nears[1:], tiles, search, residual, scaling
    )
    depth = depth_of(got, sums)
    weights, totals = gather_last(terms_of(coeffs_of(depth, ())), depth[0], depth[1])
    weights = exchange(weights, PLANE)
    solution, residual = finish(
        weights, rows, counts, search, sparse, residual, solution, totals
    )
    return (solution[None, None], residual[None, None])


def solution(mesh):
    fine = Mesh(mesh.devices.reshape(8, 2, 2, 2, 4), ALL)
    placed = (
        P(GX, GY, None, None),
        P(GX, GY, None, None),
        P(GX, GY, None),
        P(GX, GY),
        P(GX, GY, None, None),
        P(GX, GY, None),
        P(GY, None),
    )
    return jax.shard_map(
        on_device,
        mesh=fine,
        in_specs=placed,
        out_specs=(P(GX, GY, None, None), P(GX, GY, None, None)),
        check_vma=False,
    )
```

```python
import functools

import jax
import jax.numpy as jnp
from jax import lax
from jax.experimental import pallas as pl
from jax.experimental.pallas import tpu as pltpu
from jax.sharding import Mesh, PartitionSpec as P

FEAT = 8
BLOCK = 128
PROBES = 16
PTS = 1024
SHARE = 128
CHUNK = 512
CHUNKS = 8
CAP = 8
EMPTY = 72
HALF = 4
QUARTER = 1024

support_radius = 0.32
width_sq = 0.045
LOG2E = 1.4426950408889634

ALL = ("z", "yl", "c", "yh", "x")
PLANE = ("yh", "x", "yl", "c")
GX = ("z", "yl", "c")
GY = ("yh", "x")
f32 = jnp.float32
bf16 = jnp.bfloat16

VMEM = pl.BlockSpec(memory_space=pltpu.VMEM)
SMEM = pl.BlockSpec(memory_space=pltpu.SMEM)
SMALL = pltpu.CompilerParams(vmem_limit_bytes=16 * 1024 * 1024)
MIDDLE = pltpu.CompilerParams(vmem_limit_bytes=24 * 1024 * 1024)
LARGE = pltpu.CompilerParams(vmem_limit_bytes=57 * 1024 * 1024)


def exchange(parts, axes):
    return lax.all_to_all(parts, axes, 0, 0, tiled=True)


def quad_index():
    return lax.axis_index("yl") * 2 + lax.axis_index("c")


def quad_partner(value, step):
    pairs = [(i, i ^ step) for i in range(4)]
    return lax.ppermute(value, ("yl", "c"), pairs)


def even_pairs(value, axes):
    return lax.ppermute(value, axes, [(i, i ^ 1) for i in range(lax.axis_size(axes))])


def odd_pairs(value, axes):
    count = lax.axis_size(axes)
    pairs = [(i, i + 1) for i in range(1, count - 1, 2)]
    return lax.ppermute(value, axes, pairs + [(j, i) for i, j in pairs])


def after(value, *others):
    return lax.optimization_barrier((value,) + others)[0]


def split3(value):
    first = value.astype(bf16).astype(f32)
    rest = value - first
    second = rest.astype(bf16).astype(f32)
    return first, second, (rest - second).astype(bf16).astype(f32)


def augmented(points, scale, left):
    centred = points - 0.5
    norm = scale * jnp.sum(centred * centred, axis=0, keepdims=True)
    norms = [jnp.broadcast_to(part, points.shape) for part in split3(norm)]
    row = lax.broadcasted_iota(jnp.int32, points.shape, 0)
    if left:
        one, two, three = split3(centred)
        order = [one, one, two, one, two, three]
        base = 0
    else:
        one, two, three = split3((-2.0 * scale) * centred)
        order = [one, two, one, three, two, one]
        base = 3
    extra = jnp.where(row < 6, 1.0, 0.0)
    for index, part in enumerate(norms):
        extra = jnp.where(row == base + index, part, extra)
    return jnp.concatenate(order + [extra, jnp.zeros_like(extra)], axis=0).astype(bf16)


def live_lanes(count):
    lane = lax.broadcasted_iota(jnp.int32, (1, PTS), 1)
    return jnp.where(lane < count, 1.0, 0.0)


def nt_dot(left, right):
    return lax.dot_general(left, right, (((1,), (1,)), ((), ())), preferred_element_type=f32)


def call(kernel, name, out_shape, in_specs, args, scratch=(), grid=None, out_specs=None, params=SMALL, flops=0, moved=0):
    if out_specs is None:
        out_specs = jax.tree.map(lambda _: VMEM, out_shape)
    options = {} if grid is None else {"grid": grid}
    return pl.pallas_call(
        kernel,
        out_shape=out_shape,
        in_specs=in_specs,
        out_specs=out_specs,
        scratch_shapes=list(scratch),
        compiler_params=params,
        cost_estimate=pl.CostEstimate(flops=flops, bytes_accessed=moved, transcendentals=0),
        name=name,
        **options,
    )(*args)


def shape(*dims, dtype=f32):
    return jax.ShapeDtypeStruct(dims, dtype)


FIELD = shape(PROBES, PTS)


def prepare_kernel(coords, probes, precond, counts, inducing, centre_out, halo_out):
    points = coords[...]
    lane = lax.broadcasted_iota(jnp.int32, (FEAT, PTS), 1)
    short = lax.broadcasted_iota(jnp.int32, (FEAT, 128), 1)
    centre = jnp.zeros((FEAT, 128), f32)
    for index in range(16):
        picked = jnp.sum(
            jnp.where(lane == inducing[0, index], points, 0.0), axis=1, keepdims=True
        )
        centre = jnp.where(short == index, picked, centre)
    row = centre[:1]
    for feature in range(1, FEAT):
        row = row + pltpu.roll(centre, 128 - 16 * feature, 1)[feature : feature + 1]
    centre_out[...] = jnp.broadcast_to(row[None], centre_out.shape)
    halo_out[:FEAT] = points
    halo_out[FEAT:] = precond[...] * (probes[...] * live_lanes(counts[0, 0]))


def prepare(coords, probes, precond, counts, inducing):
    return call(
        prepare_kernel,
        "prepare",
        (shape(256, 1, 128), shape(FEAT + PROBES, PTS)),
        [VMEM, VMEM, VMEM, SMEM, SMEM],
        (coords, probes, precond, counts, inducing),
        params=LARGE,
    )


def factor_kernel(columns, first_out, second_out, third_out):
    quad = quad_index()
    for index in range(4):
        start = pl.multiple_of((quad ^ index) * SHARE, SHARE)
        parts = split3(columns[pl.ds(start, SHARE), :])
        for out, part in zip((first_out, second_out, third_out), parts):
            out[index * SHARE : (index + 1) * SHARE] = part.astype(bf16)


def split_factor(columns):
    return call(
        factor_kernel,
        "factor",
        (shape(4 * SHARE, QUARTER, dtype=bf16),) * 3,
        [VMEM],
        (columns,),
        moved=8 << 20,
    )


def centre_columns(parts):
    group = lax.broadcasted_iota(jnp.int32, (8, 128), 1) // 16
    tiles = []
    for index in range(4):
        tile = pltpu.roll(parts[8 * index : 8 * index + 8], 0, 1, stride=16, stride_axis=0)
        for bit in (1, 2, 4):
            tile = jnp.where(group & bit != 0, pltpu.roll(tile, 8 - bit, 0), tile)
        tiles.append(pltpu.roll(tile, 0, 1, stride=16, stride_axis=0))
    return jnp.concatenate(tiles, axis=1)


def rows_kernel(halo, centres, rows_out, sums_out, left, packed):
    left[...] = augmented(halo[:FEAT], -LOG2E / width_sq, True).astype(f32).T.astype(bf16)
    packed[...] = halo[FEAT:].astype(bf16)

    def chunk(step, carry):
        cells = centres[pl.ds(pl.multiple_of(step * 32, 32), 32), :]
        right = augmented(centre_columns(cells), -LOG2E / width_sq, False)
        power = jnp.dot(left[...], right, preferred_element_type=f32)
        rows = jnp.exp2(jnp.minimum(power, 0.0)).astype(bf16)
        rows_out[step] = rows
        sums = jnp.dot(packed[...], rows, preferred_element_type=f32)
        for part in range(4):
            sums_out[4 * step + part] = sums[:, part * SHARE : (part + 1) * SHARE]
        return carry

    lax.fori_loop(0, CHUNKS, chunk, 0, unroll=2)


def make_rows(halo, centres):
    return call(
        rows_kernel,
        "rows",
        (shape(CHUNKS, PTS, CHUNK, dtype=bf16), shape(32, PROBES, SHARE)),
        [VMEM, VMEM],
        (halo, centres),
        scratch=[pltpu.VMEM((PTS, 64), bf16), pltpu.VMEM((PROBES, PTS), bf16)],
        params=MIDDLE,
        moved=16 << 20,
    )


def project_kernel(packed, rows, sums_out):
    for step in range(CHUNKS):
        sums = jnp.dot(packed[...], rows[step], preferred_element_type=f32)
        for part in range(4):
            here = sums[:, part * SHARE : (part + 1) * SHARE]
            sums_out[4 * step + part, :PROBES] = here[:PROBES] + here[PROBES : 2 * PROBES]
            sums_out[4 * step + part, PROBES:] = here[2 * PROBES :]


def project(packed, rows):
    return call(
        project_kernel,
        "project",
        shape(32, 2 * PROBES, SHARE),
        [VMEM, VMEM],
        (packed, rows),
        params=MIDDLE,
        moved=16 << 20,
    )


def fill_table(table, sources, first, last, dtype):
    side_x, side_y = lax.axis_index("c"), lax.axis_index("x") & 1
    places_x = (1, 2 - 2 * side_x, 2 * side_x)
    places_y = (1, 2 - 2 * side_y, 2 * side_y)
    for place_y, source in zip(places_y, sources):
        for index, place_x in enumerate(places_x):
            start = (place_x * 3 + place_y) * CAP
            values = source[index, first:last].astype(dtype)
            for block in range(CAP):
                table[start + block] = values[:, block * BLOCK : (block + 1) * BLOCK]
    table[EMPTY] = jnp.zeros(table.shape[1:], dtype)


def partners(table, codes, block):
    return jnp.concatenate([table[codes[block, entry]] for entry in range(CAP)], axis=1)


def tiles_kernel(base, codes, near, even, odd, tiles_out, sparse_out, points, values):
    fill_table(points, (near, even, odd), 0, FEAT, f32)
    fill_table(values, (near, even, odd), FEAT, FEAT + PROBES, bf16)
    scale = 1.0 / (support_radius * support_radius)
    for index in range(HALF):
        block = base + index
        own = augmented(points[4 * CAP + block], scale, True).astype(f32).T.astype(bf16)
        other = augmented(partners(points, codes, block), scale, False)
        square = jnp.maximum(jnp.dot(own, other, preferred_element_type=f32), 0.0)
        ratio = jnp.sqrt(square)
        remain = jnp.maximum(1.0 - ratio, 0.0)
        second = remain * remain
        fourth = second * second
        tile = (fourth * second * remain * (7.0 * ratio + 1.0)).astype(bf16)
        tiles_out[index] = tile
        sparse_out[:, index * BLOCK : (index + 1) * BLOCK] = nt_dot(
            partners(values, codes, block), tile
        )


def make_tiles(half, codes, near, even, odd):
    return call(
        functools.partial(tiles_kernel, half * HALF),
        "tiles",
        (shape(HALF, BLOCK, PTS, dtype=bf16), shape(PROBES, HALF * BLOCK)),
        [SMEM, VMEM, VMEM, VMEM],
        (codes, near, even, odd),
        scratch=[
            pltpu.VMEM((EMPTY + 1, FEAT, BLOCK), f32),
            pltpu.VMEM((EMPTY + 1, PROBES, BLOCK), bf16),
        ],
        moved=8 << 20,
    )


def steps_of(sums):
    alpha = sums[:, 0:1] / sums[:, 1:2]
    return alpha, alpha * alpha * sums[:, 2:3] / sums[:, 0:1] - 1.0


def sparse_kernel(
    codes, near, even, odd, tiles_low, tiles_high, halo, image, scaled, sparse_low, sparse_high,
    precond, sparse_out, sums_out, values,
):
    fill_table(values, (near, even, odd), 0, 2 * PROBES, bf16)
    for block in range(CAP):
        both = nt_dot(
            partners(values, codes, block), (tiles_low, tiles_high)[block // HALF][block % HALF]
        )
        sparse_out[:, block * BLOCK : (block + 1) * BLOCK] = both[:PROBES] + both[PROBES:]
    old = halo[FEAT:]
    new = scaled[...]
    by_old = old + jnp.concatenate([sparse_low[...], sparse_high[...]], axis=1)
    by_new = new + sparse_out[...]
    products = (
        old * (old / precond[...]),
        old * image[...],
        new * image[...],
        old * by_old,
        old * by_new + new * by_old,
        new * by_new,
    )
    lane = lax.broadcasted_iota(jnp.int32, (PROBES, 128), 1)
    row = jnp.zeros((PROBES, 128), f32)
    for index, product in enumerate(products):
        row = jnp.where(lane == index, jnp.sum(product, axis=1, keepdims=True), row)
    sums_out[...] = row


def apply_tiles(codes, nears, tiles, halo, image, scaled, sparse, precond):
    return call(
        sparse_kernel,
        "sparse",
        (FIELD, shape(PROBES, 128)),
        [SMEM] + [VMEM] * 11,
        (codes, *nears, *tiles, halo, image, scaled, *sparse, precond),
        scratch=[pltpu.VMEM((EMPTY + 1, 2 * PROBES, BLOCK), bf16)],
        moved=6 << 20,
    )


def stack_kernel(own, even, odd, out):
    out[0] = own[...]
    out[1] = even[...]
    out[2] = odd[...]


def surround(value, even, odd):
    column = call(
        stack_kernel,
        "stack",
        shape(3, *value.shape, dtype=value.dtype),
        [VMEM] * 3,
        (value, even, odd),
    )
    return column, even_pairs(column, GY), odd_pairs(column, GY)


def expand(weights, rows):
    total = jnp.zeros((PROBES, PTS), f32)
    for step in range(CHUNKS):
        part = jnp.concatenate([weights[4 * step + i, :PROBES] for i in range(4)], axis=1)
        total = total + nt_dot(part, rows[step])
    return total


def image_kernel(
    weights, rows, counts, halo, sparse_low, sparse_high, precond,
    image_out, scaled_out, halo_out, packed_out,
):
    search = halo[FEAT:]
    sparse = jnp.concatenate([sparse_low[...], sparse_high[...]], axis=1)
    image = live_lanes(counts[0, 0]) * (search + sparse + expand(weights, rows))
    image_out[...] = image
    scaled = precond[...] * image
    scaled_out[...] = scaled
    first = scaled.astype(bf16)
    second = (scaled - first.astype(f32)).astype(bf16)
    rest = (search - search.astype(bf16).astype(f32)).astype(bf16)
    halo_out[:PROBES] = first
    halo_out[PROBES:] = second
    packed_out[:PROBES] = first
    packed_out[PROBES : 2 * PROBES] = second
    packed_out[2 * PROBES :] = rest


def make_image(weights, rows, counts, halo, sparse, precond):
    return call(
        image_kernel,
        "image",
        (
            FIELD,
            FIELD,
            shape(2 * PROBES, PTS, dtype=bf16),
            shape(3 * PROBES, PTS, dtype=bf16),
        ),
        [VMEM, VMEM, SMEM] + [VMEM] * 4,
        (weights, rows, counts, halo, *sparse, precond),
        params=MIDDLE,
        moved=16 << 20,
    )


def sum_share_kernel(*refs):
    parts, out = refs[0], refs[-1]
    total = jnp.sum(parts[...], axis=0)
    if len(refs) == 3:
        total = jnp.concatenate([total, refs[1][...]], axis=0)
    out[...] = jnp.broadcast_to(total[None], out.shape)


def sum_share(parts, *sums):
    height = parts.shape[1] + sum(value.shape[0] for value in sums)
    return call(
        sum_share_kernel,
        "sum_share",
        shape(8, height, SHARE),
        [VMEM] * (1 + len(sums)),
        (parts, *sums),
    )


def sum_depth_kernel(parts, *outs):
    total = jnp.sum(parts[...], axis=0)
    for index, out in enumerate(outs):
        out[...] = total[index * PROBES : (index + 1) * PROBES]


def sum_depth(parts):
    count = parts.shape[1] // PROBES
    return call(
        sum_depth_kernel, "sum_depth", (shape(PROBES, SHARE),) * count, [VMEM], (parts,)
    )


def six_products(value, factors, dot):
    first, second, third = split3(value)
    stacked = jnp.concatenate([third, second, first], axis=0).astype(bf16)
    by_first = dot(stacked, factors[0][...])
    by_second = dot(stacked[PROBES:], factors[1][...])
    by_third = dot(stacked[2 * PROBES :], factors[2][...])
    small = by_first[:PROBES] + by_second[:PROBES] + by_third
    middle = by_first[PROBES : 2 * PROBES] + by_second[PROBES:]
    return by_first[2 * PROBES :] + (middle + small)


def nn_dot(left, right):
    return jnp.dot(left, right, preferred_element_type=f32)


def coeffs_kernel(*refs):
    shares, factors, out = refs[:4], refs[4:7], refs[-1]
    value = jnp.concatenate([ref[...] for ref in shares], axis=1)
    terms = six_products(value, factors, nn_dot)
    if len(refs) == 9:
        terms = jnp.concatenate([terms, refs[7][...]], axis=1)
    out[...] = jnp.broadcast_to(terms[None], out.shape)


def coeff_terms(shares, factors, *sums):
    width = QUARTER + SHARE * len(sums)
    return call(
        coeffs_kernel,
        "coeffs",
        shape(8, PROBES, width),
        [VMEM] * (7 + len(sums)),
        (*shares, *factors, *sums),
    )


def weights_kernel(parts, first, second, third, *outs):
    total = jnp.sum(parts[...], axis=0)
    terms = six_products(total[:, :QUARTER], (first, second, third), nt_dot)
    for index, out in enumerate(outs):
        out[:, :SHARE] = terms[:, index * SHARE : (index + 1) * SHARE]
        if out.shape[1] > SHARE:
            out[:, SHARE:] = total[:, QUARTER:]


def weight_terms(parts, factors):
    width = SHARE + parts.shape[2] - QUARTER
    return call(
        weights_kernel,
        "weights",
        (shape(PROBES, width),) * 4,
        [VMEM] * 4,
        (parts, *factors),
    )


def gather_kernel(own, first, second, third, out, total_out):
    total = own[...] + first[...] + second[...] + third[...]
    total_out[...] = total
    out[...] = jnp.broadcast_to(total.astype(bf16)[None], out.shape)


def gather_weights(terms):
    return call(
        gather_kernel,
        "gather",
        (shape(32, PROBES, SHARE, dtype=bf16), shape(PROBES, SHARE)),
        [VMEM] * 4,
        tuple(terms),
    )


def gather_last_kernel(
    own, first, second, third, new_share, rest_share, old_share, old_weights, out, sums_out
):
    total = own[...] + first[...] + second[...] + third[...]
    sums = total[:, SHARE:]
    sums_out[...] = sums
    alpha, beta = steps_of(sums)
    weights = ((1.0 + beta) * old_weights[...] - alpha * total[:, :SHARE]).astype(bf16)
    share = (1.0 + beta) * (old_share[...] + rest_share[...]) - alpha * new_share[...]
    dot = jnp.sum(weights.astype(f32) * share, axis=1, keepdims=True)
    lane = lax.broadcasted_iota(jnp.int32, (PROBES, SHARE), 1)
    row = jnp.zeros((PROBES, SHARE), f32)
    for index, part in enumerate(split3(dot)):
        row = jnp.where(lane == index, part, row)
    both = jnp.concatenate([weights, row.astype(bf16)], axis=0)
    out[...] = jnp.broadcast_to(both[None], out.shape)


def gather_last(terms, new_share, rest_share, old_share, old_weights):
    return call(
        gather_last_kernel,
        "gather_last",
        (shape(32, 2 * PROBES, SHARE, dtype=bf16), shape(PROBES, 128)),
        [VMEM] * 8,
        (*terms, new_share, rest_share, old_share, old_weights),
    )


def finish_kernel(
    weights, rows, counts, halo, probes, image, scaled, sparse_low, sparse_high, sparse, sums,
    solution_out, residual_out,
):
    totals = sums[...]
    alpha, beta = steps_of(totals)
    scale = 1.0 + beta
    old = halo[FEAT:]
    field = scale * old - alpha * scaled[...]
    by_old = jnp.concatenate([sparse_low[...], sparse_high[...]], axis=1)
    live = live_lanes(counts[0, 0])
    following = live * (
        field + (scale * by_old - alpha * sparse[...]) + expand(weights, rows)
    )
    dots = jnp.sum(weights[:, PROBES:].astype(f32), axis=0)
    curve = jnp.sum(dots, axis=1, keepdims=True) + (
        scale * scale * totals[:, 3:4]
        - alpha * scale * totals[:, 4:5]
        + alpha * alpha * totals[:, 5:6]
    )
    step = beta * totals[:, 0:1] / curve
    solution_out[...] = alpha * old + step * field
    residual_out[...] = (probes[...] * live - alpha * image[...]) - step * following


def finish(weights, rows, counts, halo, probes, image, scaled, old_sparse, sparse, sums):
    return call(
        finish_kernel,
        "finish",
        (FIELD, FIELD),
        [VMEM, VMEM, SMEM] + [VMEM] * 8,
        (weights, rows, counts, halo, probes, image, scaled, *old_sparse, sparse, sums),
        params=MIDDLE,
        moved=16 << 20,
    )


def on_device(coords, probes, precond, counts, neighbours, inducing, factor):
    points = coords[0, 0]
    given = probes[0, 0]
    scaling = precond[0]
    codes = neighbours[0, 0]

    centre_parts, halo = prepare(points, given, scaling, counts, inducing[0])

    even, odd = even_pairs(halo, GX), odd_pairs(halo, GX)
    centres = exchange(centre_parts, ALL).reshape(256, 128)
    columns = lax.dynamic_slice_in_dim(factor, quad_index() * QUARTER, QUARTER, 1)
    centres = after(centres, columns)
    halos = surround(after(halo, centres), even, odd)
    factors = split_factor(after(columns, halos[0]))
    rows, parts = make_rows(halo, after(centres, halos[0], *factors))
    parts = after(parts, *halos)

    def depth_of(got, *sums):
        return sum_depth(exchange(sum_share(got, *sums), "z"))

    def coeffs_of(depth, beside):
        own = depth[0]
        shares = [own] + [quad_partner(own, step) for step in (1, 2, 3)]
        shares[0] = after(own, *beside)
        return exchange(coeff_terms(shares, factors, *depth[2:]), GY)

    def terms_of(coeffs):
        terms = weight_terms(coeffs, factors)
        return [terms[0]] + [quad_partner(terms[step], step) for step in (1, 2, 3)]

    depth = depth_of(exchange(parts, PLANE))
    low = make_tiles(0, codes, after(halos[0], depth[0]), *halos[1:])
    coeffs = coeffs_of(depth, low)
    terms = weight_terms(coeffs, factors)
    high = make_tiles(1, codes, after(halos[0], terms[0]), *halos[1:])
    terms = [after(terms[0], *high)] + [quad_partner(terms[step], step) for step in (1, 2, 3)]
    old_share = depth[0]
    weights, old_weights = gather_weights(terms)
    weights = exchange(weights, PLANE)
    tiles, old_sparse = zip(low, high)
    image, scaled, sent, packed = make_image(weights, rows, counts, halo, old_sparse, scaling)
    even, odd = even_pairs(sent, GX), odd_pairs(sent, GX)
    parts = project(packed, rows)

    nears = surround(after(sent, parts), even, odd)
    got = exchange(after(parts, nears[0]), PLANE)
    sparse, sums = apply_tiles(
        codes, (after(nears[0], got),) + nears[1:], tiles, halo, image, scaled, old_sparse, scaling
    )
    depth = depth_of(got, sums)
    weights, totals = gather_last(
        terms_of(coeffs_of(depth, ())), depth[0], depth[1], old_share, old_weights
    )
    weights = exchange(weights, PLANE)
    solution, residual = finish(
        weights, rows, counts, halo, given, image, scaled, old_sparse, sparse, totals
    )
    return (solution[None, None], residual[None, None])


def solution(mesh):
    fine = Mesh(mesh.devices.reshape(8, 2, 2, 2, 4), ALL)
    placed = (
        P(GX, GY, None, None),
        P(GX, GY, None, None),
        P(GX, GY, None),
        P(GX, GY),
        P(GX, GY, None, None),
        P(GX, GY, None),
        P(GY, None),
    )
    return jax.shard_map(
        on_device,
        mesh=fine,
        in_specs=placed,
        out_specs=(P(GX, GY, None, None), P(GX, GY, None, None)),
        check_vma=False,
    )
```

```python
import functools

import jax
import jax.numpy as jnp
from jax import lax
from jax.experimental import pallas as pl
from jax.experimental.pallas import tpu as pltpu
from jax.sharding import Mesh, PartitionSpec as P

FEAT = 8
BLOCK = 128
PROBES = 16
PTS = 1024
SHARE = 128
CHUNK = 512
CHUNKS = 8
CAP = 8
EMPTY = 72
HALF = 4
QUARTER = 1024

support_radius = 0.32
width_sq = 0.045
LOG2E = 1.4426950408889634

ALL = ("z", "yl", "c", "yh", "x")
PLANE = ("yh", "x", "yl", "c")
GX = ("z", "yl", "c")
GY = ("yh", "x")
f32 = jnp.float32
bf16 = jnp.bfloat16

VMEM = pl.BlockSpec(memory_space=pltpu.VMEM)
SMEM = pl.BlockSpec(memory_space=pltpu.SMEM)
SMALL = pltpu.CompilerParams(vmem_limit_bytes=16 * 1024 * 1024)
MIDDLE = pltpu.CompilerParams(vmem_limit_bytes=24 * 1024 * 1024)
LARGE = pltpu.CompilerParams(vmem_limit_bytes=57 * 1024 * 1024)


def exchange(parts, axes):
    return lax.all_to_all(parts, axes, 0, 0, tiled=True)


def quad_index():
    return lax.axis_index("yl") * 2 + lax.axis_index("c")


def quad_partner(value, step):
    pairs = [(i, i ^ step) for i in range(4)]
    return lax.ppermute(value, ("yl", "c"), pairs)


def even_pairs(value, axes):
    return lax.ppermute(value, axes, [(i, i ^ 1) for i in range(lax.axis_size(axes))])


def odd_pairs(value, axes):
    count = lax.axis_size(axes)
    pairs = [(i, i + 1) for i in range(1, count - 1, 2)]
    return lax.ppermute(value, axes, pairs + [(j, i) for i, j in pairs])


def after(value, *others):
    return lax.optimization_barrier((value,) + others)[0]


def split3(value):
    first = value.astype(bf16).astype(f32)
    rest = value - first
    second = rest.astype(bf16).astype(f32)
    return first, second, (rest - second).astype(bf16).astype(f32)


def augmented(points, scale, left):
    centred = points - 0.5
    norm = scale * jnp.sum(centred * centred, axis=0, keepdims=True)
    norms = [jnp.broadcast_to(part, points.shape) for part in split3(norm)]
    row = lax.broadcasted_iota(jnp.int32, points.shape, 0)
    if left:
        one, two, three = split3(centred)
        order = [one, one, two, one, two, three]
        base = 0
    else:
        one, two, three = split3((-2.0 * scale) * centred)
        order = [one, two, one, three, two, one]
        base = 3
    extra = jnp.where(row < 6, 1.0, 0.0)
    for index, part in enumerate(norms):
        extra = jnp.where(row == base + index, part, extra)
    return jnp.concatenate(order + [extra, jnp.zeros_like(extra)], axis=0).astype(bf16)


def live_lanes(count):
    lane = lax.broadcasted_iota(jnp.int32, (1, PTS), 1)
    return jnp.where(lane < count, 1.0, 0.0)


def nt_dot(left, right):
    return lax.dot_general(left, right, (((1,), (1,)), ((), ())), preferred_element_type=f32)


def call(kernel, name, out_shape, in_specs, args, scratch=(), grid=None, out_specs=None, params=SMALL, flops=0, moved=0):
    if out_specs is None:
        out_specs = jax.tree.map(lambda _: VMEM, out_shape)
    options = {} if grid is None else {"grid": grid}
    return pl.pallas_call(
        kernel,
        out_shape=out_shape,
        in_specs=in_specs,
        out_specs=out_specs,
        scratch_shapes=list(scratch),
        compiler_params=params,
        cost_estimate=pl.CostEstimate(flops=flops, bytes_accessed=moved, transcendentals=0),
        name=name,
        **options,
    )(*args)


def shape(*dims, dtype=f32):
    return jax.ShapeDtypeStruct(dims, dtype)


FIELD = shape(PROBES, PTS)


def prepare_kernel(coords, probes, precond, counts, inducing, centre_out, halo_out):
    points = coords[...]
    lane = lax.broadcasted_iota(jnp.int32, (FEAT, PTS), 1)
    short = lax.broadcasted_iota(jnp.int32, (FEAT, 128), 1)
    centre = jnp.zeros((FEAT, 128), f32)
    for index in range(16):
        picked = jnp.sum(
            jnp.where(lane == inducing[0, index], points, 0.0), axis=1, keepdims=True
        )
        centre = jnp.where(short == index, picked, centre)
    row = centre[:1]
    for feature in range(1, FEAT):
        row = row + pltpu.roll(centre, 128 - 16 * feature, 1)[feature : feature + 1]
    centre_out[...] = jnp.broadcast_to(row[None], centre_out.shape)
    halo_out[:FEAT] = points
    halo_out[FEAT:] = precond[...] * (probes[...] * live_lanes(counts[0, 0]))


def prepare(coords, probes, precond, counts, inducing):
    return call(
        prepare_kernel,
        "prepare",
        (shape(256, 1, 128), shape(FEAT + PROBES, PTS)),
        [VMEM, VMEM, VMEM, SMEM, SMEM],
        (coords, probes, precond, counts, inducing),
        params=LARGE,
    )


def factor_kernel(columns, first_out, second_out, third_out):
    quad = quad_index()
    for index in range(4):
        start = pl.multiple_of((quad ^ index) * SHARE, SHARE)
        parts = split3(columns[pl.ds(start, SHARE), :])
        for out, part in zip((first_out, second_out, third_out), parts):
            out[index * SHARE : (index + 1) * SHARE] = part.astype(bf16)


def split_factor(columns):
    return call(
        factor_kernel,
        "factor",
        (shape(4 * SHARE, QUARTER, dtype=bf16),) * 3,
        [VMEM],
        (columns,),
        moved=8 << 20,
    )


def centre_columns(parts):
    group = lax.broadcasted_iota(jnp.int32, (8, 128), 1) // 16
    tiles = []
    for index in range(4):
        tile = pltpu.roll(parts[8 * index : 8 * index + 8], 0, 1, stride=16, stride_axis=0)
        for bit in (1, 2, 4):
            tile = jnp.where(group & bit != 0, pltpu.roll(tile, 8 - bit, 0), tile)
        tiles.append(pltpu.roll(tile, 0, 1, stride=16, stride_axis=0))
    return jnp.concatenate(tiles, axis=1)


def rows_kernel(halo, centres, rows_out, sums_out, left, packed):
    left[...] = augmented(halo[:FEAT], -LOG2E / width_sq, True).astype(f32).T.astype(bf16)
    packed[...] = halo[FEAT:].astype(bf16)

    def chunk(step, carry):
        cells = centres[pl.ds(pl.multiple_of(step * 32, 32), 32), :]
        right = augmented(centre_columns(cells), -LOG2E / width_sq, False)
        power = jnp.dot(left[...], right, preferred_element_type=f32)
        rows = jnp.exp2(jnp.minimum(power, 0.0)).astype(bf16)
        rows_out[step] = rows
        sums = jnp.dot(packed[...], rows, preferred_element_type=f32)
        for part in range(4):
            sums_out[4 * step + part] = sums[:, part * SHARE : (part + 1) * SHARE]
        return carry

    lax.fori_loop(0, CHUNKS, chunk, 0, unroll=2)


def make_rows(halo, centres):
    return call(
        rows_kernel,
        "rows",
        (shape(CHUNKS, PTS, CHUNK, dtype=bf16), shape(32, PROBES, SHARE)),
        [VMEM, VMEM],
        (halo, centres),
        scratch=[pltpu.VMEM((PTS, 64), bf16), pltpu.VMEM((PROBES, PTS), bf16)],
        params=MIDDLE,
        moved=16 << 20,
    )


def project_kernel(packed, rows, sums_out):
    for step in range(CHUNKS):
        sums = jnp.dot(packed[...], rows[step], preferred_element_type=f32)
        for part in range(4):
            here = sums[:, part * SHARE : (part + 1) * SHARE]
            sums_out[4 * step + part, :PROBES] = here[:PROBES] + here[PROBES : 2 * PROBES]
            sums_out[4 * step + part, PROBES:] = here[2 * PROBES :]


def project(packed, rows):
    return call(
        project_kernel,
        "project",
        shape(32, 2 * PROBES, SHARE),
        [VMEM, VMEM],
        (packed, rows),
        params=MIDDLE,
        moved=16 << 20,
    )


def fill_table(table, sources, first, last, dtype):
    side_x, side_y = lax.axis_index("c"), lax.axis_index("x") & 1
    places_x = (1, 2 - 2 * side_x, 2 * side_x)
    places_y = (1, 2 - 2 * side_y, 2 * side_y)
    for place_y, source in zip(places_y, sources):
        for index, place_x in enumerate(places_x):
            start = (place_x * 3 + place_y) * CAP
            values = source[index, first:last].astype(dtype)
            for block in range(CAP):
                table[start + block] = values[:, block * BLOCK : (block + 1) * BLOCK]
    table[EMPTY] = jnp.zeros(table.shape[1:], dtype)


def partners(table, codes, block):
    return jnp.concatenate([table[codes[block, entry]] for entry in range(CAP)], axis=1)


def tiles_kernel(base, codes, near, even, odd, tiles_out, sparse_out, points, values):
    fill_table(points, (near, even, odd), 0, FEAT, f32)
    fill_table(values, (near, even, odd), FEAT, FEAT + PROBES, bf16)
    scale = 1.0 / (support_radius * support_radius)
    for index in range(HALF):
        block = base + index
        own = augmented(points[4 * CAP + block], scale, True).astype(f32).T.astype(bf16)
        other = augmented(partners(points, codes, block), scale, False)
        square = jnp.maximum(jnp.dot(own, other, preferred_element_type=f32), 0.0)
        ratio = jnp.sqrt(square)
        remain = jnp.maximum(1.0 - ratio, 0.0)
        second = remain * remain
        fourth = second * second
        tile = (fourth * second * remain * (7.0 * ratio + 1.0)).astype(bf16)
        tiles_out[index] = tile
        sparse_out[:, index * BLOCK : (index + 1) * BLOCK] = nt_dot(
            partners(values, codes, block), tile
        )


def make_tiles(half, codes, near, even, odd):
    return call(
        functools.partial(tiles_kernel, half * HALF),
        "tiles",
        (shape(HALF, BLOCK, PTS, dtype=bf16), shape(PROBES, HALF * BLOCK)),
        [SMEM, VMEM, VMEM, VMEM],
        (codes, near, even, odd),
        scratch=[
            pltpu.VMEM((EMPTY + 1, FEAT, BLOCK), f32),
            pltpu.VMEM((EMPTY + 1, PROBES, BLOCK), bf16),
        ],
        moved=8 << 20,
    )


def steps_of(sums):
    alpha = sums[:, 0:1] / sums[:, 1:2]
    return alpha, alpha * alpha * sums[:, 2:3] / sums[:, 0:1] - 1.0


def sparse_kernel(
    codes, near, even, odd, tiles_low, tiles_high, halo, image, scaled, sparse_low, sparse_high,
    precond, sparse_out, sums_out, values,
):
    fill_table(values, (near, even, odd), 0, PROBES, bf16)
    for block in range(CAP):
        sparse_out[:, block * BLOCK : (block + 1) * BLOCK] = nt_dot(
            partners(values, codes, block), (tiles_low, tiles_high)[block // HALF][block % HALF]
        )
    old = halo[FEAT:]
    new = scaled[...]
    by_old = old + jnp.concatenate([sparse_low[...], sparse_high[...]], axis=1)
    by_new = new + sparse_out[...]
    products = (
        old * (old / precond[...]),
        old * image[...],
        new * image[...],
        old * by_old,
        old * by_new + new * by_old,
        new * by_new,
    )
    lane = lax.broadcasted_iota(jnp.int32, (PROBES, 128), 1)
    row = jnp.zeros((PROBES, 128), f32)
    for index, product in enumerate(products):
        row = jnp.where(lane == index, jnp.sum(product, axis=1, keepdims=True), row)
    sums_out[...] = row


def apply_tiles(codes, nears, tiles, halo, image, scaled, sparse, precond):
    return call(
        sparse_kernel,
        "sparse",
        (FIELD, shape(PROBES, 128)),
        [SMEM] + [VMEM] * 11,
        (codes, *nears, *tiles, halo, image, scaled, *sparse, precond),
        scratch=[pltpu.VMEM((EMPTY + 1, PROBES, BLOCK), bf16)],
        moved=6 << 20,
    )


def stack_kernel(own, even, odd, out):
    out[0] = own[...]
    out[1] = even[...]
    out[2] = odd[...]


def surround(value, even, odd):
    column = call(
        stack_kernel,
        "stack",
        shape(3, *value.shape, dtype=value.dtype),
        [VMEM] * 3,
        (value, even, odd),
    )
    return column, even_pairs(column, GY), odd_pairs(column, GY)


def expand(weights, rows):
    total = jnp.zeros((PROBES, PTS), f32)
    for step in range(CHUNKS):
        part = jnp.concatenate([weights[4 * step + i, :PROBES] for i in range(4)], axis=1)
        total = total + nt_dot(part, rows[step])
    return total


def image_kernel(
    weights, rows, counts, halo, sparse_low, sparse_high, precond,
    image_out, scaled_out, halo_out, packed_out,
):
    search = halo[FEAT:]
    sparse = jnp.concatenate([sparse_low[...], sparse_high[...]], axis=1)
    image = live_lanes(counts[0, 0]) * (search + sparse + expand(weights, rows))
    image_out[...] = image
    scaled = precond[...] * image
    scaled_out[...] = scaled
    first = scaled.astype(bf16)
    second = (scaled - first.astype(f32)).astype(bf16)
    rest = (search - search.astype(bf16).astype(f32)).astype(bf16)
    halo_out[...] = first
    packed_out[:PROBES] = first
    packed_out[PROBES : 2 * PROBES] = second
    packed_out[2 * PROBES :] = rest


def make_image(weights, rows, counts, halo, sparse, precond):
    return call(
        image_kernel,
        "image",
        (
            FIELD,
            FIELD,
            shape(PROBES, PTS, dtype=bf16),
            shape(3 * PROBES, PTS, dtype=bf16),
        ),
        [VMEM, VMEM, SMEM] + [VMEM] * 4,
        (weights, rows, counts, halo, *sparse, precond),
        params=MIDDLE,
        moved=16 << 20,
    )


def sum_share_kernel(*refs):
    parts, out = refs[0], refs[-1]
    total = jnp.sum(parts[...], axis=0)
    if len(refs) == 3:
        total = jnp.concatenate([total, refs[1][...]], axis=0)
    out[...] = jnp.broadcast_to(total[None], out.shape)


def sum_share(parts, *sums):
    height = parts.shape[1] + sum(value.shape[0] for value in sums)
    return call(
        sum_share_kernel,
        "sum_share",
        shape(8, height, SHARE),
        [VMEM] * (1 + len(sums)),
        (parts, *sums),
    )


def sum_depth_kernel(parts, *outs):
    total = jnp.sum(parts[...], axis=0)
    for index, out in enumerate(outs):
        out[...] = total[index * PROBES : (index + 1) * PROBES]


def sum_depth(parts):
    count = parts.shape[1] // PROBES
    return call(
        sum_depth_kernel, "sum_depth", (shape(PROBES, SHARE),) * count, [VMEM], (parts,)
    )


def six_products(value, factors, dot):
    first, second, third = split3(value)
    stacked = jnp.concatenate([third, second, first], axis=0).astype(bf16)
    by_first = dot(stacked, factors[0][...])
    by_second = dot(stacked[PROBES:], factors[1][...])
    by_third = dot(stacked[2 * PROBES :], factors[2][...])
    small = by_first[:PROBES] + by_second[:PROBES] + by_third
    middle = by_first[PROBES : 2 * PROBES] + by_second[PROBES:]
    return by_first[2 * PROBES :] + (middle + small)


def nn_dot(left, right):
    return jnp.dot(left, right, preferred_element_type=f32)


def coeffs_kernel(*refs):
    shares, factors, out = refs[:4], refs[4:7], refs[-1]
    value = jnp.concatenate([ref[...] for ref in shares], axis=1)
    terms = six_products(value, factors, nn_dot)
    if len(refs) == 9:
        terms = jnp.concatenate([terms, refs[7][...]], axis=1)
    out[...] = jnp.broadcast_to(terms[None], out.shape)


def coeff_terms(shares, factors, *sums):
    width = QUARTER + SHARE * len(sums)
    return call(
        coeffs_kernel,
        "coeffs",
        shape(8, PROBES, width),
        [VMEM] * (7 + len(sums)),
        (*shares, *factors, *sums),
    )


def weights_kernel(parts, first, second, third, *outs):
    total = jnp.sum(parts[...], axis=0)
    terms = six_products(total[:, :QUARTER], (first, second, third), nt_dot)
    for index, out in enumerate(outs):
        out[:, :SHARE] = terms[:, index * SHARE : (index + 1) * SHARE]
        if out.shape[1] > SHARE:
            out[:, SHARE:] = total[:, QUARTER:]


def weight_terms(parts, factors):
    width = SHARE + parts.shape[2] - QUARTER
    return call(
        weights_kernel,
        "weights",
        (shape(PROBES, width),) * 4,
        [VMEM] * 4,
        (parts, *factors),
    )


def gather_kernel(own, first, second, third, out, total_out):
    total = own[...] + first[...] + second[...] + third[...]
    total_out[...] = total
    out[...] = jnp.broadcast_to(total.astype(bf16)[None], out.shape)


def gather_weights(terms):
    return call(
        gather_kernel,
        "gather",
        (shape(32, PROBES, SHARE, dtype=bf16), shape(PROBES, SHARE)),
        [VMEM] * 4,
        tuple(terms),
    )


def gather_last_kernel(
    own, first, second, third, new_share, rest_share, old_share, old_weights, out, sums_out
):
    total = own[...] + first[...] + second[...] + third[...]
    sums = total[:, SHARE:]
    sums_out[...] = sums
    alpha, beta = steps_of(sums)
    weights = ((1.0 + beta) * old_weights[...] - alpha * total[:, :SHARE]).astype(bf16)
    share = (1.0 + beta) * (old_share[...] + rest_share[...]) - alpha * new_share[...]
    dot = jnp.sum(weights.astype(f32) * share, axis=1, keepdims=True)
    lane = lax.broadcasted_iota(jnp.int32, (PROBES, SHARE), 1)
    row = jnp.zeros((PROBES, SHARE), f32)
    for index, part in enumerate(split3(dot)):
        row = jnp.where(lane == index, part, row)
    both = jnp.concatenate([weights, row.astype(bf16)], axis=0)
    out[...] = jnp.broadcast_to(both[None], out.shape)


def gather_last(terms, new_share, rest_share, old_share, old_weights):
    return call(
        gather_last_kernel,
        "gather_last",
        (shape(32, 2 * PROBES, SHARE, dtype=bf16), shape(PROBES, 128)),
        [VMEM] * 8,
        (*terms, new_share, rest_share, old_share, old_weights),
    )


def finish_kernel(
    weights, rows, counts, halo, probes, image, scaled, sparse_low, sparse_high, sparse, sums,
    solution_out, residual_out,
):
    totals = sums[...]
    alpha, beta = steps_of(totals)
    scale = 1.0 + beta
    old = halo[FEAT:]
    field = scale * old - alpha * scaled[...]
    by_old = jnp.concatenate([sparse_low[...], sparse_high[...]], axis=1)
    live = live_lanes(counts[0, 0])
    following = live * (
        field + (scale * by_old - alpha * sparse[...]) + expand(weights, rows)
    )
    dots = jnp.sum(weights[:, PROBES:].astype(f32), axis=0)
    curve = jnp.sum(dots, axis=1, keepdims=True) + (
        scale * scale * totals[:, 3:4]
        - alpha * scale * totals[:, 4:5]
        + alpha * alpha * totals[:, 5:6]
    )
    step = beta * totals[:, 0:1] / curve
    solution_out[...] = alpha * old + step * field
    residual_out[...] = (probes[...] * live - alpha * image[...]) - step * following


def finish(weights, rows, counts, halo, probes, image, scaled, old_sparse, sparse, sums):
    return call(
        finish_kernel,
        "finish",
        (FIELD, FIELD),
        [VMEM, VMEM, SMEM] + [VMEM] * 8,
        (weights, rows, counts, halo, probes, image, scaled, *old_sparse, sparse, sums),
        params=MIDDLE,
        moved=16 << 20,
    )


def on_device(coords, probes, precond, counts, neighbours, inducing, factor):
    points = coords[0, 0]
    given = probes[0, 0]
    scaling = precond[0]
    codes = neighbours[0, 0]

    centre_parts, halo = prepare(points, given, scaling, counts, inducing[0])

    even, odd = even_pairs(halo, GX), odd_pairs(halo, GX)
    centres = exchange(centre_parts, ALL).reshape(256, 128)
    columns = lax.dynamic_slice_in_dim(factor, quad_index() * QUARTER, QUARTER, 1)
    centres = after(centres, columns)
    halos = surround(after(halo, centres), even, odd)
    factors = split_factor(after(columns, halos[0]))
    rows, parts = make_rows(halo, after(centres, halos[0], *factors))
    parts = after(parts, *halos)

    def depth_of(got, *sums):
        return sum_depth(exchange(sum_share(got, *sums), "z"))

    def coeffs_of(depth, beside):
        own = depth[0]
        shares = [own] + [quad_partner(own, step) for step in (1, 2, 3)]
        shares[0] = after(own, *beside)
        return exchange(coeff_terms(shares, factors, *depth[2:]), GY)

    def terms_of(coeffs):
        terms = weight_terms(coeffs, factors)
        return [terms[0]] + [quad_partner(terms[step], step) for step in (1, 2, 3)]

    depth = depth_of(exchange(parts, PLANE))
    low = make_tiles(0, codes, after(halos[0], depth[0]), *halos[1:])
    coeffs = coeffs_of(depth, low)
    terms = weight_terms(coeffs, factors)
    high = make_tiles(1, codes, after(halos[0], terms[0]), *halos[1:])
    terms = [after(terms[0], *high)] + [quad_partner(terms[step], step) for step in (1, 2, 3)]
    old_share = depth[0]
    weights, old_weights = gather_weights(terms)
    weights = exchange(weights, PLANE)
    tiles, old_sparse = zip(low, high)
    image, scaled, sent, packed = make_image(weights, rows, counts, halo, old_sparse, scaling)
    even, odd = even_pairs(sent, GX), odd_pairs(sent, GX)
    parts = project(packed, rows)

    nears = surround(after(sent, parts), even, odd)
    got = exchange(after(parts, *nears), PLANE)
    sparse, sums = apply_tiles(
        codes, (after(nears[0], got),) + nears[1:], tiles, halo, image, scaled, old_sparse, scaling
    )
    depth = depth_of(got, sums)
    weights, totals = gather_last(
        terms_of(coeffs_of(depth, ())), depth[0], depth[1], old_share, old_weights
    )
    weights = exchange(weights, PLANE)
    solution, residual = finish(
        weights, rows, counts, halo, given, image, scaled, old_sparse, sparse, totals
    )
    return (solution[None, None], residual[None, None])


def solution(mesh):
    fine = Mesh(mesh.devices.reshape(8, 2, 2, 2, 4), ALL)
    placed = (
        P(GX, GY, None, None),
        P(GX, GY, None, None),
        P(GX, GY, None),
        P(GX, GY),
        P(GX, GY, None, None),
        P(GX, GY, None),
        P(GY, None),
    )
    return jax.shard_map(
        on_device,
        mesh=fine,
        in_specs=placed,
        out_specs=(P(GX, GY, None, None), P(GX, GY, None, None)),
        check_vma=False,
    )
```

```python
import functools

import jax
import jax.numpy as jnp
from jax import lax
from jax.experimental import pallas as pl
from jax.experimental.pallas import tpu as pltpu
from jax.sharding import Mesh, PartitionSpec as P

FEAT = 8
BLOCK = 128
PROBES = 16
PTS = 1024
SHARE = 128
CHUNK = 512
CHUNKS = 8
CAP = 8
EMPTY = 72
HALF = 4
QUARTER = 1024

support_radius = 0.32
width_sq = 0.045
LOG2E = 1.4426950408889634

ALL = ("z", "yl", "c", "yh", "x")
PLANE = ("yh", "x", "yl", "c")
GX = ("z", "yl", "c")
GY = ("yh", "x")
f32 = jnp.float32
bf16 = jnp.bfloat16

VMEM = pl.BlockSpec(memory_space=pltpu.VMEM)
SMEM = pl.BlockSpec(memory_space=pltpu.SMEM)
SMALL = pltpu.CompilerParams(vmem_limit_bytes=16 * 1024 * 1024)
MIDDLE = pltpu.CompilerParams(vmem_limit_bytes=24 * 1024 * 1024)
LARGE = pltpu.CompilerParams(vmem_limit_bytes=57 * 1024 * 1024)


def exchange(parts, axes):
    return lax.all_to_all(parts, axes, 0, 0, tiled=True)


def quad_index():
    return lax.axis_index("yl") * 2 + lax.axis_index("c")


def quad_partner(value, step):
    pairs = [(i, i ^ step) for i in range(4)]
    return lax.ppermute(value, ("yl", "c"), pairs)


def even_pairs(value, axes):
    return lax.ppermute(value, axes, [(i, i ^ 1) for i in range(lax.axis_size(axes))])


def odd_pairs(value, axes):
    count = lax.axis_size(axes)
    pairs = [(i, i + 1) for i in range(1, count - 1, 2)]
    return lax.ppermute(value, axes, pairs + [(j, i) for i, j in pairs])


def after(value, *others):
    return lax.optimization_barrier((value,) + others)[0]


def split3(value):
    first = value.astype(bf16).astype(f32)
    rest = value - first
    second = rest.astype(bf16).astype(f32)
    return first, second, (rest - second).astype(bf16).astype(f32)


def augmented(points, scale, left):
    centred = points - 0.5
    norm = scale * jnp.sum(centred * centred, axis=0, keepdims=True)
    norms = [jnp.broadcast_to(part, points.shape) for part in split3(norm)]
    row = lax.broadcasted_iota(jnp.int32, points.shape, 0)
    if left:
        one, two, three = split3(centred)
        order = [one, one, two, one, two, three]
        base = 0
    else:
        one, two, three = split3((-2.0 * scale) * centred)
        order = [one, two, one, three, two, one]
        base = 3
    extra = jnp.where(row < 6, 1.0, 0.0)
    for index, part in enumerate(norms):
        extra = jnp.where(row == base + index, part, extra)
    return jnp.concatenate(order + [extra, jnp.zeros_like(extra)], axis=0).astype(bf16)


def live_lanes(count):
    lane = lax.broadcasted_iota(jnp.int32, (1, PTS), 1)
    return jnp.where(lane < count, 1.0, 0.0)


def nt_dot(left, right):
    return lax.dot_general(left, right, (((1,), (1,)), ((), ())), preferred_element_type=f32)


def call(kernel, name, out_shape, in_specs, args, scratch=(), grid=None, out_specs=None, params=SMALL, flops=0, moved=0):
    if out_specs is None:
        out_specs = jax.tree.map(lambda _: VMEM, out_shape)
    options = {} if grid is None else {"grid": grid}
    return pl.pallas_call(
        kernel,
        out_shape=out_shape,
        in_specs=in_specs,
        out_specs=out_specs,
        scratch_shapes=list(scratch),
        compiler_params=params,
        cost_estimate=pl.CostEstimate(flops=flops, bytes_accessed=moved, transcendentals=0),
        name=name,
        **options,
    )(*args)


def shape(*dims, dtype=f32):
    return jax.ShapeDtypeStruct(dims, dtype)


FIELD = shape(PROBES, PTS)


def prepare_kernel(coords, probes, precond, counts, inducing, centre_out, halo_out):
    points = coords[...]
    lane = lax.broadcasted_iota(jnp.int32, (FEAT, PTS), 1)
    short = lax.broadcasted_iota(jnp.int32, (FEAT, 128), 1)
    centre = jnp.zeros((FEAT, 128), f32)
    for index in range(16):
        picked = jnp.sum(
            jnp.where(lane == inducing[0, index], points, 0.0), axis=1, keepdims=True
        )
        centre = jnp.where(short == index, picked, centre)
    row = centre[:1]
    for feature in range(1, FEAT):
        row = row + pltpu.roll(centre, 128 - 16 * feature, 1)[feature : feature + 1]
    centre_out[...] = jnp.broadcast_to(row[None], centre_out.shape)
    halo_out[:FEAT] = points
    halo_out[FEAT:] = precond[...] * (probes[...] * live_lanes(counts[0, 0]))


def prepare(coords, probes, precond, counts, inducing):
    return call(
        prepare_kernel,
        "prepare",
        (shape(256, 1, 128), shape(FEAT + PROBES, PTS)),
        [VMEM, VMEM, VMEM, SMEM, SMEM],
        (coords, probes, precond, counts, inducing),
        params=LARGE,
    )


def factor_kernel(columns, first_out, second_out, third_out):
    quad = quad_index()
    for index in range(4):
        start = pl.multiple_of((quad ^ index) * SHARE, SHARE)
        parts = split3(columns[pl.ds(start, SHARE), :])
        for out, part in zip((first_out, second_out, third_out), parts):
            out[index * SHARE : (index + 1) * SHARE] = part.astype(bf16)


def split_factor(columns):
    return call(
        factor_kernel,
        "factor",
        (shape(4 * SHARE, QUARTER, dtype=bf16),) * 3,
        [VMEM],
        (columns,),
        moved=8 << 20,
    )


def centre_columns(parts):
    group = lax.broadcasted_iota(jnp.int32, (8, 128), 1) // 16
    tiles = []
    for index in range(4):
        tile = pltpu.roll(parts[8 * index : 8 * index + 8], 0, 1, stride=16, stride_axis=0)
        for bit in (1, 2, 4):
            tile = jnp.where(group & bit != 0, pltpu.roll(tile, 8 - bit, 0), tile)
        tiles.append(pltpu.roll(tile, 0, 1, stride=16, stride_axis=0))
    return jnp.concatenate(tiles, axis=1)


def rows_kernel(halo, centres, rows_out, sums_out, left, packed):
    left[...] = augmented(halo[:FEAT], -LOG2E / width_sq, True).astype(f32).T.astype(bf16)
    packed[...] = halo[FEAT:].astype(bf16)

    def chunk(step, carry):
        cells = centres[pl.ds(pl.multiple_of(step * 32, 32), 32), :]
        right = augmented(centre_columns(cells), -LOG2E / width_sq, False)
        power = jnp.dot(left[...], right, preferred_element_type=f32)
        rows = jnp.exp2(jnp.minimum(power, 0.0)).astype(bf16)
        rows_out[step] = rows
        sums = jnp.dot(packed[...], rows, preferred_element_type=f32)
        for part in range(4):
            sums_out[4 * step + part] = sums[:, part * SHARE : (part + 1) * SHARE]
        return carry

    lax.fori_loop(0, CHUNKS, chunk, 0, unroll=4)


def make_rows(halo, centres):
    return call(
        rows_kernel,
        "rows",
        (shape(CHUNKS, PTS, CHUNK, dtype=bf16), shape(32, PROBES, SHARE)),
        [VMEM, VMEM],
        (halo, centres),
        scratch=[pltpu.VMEM((PTS, 64), bf16), pltpu.VMEM((PROBES, PTS), bf16)],
        params=MIDDLE,
        moved=16 << 20,
    )


def project_kernel(packed, rows, sums_out):
    for step in range(CHUNKS):
        sums = jnp.dot(packed[...], rows[step], preferred_element_type=f32)
        for part in range(4):
            here = sums[:, part * SHARE : (part + 1) * SHARE]
            sums_out[4 * step + part, :PROBES] = here[:PROBES] + here[PROBES : 2 * PROBES]
            sums_out[4 * step + part, PROBES:] = here[2 * PROBES :]


def project(packed, rows):
    return call(
        project_kernel,
        "project",
        shape(32, 2 * PROBES, SHARE),
        [VMEM, VMEM],
        (packed, rows),
        params=MIDDLE,
        moved=16 << 20,
    )


def fill_table(table, sources, first, last, dtype):
    side_x, side_y = lax.axis_index("c"), lax.axis_index("x") & 1
    places_x = (1, 2 - 2 * side_x, 2 * side_x)
    places_y = (1, 2 - 2 * side_y, 2 * side_y)
    for place_y, source in zip(places_y, sources):
        for index, place_x in enumerate(places_x):
            start = (place_x * 3 + place_y) * CAP
            values = source[index, first:last].astype(dtype)
            for block in range(CAP):
                table[start + block] = values[:, block * BLOCK : (block + 1) * BLOCK]
    table[EMPTY] = jnp.zeros(table.shape[1:], dtype)


def partners(table, codes, block):
    return jnp.concatenate([table[codes[block, entry]] for entry in range(CAP)], axis=1)


def tiles_kernel(base, codes, near, even, odd, tiles_out, sparse_out, points, values):
    fill_table(points, (near, even, odd), 0, FEAT, f32)
    fill_table(values, (near, even, odd), FEAT, FEAT + PROBES, bf16)
    scale = 1.0 / (support_radius * support_radius)
    for index in range(HALF):
        block = base + index
        own = augmented(points[4 * CAP + block], scale, True).astype(f32).T.astype(bf16)
        other = augmented(partners(points, codes, block), scale, False)
        square = jnp.maximum(jnp.dot(own, other, preferred_element_type=f32), 0.0)
        ratio = jnp.sqrt(square)
        remain = jnp.maximum(1.0 - ratio, 0.0)
        second = remain * remain
        fourth = second * second
        tile = (fourth * second * remain * (7.0 * ratio + 1.0)).astype(bf16)
        tiles_out[index] = tile
        sparse_out[:, index * BLOCK : (index + 1) * BLOCK] = nt_dot(
            partners(values, codes, block), tile
        )


def make_tiles(half, codes, near, even, odd):
    return call(
        functools.partial(tiles_kernel, half * HALF),
        "tiles",
        (shape(HALF, BLOCK, PTS, dtype=bf16), shape(PROBES, HALF * BLOCK)),
        [SMEM, VMEM, VMEM, VMEM],
        (codes, near, even, odd),
        scratch=[
            pltpu.VMEM((EMPTY + 1, FEAT, BLOCK), f32),
            pltpu.VMEM((EMPTY + 1, PROBES, BLOCK), bf16),
        ],
        moved=8 << 20,
    )


def steps_of(sums):
    alpha = sums[:, 0:1] / sums[:, 1:2]
    return alpha, alpha * alpha * sums[:, 2:3] / sums[:, 0:1] - 1.0


def sparse_kernel(
    codes, near, even, odd, tiles_low, tiles_high, halo, image, scaled, sparse_low, sparse_high,
    precond, sparse_out, sums_out, values,
):
    fill_table(values, (near, even, odd), 0, PROBES, bf16)
    for block in range(CAP):
        sparse_out[:, block * BLOCK : (block + 1) * BLOCK] = nt_dot(
            partners(values, codes, block), (tiles_low, tiles_high)[block // HALF][block % HALF]
        )
    old = halo[FEAT:]
    new = scaled[...]
    by_old = old + jnp.concatenate([sparse_low[...], sparse_high[...]], axis=1)
    by_new = new + sparse_out[...]
    products = (
        old * (old / precond[...]),
        old * image[...],
        new * image[...],
        old * by_old,
        old * by_new + new * by_old,
        new * by_new,
    )
    lane = lax.broadcasted_iota(jnp.int32, (PROBES, 128), 1)
    row = jnp.zeros((PROBES, 128), f32)
    for index, product in enumerate(products):
        row = jnp.where(lane == index, jnp.sum(product, axis=1, keepdims=True), row)
    sums_out[...] = row


def apply_tiles(codes, nears, tiles, halo, image, scaled, sparse, precond):
    return call(
        sparse_kernel,
        "sparse",
        (FIELD, shape(PROBES, 128)),
        [SMEM] + [VMEM] * 11,
        (codes, *nears, *tiles, halo, image, scaled, *sparse, precond),
        scratch=[pltpu.VMEM((EMPTY + 1, PROBES, BLOCK), bf16)],
        moved=6 << 20,
    )


def stack_kernel(own, even, odd, out):
    out[0] = own[...]
    out[1] = even[...]
    out[2] = odd[...]


def surround(value, even, odd):
    column = call(
        stack_kernel,
        "stack",
        shape(3, *value.shape, dtype=value.dtype),
        [VMEM] * 3,
        (value, even, odd),
    )
    return column, even_pairs(column, GY), odd_pairs(column, GY)


def expand(weights, rows):
    total = jnp.zeros((PROBES, PTS), f32)
    for step in range(CHUNKS):
        part = jnp.concatenate([weights[4 * step + i, :PROBES] for i in range(4)], axis=1)
        total = total + nt_dot(part, rows[step])
    return total


def image_kernel(
    weights, rows, counts, halo, sparse_low, sparse_high, precond,
    image_out, scaled_out, halo_out, packed_out,
):
    search = halo[FEAT:]
    sparse = jnp.concatenate([sparse_low[...], sparse_high[...]], axis=1)
    image = live_lanes(counts[0, 0]) * (search + sparse + expand(weights, rows))
    image_out[...] = image
    scaled = precond[...] * image
    scaled_out[...] = scaled
    first = scaled.astype(bf16)
    second = (scaled - first.astype(f32)).astype(bf16)
    rest = (search - search.astype(bf16).astype(f32)).astype(bf16)
    halo_out[...] = first
    packed_out[:PROBES] = first
    packed_out[PROBES : 2 * PROBES] = second
    packed_out[2 * PROBES :] = rest


def make_image(weights, rows, counts, halo, sparse, precond):
    return call(
        image_kernel,
        "image",
        (
            FIELD,
            FIELD,
            shape(PROBES, PTS, dtype=bf16),
            shape(3 * PROBES, PTS, dtype=bf16),
        ),
        [VMEM, VMEM, SMEM] + [VMEM] * 4,
        (weights, rows, counts, halo, *sparse, precond),
        params=MIDDLE,
        moved=16 << 20,
    )


def sum_share_kernel(*refs):
    parts, out = refs[0], refs[-1]
    total = jnp.sum(parts[...], axis=0)
    if len(refs) == 3:
        total = jnp.concatenate([total, refs[1][...]], axis=0)
    out[...] = jnp.broadcast_to(total[None], out.shape)


def sum_share(parts, *sums):
    height = parts.shape[1] + sum(value.shape[0] for value in sums)
    return call(
        sum_share_kernel,
        "sum_share",
        shape(8, height, SHARE),
        [VMEM] * (1 + len(sums)),
        (parts, *sums),
    )


def sum_depth_kernel(parts, *outs):
    total = jnp.sum(parts[...], axis=0)
    for index, out in enumerate(outs):
        out[...] = total[index * PROBES : (index + 1) * PROBES]


def sum_depth(parts):
    count = parts.shape[1] // PROBES
    return call(
        sum_depth_kernel, "sum_depth", (shape(PROBES, SHARE),) * count, [VMEM], (parts,)
    )


def six_products(value, factors, dot):
    first, second, third = split3(value)
    stacked = jnp.concatenate([third, second, first], axis=0).astype(bf16)
    by_first = dot(stacked, factors[0][...])
    by_second = dot(stacked[PROBES:], factors[1][...])
    by_third = dot(stacked[2 * PROBES :], factors[2][...])
    small = by_first[:PROBES] + by_second[:PROBES] + by_third
    middle = by_first[PROBES : 2 * PROBES] + by_second[PROBES:]
    return by_first[2 * PROBES :] + (middle + small)


def nn_dot(left, right):
    return jnp.dot(left, right, preferred_element_type=f32)


def coeffs_kernel(*refs):
    shares, factors, out = refs[:4], refs[4:7], refs[-1]
    value = jnp.concatenate([ref[...] for ref in shares], axis=1)
    terms = six_products(value, factors, nn_dot)
    if len(refs) == 9:
        terms = jnp.concatenate([terms, refs[7][...]], axis=1)
    out[...] = jnp.broadcast_to(terms[None], out.shape)


def coeff_terms(shares, factors, *sums):
    width = QUARTER + SHARE * len(sums)
    return call(
        coeffs_kernel,
        "coeffs",
        shape(8, PROBES, width),
        [VMEM] * (7 + len(sums)),
        (*shares, *factors, *sums),
    )


def weights_kernel(parts, first, second, third, *outs):
    total = jnp.sum(parts[...], axis=0)
    terms = six_products(total[:, :QUARTER], (first, second, third), nt_dot)
    for index, out in enumerate(outs):
        out[:, :SHARE] = terms[:, index * SHARE : (index + 1) * SHARE]
        if out.shape[1] > SHARE:
            out[:, SHARE:] = total[:, QUARTER:]


def weight_terms(parts, factors):
    width = SHARE + parts.shape[2] - QUARTER
    return call(
        weights_kernel,
        "weights",
        (shape(PROBES, width),) * 4,
        [VMEM] * 4,
        (parts, *factors),
    )


def gather_kernel(own, first, second, third, out, total_out):
    total = own[...] + first[...] + second[...] + third[...]
    total_out[...] = total
    out[...] = jnp.broadcast_to(total.astype(bf16)[None], out.shape)


def gather_weights(terms):
    return call(
        gather_kernel,
        "gather",
        (shape(32, PROBES, SHARE, dtype=bf16), shape(PROBES, SHARE)),
        [VMEM] * 4,
        tuple(terms),
    )


def gather_last_kernel(
    own, first, second, third, new_share, rest_share, old_share, old_weights, out, sums_out
):
    total = own[...] + first[...] + second[...] + third[...]
    sums = total[:, SHARE:]
    sums_out[...] = sums
    alpha, beta = steps_of(sums)
    weights = ((1.0 + beta) * old_weights[...] - alpha * total[:, :SHARE]).astype(bf16)
    share = (1.0 + beta) * (old_share[...] + rest_share[...]) - alpha * new_share[...]
    dot = jnp.sum(weights.astype(f32) * share, axis=1, keepdims=True)
    lane = lax.broadcasted_iota(jnp.int32, (PROBES, SHARE), 1)
    row = jnp.zeros((PROBES, SHARE), f32)
    for index, part in enumerate(split3(dot)):
        row = jnp.where(lane == index, part, row)
    both = jnp.concatenate([weights, row.astype(bf16)], axis=0)
    out[...] = jnp.broadcast_to(both[None], out.shape)


def gather_last(terms, new_share, rest_share, old_share, old_weights):
    return call(
        gather_last_kernel,
        "gather_last",
        (shape(32, 2 * PROBES, SHARE, dtype=bf16), shape(PROBES, 128)),
        [VMEM] * 8,
        (*terms, new_share, rest_share, old_share, old_weights),
    )


def finish_kernel(
    weights, rows, counts, halo, probes, image, scaled, sparse_low, sparse_high, sparse, sums,
    solution_out, residual_out,
):
    totals = sums[...]
    alpha, beta = steps_of(totals)
    scale = 1.0 + beta
    old = halo[FEAT:]
    field = scale * old - alpha * scaled[...]
    by_old = jnp.concatenate([sparse_low[...], sparse_high[...]], axis=1)
    live = live_lanes(counts[0, 0])
    following = live * (
        field + (scale * by_old - alpha * sparse[...]) + expand(weights, rows)
    )
    dots = jnp.sum(weights[:, PROBES:].astype(f32), axis=0)
    curve = jnp.sum(dots, axis=1, keepdims=True) + (
        scale * scale * totals[:, 3:4]
        - alpha * scale * totals[:, 4:5]
        + alpha * alpha * totals[:, 5:6]
    )
    step = beta * totals[:, 0:1] / curve
    solution_out[...] = alpha * old + step * field
    residual_out[...] = (probes[...] * live - alpha * image[...]) - step * following


def finish(weights, rows, counts, halo, probes, image, scaled, old_sparse, sparse, sums):
    return call(
        finish_kernel,
        "finish",
        (FIELD, FIELD),
        [VMEM, VMEM, SMEM] + [VMEM] * 8,
        (weights, rows, counts, halo, probes, image, scaled, *old_sparse, sparse, sums),
        params=MIDDLE,
        moved=16 << 20,
    )


def on_device(coords, probes, precond, counts, neighbours, inducing, factor):
    points = coords[0, 0]
    given = probes[0, 0]
    scaling = precond[0]
    codes = neighbours[0, 0]

    centre_parts, halo = prepare(points, given, scaling, counts, inducing[0])

    even, odd = even_pairs(halo, GX), odd_pairs(halo, GX)
    centres = exchange(centre_parts, ALL).reshape(256, 128)
    columns = lax.dynamic_slice_in_dim(factor, quad_index() * QUARTER, QUARTER, 1)
    centres = after(centres, columns)
    halos = surround(after(halo, centres), even, odd)
    factors = split_factor(after(columns, halos[0]))
    rows, parts = make_rows(halo, after(centres, halos[0], *factors))
    parts = after(parts, *halos)

    def depth_of(got, *sums):
        return sum_depth(exchange(sum_share(got, *sums), "z"))

    def coeffs_of(depth, beside):
        own = depth[0]
        shares = [own] + [quad_partner(own, step) for step in (1, 2, 3)]
        shares[0] = after(own, *beside)
        return exchange(coeff_terms(shares, factors, *depth[2:]), GY)

    def terms_of(coeffs):
        terms = weight_terms(coeffs, factors)
        return [terms[0]] + [quad_partner(terms[step], step) for step in (1, 2, 3)]

    depth = depth_of(exchange(parts, PLANE))
    low = make_tiles(0, codes, after(halos[0], depth[0]), *halos[1:])
    coeffs = coeffs_of(depth, low)
    terms = weight_terms(coeffs, factors)
    high = make_tiles(1, codes, after(halos[0], terms[0]), *halos[1:])
    terms = [after(terms[0], *high)] + [quad_partner(terms[step], step) for step in (1, 2, 3)]
    old_share = depth[0]
    weights, old_weights = gather_weights(terms)
    weights = exchange(weights, PLANE)
    tiles, old_sparse = zip(low, high)
    image, scaled, sent, packed = make_image(weights, rows, counts, halo, old_sparse, scaling)
    even, odd = even_pairs(sent, GX), odd_pairs(sent, GX)
    parts = project(packed, rows)

    nears = surround(after(sent, parts), even, odd)
    got = exchange(after(parts, *nears), PLANE)
    sparse, sums = apply_tiles(
        codes, (after(nears[0], got),) + nears[1:], tiles, halo, image, scaled, old_sparse, scaling
    )
    depth = depth_of(got, sums)
    weights, totals = gather_last(
        terms_of(coeffs_of(depth, ())), depth[0], depth[1], old_share, old_weights
    )
    weights = exchange(weights, PLANE)
    solution, residual = finish(
        weights, rows, counts, halo, given, image, scaled, old_sparse, sparse, totals
    )
    return (solution[None, None], residual[None, None])


def solution(mesh):
    fine = Mesh(mesh.devices.reshape(8, 2, 2, 2, 4), ALL)
    placed = (
        P(GX, GY, None, None),
        P(GX, GY, None, None),
        P(GX, GY, None),
        P(GX, GY),
        P(GX, GY, None, None),
        P(GX, GY, None),
        P(GY, None),
    )
    return jax.shard_map(
        on_device,
        mesh=fine,
        in_specs=placed,
        out_specs=(P(GX, GY, None, None), P(GX, GY, None, None)),
        check_vma=False,
    )
```

```python
import functools

import jax
import jax.numpy as jnp
from jax import lax
from jax.experimental import pallas as pl
from jax.experimental.pallas import tpu as pltpu
from jax.sharding import Mesh, PartitionSpec as P

FEAT = 8
BLOCK = 128
PROBES = 16
PTS = 1024
SHARE = 128
CHUNK = 512
CHUNKS = 8
CAP = 8
EMPTY = 72
HALF = 4
QUARTER = 1024

support_radius = 0.32
width_sq = 0.045
LOG2E = 1.4426950408889634

ALL = ("z", "yl", "c", "yh", "x")
PLANE = ("yh", "x", "yl", "c")
GX = ("z", "yl", "c")
GY = ("yh", "x")
f32 = jnp.float32
bf16 = jnp.bfloat16

VMEM = pl.BlockSpec(memory_space=pltpu.VMEM)
SMEM = pl.BlockSpec(memory_space=pltpu.SMEM)
SMALL = pltpu.CompilerParams(vmem_limit_bytes=16 * 1024 * 1024)
MIDDLE = pltpu.CompilerParams(vmem_limit_bytes=24 * 1024 * 1024)
LARGE = pltpu.CompilerParams(vmem_limit_bytes=57 * 1024 * 1024)


def exchange(parts, axes):
    return lax.all_to_all(parts, axes, 0, 0, tiled=True)


def quad_index():
    return lax.axis_index("yl") * 2 + lax.axis_index("c")


def quad_partner(value, step):
    pairs = [(i, i ^ step) for i in range(4)]
    return lax.ppermute(value, ("yl", "c"), pairs)


def even_pairs(value, axes):
    return lax.ppermute(value, axes, [(i, i ^ 1) for i in range(lax.axis_size(axes))])


def odd_pairs(value, axes):
    count = lax.axis_size(axes)
    pairs = [(i, i + 1) for i in range(1, count - 1, 2)]
    return lax.ppermute(value, axes, pairs + [(j, i) for i, j in pairs])


def after(value, *others):
    return lax.optimization_barrier((value,) + others)[0]


def split3(value):
    first = value.astype(bf16).astype(f32)
    rest = value - first
    second = rest.astype(bf16).astype(f32)
    return first, second, (rest - second).astype(bf16).astype(f32)


def augmented(points, scale, left):
    centred = points - 0.5
    norm = scale * jnp.sum(centred * centred, axis=0, keepdims=True)
    norms = [jnp.broadcast_to(part, points.shape) for part in split3(norm)]
    row = lax.broadcasted_iota(jnp.int32, points.shape, 0)
    if left:
        one, two, three = split3(centred)
        order = [one, one, two, one, two, three]
        base = 0
    else:
        one, two, three = split3((-2.0 * scale) * centred)
        order = [one, two, one, three, two, one]
        base = 3
    extra = jnp.where(row < 6, 1.0, 0.0)
    for index, part in enumerate(norms):
        extra = jnp.where(row == base + index, part, extra)
    return jnp.concatenate(order + [extra, jnp.zeros_like(extra)], axis=0).astype(bf16)


def live_lanes(count):
    lane = lax.broadcasted_iota(jnp.int32, (1, PTS), 1)
    return jnp.where(lane < count, 1.0, 0.0)


def nt_dot(left, right):
    return lax.dot_general(left, right, (((1,), (1,)), ((), ())), preferred_element_type=f32)


def call(kernel, name, out_shape, in_specs, args, scratch=(), grid=None, out_specs=None, params=SMALL, flops=0, moved=0):
    if out_specs is None:
        out_specs = jax.tree.map(lambda _: VMEM, out_shape)
    options = {} if grid is None else {"grid": grid}
    return pl.pallas_call(
        kernel,
        out_shape=out_shape,
        in_specs=in_specs,
        out_specs=out_specs,
        scratch_shapes=list(scratch),
        compiler_params=params,
        cost_estimate=pl.CostEstimate(flops=flops, bytes_accessed=moved, transcendentals=0),
        name=name,
        **options,
    )(*args)


def shape(*dims, dtype=f32):
    return jax.ShapeDtypeStruct(dims, dtype)


FIELD = shape(PROBES, PTS)


def prepare_kernel(coords, probes, precond, counts, inducing, centre_out, halo_out):
    points = coords[...]
    lane = lax.broadcasted_iota(jnp.int32, (FEAT, PTS), 1)
    short = lax.broadcasted_iota(jnp.int32, (FEAT, 128), 1)
    centre = jnp.zeros((FEAT, 128), f32)
    for index in range(16):
        picked = jnp.sum(
            jnp.where(lane == inducing[0, index], points, 0.0), axis=1, keepdims=True
        )
        centre = jnp.where(short == index, picked, centre)
    row = centre[:1]
    for feature in range(1, FEAT):
        row = row + pltpu.roll(centre, 128 - 16 * feature, 1)[feature : feature + 1]
    centre_out[...] = jnp.broadcast_to(row[None], centre_out.shape)
    halo_out[:FEAT] = points
    halo_out[FEAT:] = precond[...] * (probes[...] * live_lanes(counts[0, 0]))


def prepare(coords, probes, precond, counts, inducing):
    return call(
        prepare_kernel,
        "prepare",
        (shape(256, 1, 128), shape(FEAT + PROBES, PTS)),
        [VMEM, VMEM, VMEM, SMEM, SMEM],
        (coords, probes, precond, counts, inducing),
        params=MIDDLE,
    )


def factor_kernel(columns, first_out, second_out, third_out):
    quad = quad_index()
    for index in range(4):
        start = pl.multiple_of((quad ^ index) * SHARE, SHARE)
        parts = split3(columns[pl.ds(start, SHARE), :])
        for out, part in zip((first_out, second_out, third_out), parts):
            out[index * SHARE : (index + 1) * SHARE] = part.astype(bf16)


def split_factor(columns):
    return call(
        factor_kernel,
        "factor",
        (shape(4 * SHARE, QUARTER, dtype=bf16),) * 3,
        [VMEM],
        (columns,),
        moved=8 << 20,
    )


def centre_columns(parts):
    group = lax.broadcasted_iota(jnp.int32, (8, 128), 1) // 16
    tiles = []
    for index in range(4):
        tile = pltpu.roll(parts[8 * index : 8 * index + 8], 0, 1, stride=16, stride_axis=0)
        for bit in (1, 2, 4):
            tile = jnp.where(group & bit != 0, pltpu.roll(tile, 8 - bit, 0), tile)
        tiles.append(pltpu.roll(tile, 0, 1, stride=16, stride_axis=0))
    return jnp.concatenate(tiles, axis=1)


def rows_kernel(halo, centres, rows_out, sums_out, left, packed):
    left[...] = augmented(halo[:FEAT], -LOG2E / width_sq, True).astype(f32).T.astype(bf16)
    packed[...] = halo[FEAT:].astype(bf16)

    def chunk(step, carry):
        cells = centres[pl.ds(pl.multiple_of(step * 32, 32), 32), :]
        right = augmented(centre_columns(cells), -LOG2E / width_sq, False)
        power = jnp.dot(left[...], right, preferred_element_type=f32)
        rows = jnp.exp2(jnp.minimum(power, 0.0)).astype(bf16)
        rows_out[step] = rows
        sums = jnp.dot(packed[...], rows, preferred_element_type=f32)
        for part in range(4):
            sums_out[4 * step + part] = sums[:, part * SHARE : (part + 1) * SHARE]
        return carry

    lax.fori_loop(0, CHUNKS, chunk, 0, unroll=2)


def make_rows(halo, centres):
    return call(
        rows_kernel,
        "rows",
        (shape(CHUNKS, PTS, CHUNK, dtype=bf16), shape(32, PROBES, SHARE)),
        [VMEM, VMEM],
        (halo, centres),
        scratch=[pltpu.VMEM((PTS, 64), bf16), pltpu.VMEM((PROBES, PTS), bf16)],
        params=MIDDLE,
        moved=16 << 20,
    )


def project_kernel(packed, rows, sums_out):
    for step in range(CHUNKS):
        sums = jnp.dot(packed[...], rows[step], preferred_element_type=f32)
        for part in range(4):
            here = sums[:, part * SHARE : (part + 1) * SHARE]
            sums_out[4 * step + part, :PROBES] = here[:PROBES] + here[PROBES : 2 * PROBES]
            sums_out[4 * step + part, PROBES:] = here[2 * PROBES :]


def project(packed, rows):
    return call(
        project_kernel,
        "project",
        shape(32, 2 * PROBES, SHARE),
        [VMEM, VMEM],
        (packed, rows),
        params=MIDDLE,
        moved=16 << 20,
    )


def fill_table(table, sources, first, last, dtype):
    side_x, side_y = lax.axis_index("c"), lax.axis_index("x") & 1
    places_x = (1, 2 - 2 * side_x, 2 * side_x)
    places_y = (1, 2 - 2 * side_y, 2 * side_y)
    for place_y, source in zip(places_y, sources):
        for index, place_x in enumerate(places_x):
            start = (place_x * 3 + place_y) * CAP
            values = source[index, first:last].astype(dtype)
            for block in range(CAP):
                table[start + block] = values[:, block * BLOCK : (block + 1) * BLOCK]
    table[EMPTY] = jnp.zeros(table.shape[1:], dtype)


def partners(table, codes, block):
    return jnp.concatenate([table[codes[block, entry]] for entry in range(CAP)], axis=1)


def tiles_kernel(base, codes, near, even, odd, tiles_out, sparse_out, points, values):
    fill_table(points, (near, even, odd), 0, FEAT, f32)
    fill_table(values, (near, even, odd), FEAT, FEAT + PROBES, bf16)
    scale = 1.0 / (support_radius * support_radius)
    for index in range(HALF):
        block = base + index
        own = augmented(points[4 * CAP + block], scale, True).astype(f32).T.astype(bf16)
        other = augmented(partners(points, codes, block), scale, False)
        square = jnp.maximum(jnp.dot(own, other, preferred_element_type=f32), 0.0)
        ratio = jnp.sqrt(square)
        remain = jnp.maximum(1.0 - ratio, 0.0)
        second = remain * remain
        fourth = second * second
        tile = (fourth * second * remain * (7.0 * ratio + 1.0)).astype(bf16)
        tiles_out[index] = tile
        sparse_out[:, index * BLOCK : (index + 1) * BLOCK] = nt_dot(
            partners(values, codes, block), tile
        )


def make_tiles(half, codes, near, even, odd):
    return call(
        functools.partial(tiles_kernel, half * HALF),
        "tiles",
        (shape(HALF, BLOCK, PTS, dtype=bf16), shape(PROBES, HALF * BLOCK)),
        [SMEM, VMEM, VMEM, VMEM],
        (codes, near, even, odd),
        scratch=[
            pltpu.VMEM((EMPTY + 1, FEAT, BLOCK), f32),
            pltpu.VMEM((EMPTY + 1, PROBES, BLOCK), bf16),
        ],
        moved=8 << 20,
    )


def steps_of(sums):
    alpha = sums[:, 0:1] / sums[:, 1:2]
    return alpha, alpha * alpha * sums[:, 2:3] / sums[:, 0:1] - 1.0


def sparse_kernel(
    codes, near, even, odd, tiles_low, tiles_high, halo, image, scaled, sparse_low, sparse_high,
    precond, sparse_out, sums_out, values,
):
    fill_table(values, (near, even, odd), 0, PROBES, bf16)
    for block in range(CAP):
        sparse_out[:, block * BLOCK : (block + 1) * BLOCK] = nt_dot(
            partners(values, codes, block), (tiles_low, tiles_high)[block // HALF][block % HALF]
        )
    old = halo[FEAT:]
    new = scaled[...]
    by_old = old + jnp.concatenate([sparse_low[...], sparse_high[...]], axis=1)
    by_new = new + sparse_out[...]
    products = (
        old * (old / precond[...]),
        old * image[...],
        new * image[...],
        old * by_old,
        old * by_new + new * by_old,
        new * by_new,
    )
    lane = lax.broadcasted_iota(jnp.int32, (PROBES, 128), 1)
    row = jnp.zeros((PROBES, 128), f32)
    for index, product in enumerate(products):
        row = jnp.where(lane == index, jnp.sum(product, axis=1, keepdims=True), row)
    sums_out[...] = row


def apply_tiles(codes, nears, tiles, halo, image, scaled, sparse, precond):
    return call(
        sparse_kernel,
        "sparse",
        (FIELD, shape(PROBES, 128)),
        [SMEM] + [VMEM] * 11,
        (codes, *nears, *tiles, halo, image, scaled, *sparse, precond),
        scratch=[pltpu.VMEM((EMPTY + 1, PROBES, BLOCK), bf16)],
        moved=6 << 20,
    )


def stack_kernel(own, even, odd, out):
    out[0] = own[...]
    out[1] = even[...]
    out[2] = odd[...]


def surround(value, even, odd):
    column = call(
        stack_kernel,
        "stack",
        shape(3, *value.shape, dtype=value.dtype),
        [VMEM] * 3,
        (value, even, odd),
    )
    return column, even_pairs(column, GY), odd_pairs(column, GY)


def expand(weights, rows):
    total = jnp.zeros((PROBES, PTS), f32)
    for step in range(CHUNKS):
        part = jnp.concatenate([weights[4 * step + i, :PROBES] for i in range(4)], axis=1)
        total = total + nt_dot(part, rows[step])
    return total


def image_kernel(
    weights, rows, counts, halo, sparse_low, sparse_high, precond,
    image_out, scaled_out, halo_out, packed_out,
):
    search = halo[FEAT:]
    sparse = jnp.concatenate([sparse_low[...], sparse_high[...]], axis=1)
    image = live_lanes(counts[0, 0]) * (search + sparse + expand(weights, rows))
    image_out[...] = image
    scaled = precond[...] * image
    scaled_out[...] = scaled
    first = scaled.astype(bf16)
    second = (scaled - first.astype(f32)).astype(bf16)
    rest = (search - search.astype(bf16).astype(f32)).astype(bf16)
    halo_out[...] = first
    packed_out[:PROBES] = first
    packed_out[PROBES : 2 * PROBES] = second
    packed_out[2 * PROBES :] = rest


def make_image(weights, rows, counts, halo, sparse, precond):
    return call(
        image_kernel,
        "image",
        (
            FIELD,
            FIELD,
            shape(PROBES, PTS, dtype=bf16),
            shape(3 * PROBES, PTS, dtype=bf16),
        ),
        [VMEM, VMEM, SMEM] + [VMEM] * 4,
        (weights, rows, counts, halo, *sparse, precond),
        params=MIDDLE,
        moved=16 << 20,
    )


def sum_share_kernel(*refs):
    parts, out = refs[0], refs[-1]
    total = jnp.sum(parts[...], axis=0)
    if len(refs) == 3:
        total = jnp.concatenate([total, refs[1][...]], axis=0)
    out[...] = jnp.broadcast_to(total[None], out.shape)


def sum_share(parts, *sums):
    height = parts.shape[1] + sum(value.shape[0] for value in sums)
    return call(
        sum_share_kernel,
        "sum_share",
        shape(8, height, SHARE),
        [VMEM] * (1 + len(sums)),
        (parts, *sums),
    )


def sum_depth_kernel(parts, *outs):
    total = jnp.sum(parts[...], axis=0)
    for index, out in enumerate(outs):
        out[...] = total[index * PROBES : (index + 1) * PROBES]


def sum_depth(parts):
    count = parts.shape[1] // PROBES
    return call(
        sum_depth_kernel, "sum_depth", (shape(PROBES, SHARE),) * count, [VMEM], (parts,)
    )


def six_products(value, factors, dot):
    first, second, third = split3(value)
    stacked = jnp.concatenate([third, second, first], axis=0).astype(bf16)
    by_first = dot(stacked, factors[0][...])
    by_second = dot(stacked[PROBES:], factors[1][...])
    by_third = dot(stacked[2 * PROBES :], factors[2][...])
    small = by_first[:PROBES] + by_second[:PROBES] + by_third
    middle = by_first[PROBES : 2 * PROBES] + by_second[PROBES:]
    return by_first[2 * PROBES :] + (middle + small)


def nn_dot(left, right):
    return jnp.dot(left, right, preferred_element_type=f32)


def coeffs_kernel(*refs):
    shares, factors, out = refs[:4], refs[4:7], refs[-1]
    value = jnp.concatenate([ref[...] for ref in shares], axis=1)
    terms = six_products(value, factors, nn_dot)
    if len(refs) == 9:
        terms = jnp.concatenate([terms, refs[7][...]], axis=1)
    out[...] = jnp.broadcast_to(terms[None], out.shape)


def coeff_terms(shares, factors, *sums):
    width = QUARTER + SHARE * len(sums)
    return call(
        coeffs_kernel,
        "coeffs",
        shape(8, PROBES, width),
        [VMEM] * (7 + len(sums)),
        (*shares, *factors, *sums),
    )


def weights_kernel(parts, first, second, third, *outs):
    total = jnp.sum(parts[...], axis=0)
    terms = six_products(total[:, :QUARTER], (first, second, third), nt_dot)
    for index, out in enumerate(outs):
        out[:, :SHARE] = terms[:, index * SHARE : (index + 1) * SHARE]
        if out.shape[1] > SHARE:
            out[:, SHARE:] = total[:, QUARTER:]


def weight_terms(parts, factors):
    width = SHARE + parts.shape[2] - QUARTER
    return call(
        weights_kernel,
        "weights",
        (shape(PROBES, width),) * 4,
        [VMEM] * 4,
        (parts, *factors),
    )


def gather_kernel(own, first, second, third, out, total_out):
    total = own[...] + first[...] + second[...] + third[...]
    total_out[...] = total
    out[...] = jnp.broadcast_to(total.astype(bf16)[None], out.shape)


def gather_weights(terms):
    return call(
        gather_kernel,
        "gather",
        (shape(32, PROBES, SHARE, dtype=bf16), shape(PROBES, SHARE)),
        [VMEM] * 4,
        tuple(terms),
    )


def gather_last_kernel(
    own, first, second, third, new_share, rest_share, old_share, old_weights, out, sums_out
):
    total = own[...] + first[...] + second[...] + third[...]
    sums = total[:, SHARE:]
    sums_out[...] = sums
    alpha, beta = steps_of(sums)
    weights = ((1.0 + beta) * old_weights[...] - alpha * total[:, :SHARE]).astype(bf16)
    share = (1.0 + beta) * (old_share[...] + rest_share[...]) - alpha * new_share[...]
    dot = jnp.sum(weights.astype(f32) * share, axis=1, keepdims=True)
    lane = lax.broadcasted_iota(jnp.int32, (PROBES, SHARE), 1)
    row = jnp.zeros((PROBES, SHARE), f32)
    for index, part in enumerate(split3(dot)):
        row = jnp.where(lane == index, part, row)
    both = jnp.concatenate([weights, row.astype(bf16)], axis=0)
    out[...] = jnp.broadcast_to(both[None], out.shape)


def gather_last(terms, new_share, rest_share, old_share, old_weights):
    return call(
        gather_last_kernel,
        "gather_last",
        (shape(32, 2 * PROBES, SHARE, dtype=bf16), shape(PROBES, 128)),
        [VMEM] * 8,
        (*terms, new_share, rest_share, old_share, old_weights),
    )


def finish_kernel(
    weights, rows, counts, halo, probes, image, scaled, sparse_low, sparse_high, sparse, sums,
    solution_out, residual_out,
):
    totals = sums[...]
    alpha, beta = steps_of(totals)
    scale = 1.0 + beta
    old = halo[FEAT:]
    field = scale * old - alpha * scaled[...]
    by_old = jnp.concatenate([sparse_low[...], sparse_high[...]], axis=1)
    live = live_lanes(counts[0, 0])
    following = live * (
        field + (scale * by_old - alpha * sparse[...]) + expand(weights, rows)
    )
    dots = jnp.sum(weights[:, PROBES:].astype(f32), axis=0)
    curve = jnp.sum(dots, axis=1, keepdims=True) + (
        scale * scale * totals[:, 3:4]
        - alpha * scale * totals[:, 4:5]
        + alpha * alpha * totals[:, 5:6]
    )
    step = beta * totals[:, 0:1] / curve
    solution_out[...] = alpha * old + step * field
    residual_out[...] = (probes[...] * live - alpha * image[...]) - step * following


def finish(weights, rows, counts, halo, probes, image, scaled, old_sparse, sparse, sums):
    return call(
        finish_kernel,
        "finish",
        (FIELD, FIELD),
        [VMEM, VMEM, SMEM] + [VMEM] * 8,
        (weights, rows, counts, halo, probes, image, scaled, *old_sparse, sparse, sums),
        params=MIDDLE,
        moved=16 << 20,
    )


def on_device(coords, probes, precond, counts, neighbours, inducing, factor):
    points = coords[0, 0]
    given = probes[0, 0]
    scaling = precond[0]
    codes = neighbours[0, 0]

    centre_parts, halo = prepare(points, given, scaling, counts, inducing[0])

    even, odd = even_pairs(halo, GX), odd_pairs(halo, GX)
    centres = exchange(centre_parts, ALL).reshape(256, 128)
    columns = lax.dynamic_slice_in_dim(factor, quad_index() * QUARTER, QUARTER, 1)
    centres = after(centres, columns)
    halos = surround(after(halo, centres), even, odd)
    factors = split_factor(after(columns, halos[0]))
    rows, parts = make_rows(halo, after(centres, halos[0], *factors))
    parts = after(parts, *halos)

    def depth_of(got, *sums):
        return sum_depth(exchange(sum_share(got, *sums), "z"))

    def coeffs_of(depth, beside):
        own = depth[0]
        shares = [own] + [quad_partner(own, step) for step in (1, 2, 3)]
        shares[0] = after(own, *beside)
        return exchange(coeff_terms(shares, factors, *depth[2:]), GY)

    def terms_of(coeffs):
        terms = weight_terms(coeffs, factors)
        return [terms[0]] + [quad_partner(terms[step], step) for step in (1, 2, 3)]

    depth = depth_of(exchange(parts, PLANE))
    low = make_tiles(0, codes, after(halos[0], depth[0]), *halos[1:])
    coeffs = coeffs_of(depth, low)
    terms = weight_terms(coeffs, factors)
    high = make_tiles(1, codes, after(halos[0], terms[0]), *halos[1:])
    terms = [after(terms[0], *high)] + [quad_partner(terms[step], step) for step in (1, 2, 3)]
    old_share = depth[0]
    weights, old_weights = gather_weights(terms)
    weights = exchange(weights, PLANE)
    tiles, old_sparse = zip(low, high)
    image, scaled, sent, packed = make_image(weights, rows, counts, halo, old_sparse, scaling)
    even, odd = even_pairs(sent, GX), odd_pairs(sent, GX)
    parts = project(packed, rows)

    nears = surround(after(sent, parts), even, odd)
    got = exchange(after(parts, *nears), PLANE)
    sparse, sums = apply_tiles(
        codes, (after(nears[0], got),) + nears[1:], tiles, halo, image, scaled, old_sparse, scaling
    )
    depth = depth_of(got, sums)
    weights, totals = gather_last(
        terms_of(coeffs_of(depth, ())), depth[0], depth[1], old_share, old_weights
    )
    weights = exchange(weights, PLANE)
    solution, residual = finish(
        weights, rows, counts, halo, given, image, scaled, old_sparse, sparse, totals
    )
    return (solution[None, None], residual[None, None])


def solution(mesh):
    fine = Mesh(mesh.devices.reshape(8, 2, 2, 2, 4), ALL)
    placed = (
        P(GX, GY, None, None),
        P(GX, GY, None, None),
        P(GX, GY, None),
        P(GX, GY),
        P(GX, GY, None, None),
        P(GX, GY, None),
        P(GY, None),
    )
    return jax.shard_map(
        on_device,
        mesh=fine,
        in_specs=placed,
        out_specs=(P(GX, GY, None, None), P(GX, GY, None, None)),
        check_vma=False,
    )
```
